32 devices in a mesh: dp: 4 (over x, core), fsdp: 8 (over z, y).
Axes of the slice: x: 2, y: 2, z: 4, core: 2. Of those that a mesh axis runs over, the one named last changes fastest.
Arguments:
- frames: bfloat16 [32, 512, 512], P(('dp', 'fsdp')), may hold values from -12 to 12
- cotangent: bfloat16 [32, 512, 512], P(('dp', 'fsdp')), may hold values from -6 to 6
- seq_lengths: int32 [32], P(('dp', 'fsdp')), may hold values from 64 to 512, as said below
- ffn_in_master: float32 [2, 512, 2048], P(None, ('dp', 'fsdp')), may hold values from -0.25 to 0.25
- ffn_out_master: float32 [2, 2048, 512], P(None, ('dp', 'fsdp')), may hold values from -0.125 to 0.125
- mix_in_master: float32 [2, 512, 1024], P(None, ('dp', 'fsdp')), may hold values from -0.25 to 0.25
- mix_out_master: float32 [2, 512, 512], P(None, ('dp', 'fsdp')), may hold values from -0.25 to 0.25
- vector_master: float32 [30, 512], P(None, ('dp', 'fsdp')), may hold values from -5.3 to 2
- ffn_in_first: float32 [2, 512, 2048], P(None, ('dp', 'fsdp')), may hold values from -112 to 112
- ffn_out_first: float32 [2, 2048, 512], P(None, ('dp', 'fsdp')), may hold values from -160 to 160
- mix_in_first: float32 [2, 512, 1024], P(None, ('dp', 'fsdp')), may hold values from -160 to 160
- mix_out_first: float32 [2, 512, 512], P(None, ('dp', 'fsdp')), may hold values from -320 to 320
- vector_first: float32 [30, 512], P(None, ('dp', 'fsdp')), may hold values from -384 to 384
- ffn_in_second: float32 [2, 512, 2048], P(None, ('dp', 'fsdp')), may hold values from 184.32 to 1474.56
- ffn_out_second: float32 [2, 2048, 512], P(None, ('dp', 'fsdp')), may hold values from 327.68 to 2621.44
- mix_in_second: float32 [2, 512, 1024], P(None, ('dp', 'fsdp')), may hold values from 327.68 to 2621.44
- mix_out_second: float32 [2, 512, 512], P(None, ('dp', 'fsdp')), may hold values from 1310.72 to 10485.76
- vector_second: float32 [30, 512], P(None, ('dp', 'fsdp')), may hold values from 2048 to 16384
Outputs:
- activations: float32 [32, 512, 512], P(('dp', 'fsdp'))
- input_grad: float32 [32, 512, 512], P(('dp', 'fsdp'))
- ffn_in_new: float32 [2, 512, 2048], P(None, ('dp', 'fsdp'))
- ffn_out_new: float32 [2, 2048, 512], P(None, ('dp', 'fsdp'))
- mix_in_new: float32 [2, 512, 1024], P(None, ('dp', 'fsdp'))
- mix_out_new: float32 [2, 512, 512], P(None, ('dp', 'fsdp'))
- vector_new: float32 [30, 512], P(None, ('dp', 'fsdp'))
- ffn_in_first_new: float32 [2, 512, 2048], P(None, ('dp', 'fsdp'))
- ffn_out_first_new: float32 [2, 2048, 512], P(None, ('dp', 'fsdp'))
- mix_in_first_new: float32 [2, 512, 1024], P(None, ('dp', 'fsdp'))
- mix_out_first_new: float32 [2, 512, 512], P(None, ('dp', 'fsdp'))
- vector_first_new: float32 [30, 512], P(None, ('dp', 'fsdp'))
- ffn_in_second_new: float32 [2, 512, 2048], P(None, ('dp', 'fsdp'))
- ffn_out_second_new: float32 [2, 2048, 512], P(None, ('dp', 'fsdp'))
- mix_in_second_new: float32 [2, 512, 1024], P(None, ('dp', 'fsdp'))
- mix_out_second_new: float32 [2, 512, 512], P(None, ('dp', 'fsdp'))
- vector_second_new: float32 [30, 512], P(None, ('dp', 'fsdp'))
- ffn_in_copy: bfloat16 [2, 512, 2048], P(None, ('dp', 'fsdp'))
- ffn_out_copy: bfloat16 [2, 2048, 512], P(None, ('dp', 'fsdp'))
- mix_in_copy: bfloat16 [2, 512, 1024], P(None, ('dp', 'fsdp'))
- mix_out_copy: bfloat16 [2, 512, 512], P(None, ('dp', 'fsdp'))
- vector_copy: bfloat16 [30, 512], P(None, ('dp', 'fsdp'))
- sublayer_rms: float32 [5], replicated
The draws below stay inside these ranges and needn't reach their ends.
Inputs may be any that keep to these rules, and one draw needn't show every extreme that they name: `seq_lengths`: every draw holds a sequence of length 512 and one of length 64.
All inputs are finite; a program needn't handle non-finite values.
Results may differ from the reference program's by a relative error of at most 0.022.
The reference program's roundings to bfloat16 on the way count: a program that leaves them out, or rounds other values in their place, can miss the bound.
Values may be sent and summed in bfloat16 or wider, within the bound.
No kernel may reach another device: no remote copies, remote signals or barrier semaphores. Data moves between devices by JAX's collectives and lax.ppermute only.
A program may use at most 192 MiB of HBM per device.

```python
import math
import jax
import jax.numpy as jnp
from jax import lax

D = 512
FF = 2048
HEADS = 8
NSTATE = 32
KERNEL = 15
STEP_NUMBER = 5
SEQ_DEV = 1
LMAX = 512
SEQS = 32
TOKENS = 16384
NV = 30
N_DP = 4
N_FSDP = 8


def draw_frames(key, part):
    key = jax.random.fold_in(key, 37)
    seq_rows = jnp.arange(SEQS, dtype=jnp.int32)
    device_rank = (seq_rows // SEQ_DEV).astype(jnp.float32)
    spread_top = max(N_DP * N_FSDP - 1, 1)
    row_scale = 1.0 + 2.0 * device_rank / spread_top
    values = jnp.clip(jax.random.normal(key, (SEQS, LMAX, D), jnp.float32), -4.0, 4.0)
    drawn = jnp.clip(values * row_scale[:, None, None], -12.0, 12.0)
    return drawn.astype(jnp.bfloat16)


def draw_seq_lengths(key, part):
    key = jax.random.fold_in(key, 11)
    seq_rows = jnp.arange(SEQS, dtype=jnp.int32)
    device_rank = seq_rows // SEQ_DEV
    outer_rank = device_rank // N_FSDP
    inner_rank = device_rank % N_FSDP
    base_len = LMAX // 5 + 2 * LMAX * outer_rank // (5 * max(N_DP - 1, 1)) + 2 * LMAX * inner_rank // (5 * max(N_FSDP - 1, 1))
    jitter = jax.random.randint(key, (SEQS,), -(LMAX // 8), LMAX // 8 + 1, dtype=jnp.int32)
    drawn = jnp.clip(base_len + jitter, LMAX // 8, LMAX)
    drawn = drawn.at[0].set(LMAX // 8).at[SEQS - 1].set(LMAX)
    return drawn.astype(jnp.int32)


def draw_vector_master(key, part):
    key = jax.random.fold_in(key, 23)
    sub_keys = jax.random.split(key, 7)
    gains = jax.random.uniform(sub_keys[0], (6, D), jnp.float32, 0.6, 1.4)
    shifts = jnp.clip(0.1 * jax.random.normal(sub_keys[1], (6, D), jnp.float32), -0.4, 0.4)
    norm_rows = jnp.stack([gains, shifts], axis=1).reshape(12, D)
    skip_gains = jnp.clip(0.5 * jax.random.normal(sub_keys[2], (1, D), jnp.float32), -2.0, 2.0)
    decay_logs = jax.random.uniform(sub_keys[3], (1, HEADS * NSTATE), jnp.float32, -5.3, -1.2)
    coefficient = jnp.clip(0.05 * jax.random.normal(sub_keys[4], (1, HEADS * NSTATE), jnp.float32), -0.2, 0.2)
    ssm_params = jnp.concatenate([decay_logs, coefficient], axis=1)
    taps = jnp.clip(jax.random.normal(sub_keys[5], (KERNEL, D), jnp.float32) / KERNEL ** 0.5, -1.0, 1.0)
    tap_bias = jnp.clip(0.2 * jax.random.normal(sub_keys[6], (1, D), jnp.float32), -0.8, 0.8)
    return jnp.concatenate([norm_rows, skip_gains, ssm_params, taps, tap_bias], axis=0)


def block_levels(stream_key, extent, shards, low, largest):
    loudness, own = 1.0, jax.random.fold_in(stream_key, 6)
    for position, shards_of in shards:
        heights = jnp.exp(jax.random.uniform(jax.random.fold_in(own, position), (shards_of,), jnp.float32, low / len(shards), largest / len(shards)))
        loudness = loudness * jnp.repeat(heights, extent[position] // shards_of).reshape([-1 if axis == position else 1 for axis in range(len(extent))])
    return loudness


def bell_draw(rng, dims, spread, limit, cuts=(), kind=jnp.bfloat16):
    array = spread * jax.random.normal(rng, dims, jnp.float32)
    if cuts:
        array = array * block_levels(rng, dims, cuts, -0.22, 0.18)
    return jnp.clip(array, -limit, limit).astype(kind)


def setup_inputs(seed: int = 0) -> dict:
    keys = jax.random.split(jax.random.key(seed), 19)
    frames = draw_frames(jax.random.fold_in(keys[18], 71), 0)
    cotangent = bell_draw(keys[1], (SEQS, LMAX, D), 1.0, 6.0, ((0, 32),))
    seq_lengths = draw_seq_lengths(jax.random.fold_in(keys[18], 71), 0)
    ffn_in_master = bell_draw(keys[3], (2, D, FF), D ** -0.5, 0.25, ((1, 32),), jnp.float32)
    ffn_out_master = bell_draw(keys[4], (2, FF, D), FF ** -0.5, 0.125, ((1, 32),), jnp.float32)
    mix_in_master = bell_draw(keys[5], (2, D, 2 * D), D ** -0.5, 0.25, ((1, 32),), jnp.float32)
    mix_out_master = bell_draw(keys[6], (2, D, D), D ** -0.5, 0.25, ((1, 32),), jnp.float32)
    vector_master = draw_vector_master(jax.random.fold_in(keys[18], 71), 0)
    ffn_in_first = bell_draw(keys[8], (2, D, FF), (0.15 * TOKENS ** 0.5), 112.0, ((1, 32),), jnp.float32)
    ffn_out_first = bell_draw(keys[9], (2, FF, D), (0.2 * TOKENS ** 0.5), 160.0, ((1, 32),), jnp.float32)
    mix_in_first = bell_draw(keys[10], (2, D, 2 * D), (0.2 * TOKENS ** 0.5), 160.0, ((1, 32),), jnp.float32)
    mix_out_first = bell_draw(keys[11], (2, D, D), (0.4 * TOKENS ** 0.5), 320.0, ((1, 32),), jnp.float32)
    vector_first = bell_draw(keys[12], (NV, D), (0.5 * TOKENS ** 0.5), 384.0, ((1, 32),), jnp.float32)
    ffn_in_second = jnp.clip(jnp.exp(math.log(1474.56) - 2.0794415 * jax.random.uniform(keys[13], (2, D, FF), jnp.float32) ** block_levels(keys[13], (2, D, FF), ((1, 32),), -0.2, 0.2)), 184.32, 1474.56)
    ffn_out_second = jnp.clip(jnp.exp(math.log(2621.44) - 2.0794415 * jax.random.uniform(keys[14], (2, FF, D), jnp.float32) ** block_levels(keys[14], (2, FF, D), ((1, 32),), -0.2, 0.2)), 327.68, 2621.44)
    mix_in_second = jnp.clip(jnp.exp(math.log(2621.44) - 2.0794415 * jax.random.uniform(keys[15], (2, D, 2 * D), jnp.float32) ** block_levels(keys[15], (2, D, 2 * D), ((1, 32),), -0.2, 0.2)), 327.68, 2621.44)
    mix_out_second = jnp.clip(jnp.exp(math.log(10485.76) - 2.0794415 * jax.random.uniform(keys[16], (2, D, D), jnp.float32) ** block_levels(keys[16], (2, D, D), ((1, 32),), -0.2, 0.2)), 1310.72, 10485.76)
    vector_second = jnp.clip(jnp.exp(math.log(16384.0) - 2.0794415 * jax.random.uniform(keys[17], (NV, D), jnp.float32) ** block_levels(keys[17], (NV, D), ((1, 32),), -0.2, 0.2)), 2048.0, 16384.0)
    return {"frames": frames, "cotangent": cotangent, "seq_lengths": seq_lengths, "ffn_in_master": ffn_in_master, "ffn_out_master": ffn_out_master, "mix_in_master": mix_in_master, "mix_out_master": mix_out_master, "vector_master": vector_master, "ffn_in_first": ffn_in_first, "ffn_out_first": ffn_out_first, "mix_in_first": mix_in_first, "mix_out_first": mix_out_first, "vector_first": vector_first, "ffn_in_second": ffn_in_second, "ffn_out_second": ffn_out_second, "mix_in_second": mix_in_second, "mix_out_second": mix_out_second, "vector_second": vector_second}


NORM_EPS = 1e-05
BETA_FIRST = 0.5
BETA_SECOND = 0.6
ADAM_EPS = 1e-08
RATE_MATRIX = 0.02
RATE_VECTOR = 0.2
WEIGHT_DECAY = 0.01
HIGHEST = lax.Precision.HIGHEST
skip_row = 12
ssm_row = 13
tap_first = 14

@jax.custom_vjp
def low(v):
    return lax.optimization_barrier(v.astype(jnp.bfloat16)).astype(jnp.float32)

@jax.custom_vjp
def low_back(v):
    return v

def low_keep(v):
    return (low(v), None)

def low_pass(kept, grad):
    return (grad,)

def back_keep(v):
    return (v, None)

def back_low(kept, grad):
    return (low(grad),)
low.defvjp(low_keep, low_pass)
low_back.defvjp(back_keep, back_low)

def layer_norm(values, vectors, norm_index):
    scale_row = vectors[2 * norm_index]
    shift_row = vectors[2 * norm_index + 1]
    average = lax.optimization_barrier(jnp.mean(values, axis=-1, keepdims=True))
    centered = values - average
    variance = lax.optimization_barrier(jnp.mean(centered * centered, axis=-1, keepdims=True))
    return centered * lax.rsqrt(variance + NORM_EPS) * scale_row + shift_row

def causal_toeplitz(kernel):
    head_count, length = kernel.shape
    backward_row = jnp.concatenate([jnp.flip(kernel, axis=1), jnp.zeros((head_count, length), jnp.float32)], axis=1)
    repeated = jnp.broadcast_to(backward_row[:, None, :], (head_count, length, 2 * length)).reshape(head_count, 2 * length * length)
    skewed = repeated[:, :length * (2 * length - 1)].reshape(head_count, length, 2 * length - 1)
    return skewed[:, :, length - 1:]

def long_conv(signal, vectors):
    seq_count, length, channels = signal.shape
    states = NSTATE
    decay_logs = vectors[ssm_row, :HEADS * states].reshape(HEADS, states)
    coefficient = vectors[ssm_row, HEADS * states:].reshape(HEADS, states)
    decay_rates = jnp.exp(decay_logs)
    lag_times = jnp.arange(length).astype(jnp.float32)
    kernel = lax.optimization_barrier(jnp.sum(coefficient[:, :, None] * jnp.exp(-decay_rates[:, :, None] * lag_times[None, None, :]), axis=1))
    toeplitz = causal_toeplitz(kernel)
    by_head = signal.reshape(seq_count, length, HEADS, channels // HEADS)
    convolved = jnp.einsum('hts,bshc->bthc', toeplitz, by_head, precision=HIGHEST)
    return convolved.reshape(seq_count, length, channels) + vectors[skip_row] * signal

def ssm_piece(projected, valid, vectors):
    channels = projected.shape[-1] // 2
    signal = projected[..., :channels] * valid
    gate_part = projected[..., channels:]
    return long_conv(signal, vectors) * jax.nn.silu(gate_part)

def conv_piece(projected, valid, vectors):
    channels = projected.shape[-1] // 2
    length = projected.shape[1]
    glu_out = projected[..., :channels] * jax.nn.sigmoid(projected[..., channels:]) * valid
    margin = KERNEL // 2
    padded = jnp.pad(glu_out, ((0, 0), (margin, margin), (0, 0)))
    summed = vectors[tap_first + KERNEL] + padded[:, 0:length] * vectors[tap_first]
    for offset in range(1, KERNEL):
        summed = summed + padded[:, offset:offset + length] * vectors[tap_first + offset]
    return jax.nn.silu(layer_norm(summed, vectors, 3))

def forward(inputs, valid, ffn_in, ffn_out, mix_in, mix_out, vectors):
    seq_count, length, channels = inputs.shape

    def branch(residual, norm_index, weight_in, weight_out, local_fn):
        normed = low(layer_norm(residual, vectors, norm_index)).reshape(seq_count * length, channels)
        projected = low_back(jnp.dot(normed, weight_in, precision=HIGHEST, preferred_element_type=jnp.float32))
        activated = low(local_fn(projected.reshape(seq_count, length, -1)))
        flat_act = activated.reshape(seq_count * length, -1)
        output = low_back(jnp.dot(flat_act, weight_out, precision=HIGHEST, preferred_element_type=jnp.float32))
        return output.reshape(seq_count, length, channels)

    def silu_fn(projected):
        return jax.nn.silu(projected)

    def ssm_fn(projected):
        return ssm_piece(projected, valid, vectors)

    def conv_fn(projected):
        return conv_piece(projected, valid, vectors)
    first_part = 0.5 * branch(inputs, 0, ffn_in[0], ffn_out[0], silu_fn)
    after_first = inputs + first_part
    ssm_part = branch(after_first, 1, mix_in[0], mix_out[0], ssm_fn)
    after_ssm = after_first + ssm_part
    conv_part = branch(after_ssm, 2, mix_in[1], mix_out[1], conv_fn)
    after_conv = after_ssm + conv_part
    last_part = 0.5 * branch(after_conv, 4, ffn_in[1], ffn_out[1], silu_fn)
    after_last = after_conv + last_part
    return (layer_norm(after_last, vectors, 5), (first_part, ssm_part, conv_part, last_part, after_last))

def adamw(master, first, second, gradient, rate, decay):
    first_new = BETA_FIRST * first + (1.0 - BETA_FIRST) * gradient
    second_new = BETA_SECOND * second + (1.0 - BETA_SECOND) * gradient * gradient
    first_hat = first_new / (1.0 - BETA_FIRST ** STEP_NUMBER)
    second_hat = second_new / (1.0 - BETA_SECOND ** STEP_NUMBER)
    updated = master - rate * (first_hat / (jnp.sqrt(second_hat) + ADAM_EPS) + decay * master)
    return (updated, first_new, second_new, updated.astype(jnp.bfloat16))

def reference(frames, cotangent, seq_lengths, ffn_in_master, ffn_out_master, mix_in_master, mix_out_master, vector_master, ffn_in_first, ffn_out_first, mix_in_first, mix_out_first, vector_first, ffn_in_second, ffn_out_second, mix_in_second, mix_out_second, vector_second):
    masters = (ffn_in_master, ffn_out_master, mix_in_master, mix_out_master, vector_master)
    weights = tuple((low(master) for master in masters))
    group_size = math.gcd(SEQS, max(1, 4096 // LMAX))
    rounds = SEQS // group_size
    positions = jnp.arange(LMAX, dtype=jnp.int32)
    valid_all = (positions[None, :] < seq_lengths[:, None]).astype(jnp.float32)[:, :, None]
    inputs_all = frames.astype(jnp.float32).reshape(rounds, group_size, LMAX, D)
    back_all = cotangent.astype(jnp.float32).reshape(rounds, group_size, LMAX, D)
    valid_groups = valid_all.reshape(rounds, group_size, LMAX, 1)

    def one_round(carried, round_item):
        grad_sums, stat_sums = carried
        inputs, back_rows, valid = round_item

        def apply_layer(inputs, *params):
            return forward(inputs, valid, *params)
        outputs, pull_back, piece_outs = jax.vjp(apply_layer, inputs, *weights, has_aux=True)
        gradients = pull_back(back_rows)
        grad_sums = tuple((running + gradient for running, gradient in zip(grad_sums, gradients[1:])))
        squares = [jnp.sum(valid * piece_out * piece_out) for piece_out in piece_outs]
        stat_sums = stat_sums + jnp.stack(squares + [jnp.sum(valid)])
        return ((grad_sums, stat_sums), (outputs, gradients[0]))
    initial = (tuple((jnp.zeros_like(weight) for weight in weights)), jnp.zeros((6,), jnp.float32))
    (grad_sums, stat_sums), (outputs, input_grads) = lax.scan(one_round, initial, (inputs_all, back_all, valid_groups))
    activations = outputs.reshape(SEQS, LMAX, D)
    input_grad = input_grads.reshape(SEQS, LMAX, D)
    sublayer_rms = jnp.sqrt(stat_sums[:5] / (stat_sums[5] * D))
    firsts = (ffn_in_first, ffn_out_first, mix_in_first, mix_out_first, vector_first)
    seconds = (ffn_in_second, ffn_out_second, mix_in_second, mix_out_second, vector_second)
    results = [adamw(masters[slot_index], firsts[slot_index], seconds[slot_index], grad_sums[slot_index], RATE_MATRIX if slot_index < 4 else RATE_VECTOR, WEIGHT_DECAY if slot_index < 4 else 0.0) for slot_index in range(5)]
    return (activations, input_grad, results[0][0], results[1][0], results[2][0], results[3][0], results[4][0], results[0][1], results[1][1], results[2][1], results[3][1], results[4][1], results[0][2], results[1][2], results[2][2], results[3][2], results[4][2], results[0][3], results[1][3], results[2][3], results[3][3], results[4][3], sublayer_rms)
```

```python
import jax
import numpy as np
import jax.numpy as jnp
from jax import lax
from jax.sharding import PartitionSpec as P

HEADS = 8
NSTATE = 32
KERNEL = 15
STEP_NUMBER = 5


NORM_EPS = 1e-05
BETA_FIRST = 0.5
BETA_SECOND = 0.6
ADAM_EPS = 1e-08
RATE_MATRIX = 0.02
RATE_VECTOR = 0.2
WEIGHT_DECAY = 0.01
HIGHEST = lax.Precision.HIGHEST
skip_row = 12
ssm_row = 13
tap_first = 14


def layer_norm(values, vectors, norm_index):
    scale_row = vectors[2 * norm_index]
    shift_row = vectors[2 * norm_index + 1]
    average = jnp.mean(values, axis=-1, keepdims=True)
    centered = values - average
    variance = jnp.mean(centered * centered, axis=-1, keepdims=True)
    return centered * lax.rsqrt(variance + NORM_EPS) * scale_row + shift_row


def causal_toeplitz(kernel):
    head_count, length = kernel.shape
    backward_row = jnp.concatenate(
        [jnp.flip(kernel, axis=1), jnp.zeros((head_count, length), jnp.float32)], axis=1
    )
    repeated = jnp.broadcast_to(backward_row[:, None, :], (head_count, length, 2 * length)).reshape(
        head_count, 2 * length * length
    )
    skewed = repeated[:, : length * (2 * length - 1)].reshape(head_count, length, 2 * length - 1)
    return skewed[:, :, length - 1 :]


def long_conv(signal, vectors):
    seq_count, length, channels = signal.shape
    states = NSTATE
    decay_logs = vectors[ssm_row, : HEADS * states].reshape(HEADS, states)
    coefficient = vectors[ssm_row, HEADS * states :].reshape(HEADS, states)
    decay_rates = jnp.exp(decay_logs)
    lag_times = jnp.arange(length).astype(jnp.float32)
    kernel = jnp.sum(
        coefficient[:, :, None] * jnp.exp(-decay_rates[:, :, None] * lag_times[None, None, :]),
        axis=1,
    )
    toeplitz = causal_toeplitz(kernel)
    by_head = signal.reshape(seq_count, length, HEADS, channels // HEADS)
    convolved = jnp.einsum("hts,bshc->bthc", toeplitz, by_head, precision=HIGHEST)
    return convolved.reshape(seq_count, length, channels) + vectors[skip_row] * signal


def ssm_piece(projected, valid, vectors):
    channels = projected.shape[-1] // 2
    signal = projected[..., :channels] * valid
    gate_part = projected[..., channels:]
    return long_conv(signal, vectors) * jax.nn.silu(gate_part)


def conv_piece(projected, valid, vectors):
    channels = projected.shape[-1] // 2
    length = projected.shape[1]
    glu_out = projected[..., :channels] * jax.nn.sigmoid(projected[..., channels:]) * valid
    margin = KERNEL // 2
    padded = jnp.pad(glu_out, ((0, 0), (margin, margin), (0, 0)))
    summed = vectors[tap_first + KERNEL] + padded[:, 0:length] * vectors[tap_first]
    for offset in range(1, KERNEL):
        summed = summed + padded[:, offset : offset + length] * vectors[tap_first + offset]
    return jax.nn.silu(layer_norm(summed, vectors, 3))


def adamw(master, first, second, gradient, rate, decay):
    first_new = BETA_FIRST * first + (1.0 - BETA_FIRST) * gradient
    second_new = BETA_SECOND * second + (1.0 - BETA_SECOND) * gradient * gradient
    first_hat = first_new / (1.0 - BETA_FIRST**STEP_NUMBER)
    second_hat = second_new / (1.0 - BETA_SECOND**STEP_NUMBER)
    updated = master - rate * (first_hat / (jnp.sqrt(second_hat) + ADAM_EPS) + decay * master)
    return (updated, first_new, second_new, updated.astype(jnp.bfloat16))


def matmul(left_side, right_side):
    return jnp.dot(left_side, right_side, preferred_element_type=jnp.float32)


def inner_rows(left_side, right_side):
    return lax.dot_general(
        left_side, right_side, (((0,), (0,)), ((), ())), preferred_element_type=jnp.float32
    )


def inner_cols(left_side, right_side):
    return lax.dot_general(
        left_side, right_side, (((1,), (1,)), ((), ())), preferred_element_type=jnp.float32
    )


def run_branch(residual, norm_index, weight_in, weight_out, local_fn, vectors):
    seq_count, length, channels = residual.shape
    normed, pull_norm = jax.vjp(
        lambda values, params: layer_norm(values, params, norm_index), residual, vectors
    )
    normed_low = normed.astype(jnp.bfloat16).reshape(seq_count * length, channels)
    projected = matmul(normed_low, weight_in).reshape(seq_count, length, -1)
    activated, pull_local = jax.vjp(local_fn, projected, vectors)
    active_low = activated.astype(jnp.bfloat16).reshape(seq_count * length, -1)
    output = matmul(active_low, weight_out).reshape(seq_count, length, channels)
    return (output, (pull_norm, normed_low, pull_local, active_low))


def back_branch(grad_output, saved, weight_in, weight_out):
    pull_norm, normed_low, pull_local, active_low = saved
    seq_count, length, channels = grad_output.shape
    grad_low = grad_output.reshape(seq_count * length, channels).astype(jnp.bfloat16)
    grad_out_weight = inner_rows(active_low, grad_low)
    grad_active = inner_cols(grad_low, weight_out).reshape(seq_count, length, -1)
    grad_projected, grad_vec_local = pull_local(grad_active)
    grad_proj_low = grad_projected.reshape(seq_count * length, -1).astype(jnp.bfloat16)
    grad_in_weight = inner_rows(normed_low, grad_proj_low)
    grad_normed = inner_cols(grad_proj_low, weight_in).reshape(seq_count, length, channels)
    grad_residual, grad_vec_norm = pull_norm(grad_normed)
    return (grad_residual, grad_in_weight, grad_out_weight, grad_vec_local + grad_vec_norm)


def piece_tables():
    tables = []
    for me in range(32):
        core = (me >> 3) & 1
        pieces = []
        for side in (0, 1):
            base = me ^ (8 * side)
            across = ((16, 1), (1, 16))[core ^ side]
            for spot in range(16):
                rel = (across[0] if spot & 8 else 0) | (across[1] if spot & 4 else 0)
                rel |= (2 if spot & 2 else 0) | (4 if spot & 1 else 0)
                pieces.append(base ^ rel)
        tables.append(pieces)
    return np.array(tables, np.int32)


TABLES = piece_tables()
SPOTS = np.argsort(TABLES, axis=1).astype(np.int32)
AXES = ("dp", "fsdp")
CORE, Z_HIGH, Z_LOW = 8, 4, 2
STAGES = (Z_HIGH, Z_LOW, (1, 16), (16, 1))


def swap(values, mask):
    masks = mask if isinstance(mask, tuple) else (mask, mask)
    return lax.ppermute(values, AXES, [(i, i ^ masks[(i >> 3) & 1]) for i in range(32)])


def gather_pieces(shard, extra=None):
    rows = shard.shape[0]
    held = shard[None]
    for mask in STAGES + (CORE,):
        if extra is None:
            got = swap(held, mask)
        else:
            sent = jnp.concatenate([held.reshape(-1, 512), extra])
            got = swap(sent, mask)
            extra = extra + got[-extra.shape[0] :]
            got = got[: -extra.shape[0]].reshape(held.shape)
        if mask != CORE:
            held = jnp.concatenate([held, got])
    return held, got, extra


def reduce_pieces(kept, sent):
    got = swap(sent, CORE)
    half = 8
    for mask in STAGES[::-1]:
        sent = (kept[half:].astype(jnp.float32) + got[half:].astype(jnp.float32)).astype(jnp.bfloat16)
        new = swap(sent, mask)
        kept = (kept[:half].astype(jnp.float32) + got[:half].astype(jnp.float32)).astype(jnp.bfloat16)
        got = new
        half //= 2
    return (kept[0].astype(jnp.float32) + got[0].astype(jnp.float32))


def sum_all(values):
    for mask in (CORE,) + STAGES[::-1]:
        values = values + swap(values, mask)
    return values


def cut_columns(matrix):
    rows, columns = matrix.shape
    return matrix.reshape(rows, columns // 512, 512).transpose(1, 0, 2).reshape(-1, 512)


def pieces_of(matrix):
    by_piece = matrix.reshape(32, matrix.shape[0] // 32, -1, 512)
    return jnp.moveaxis(by_piece, 2, 1).reshape(32, -1, 512)


def join_columns(pieces, columns):
    lead = pieces.shape[:-2]
    rows = pieces.shape[-2] // columns
    moved = jnp.moveaxis(pieces.reshape(*lead, columns, rows, 512), -3, -2)
    return moved.reshape(*lead, rows, columns * 512)


def local(
    frames,
    cotangent,
    seq_lengths,
    ffn_in_master,
    ffn_out_master,
    mix_in_master,
    mix_out_master,
    vector_master,
    ffn_in_first,
    ffn_out_first,
    mix_in_first,
    mix_out_first,
    vector_first,
    ffn_in_second,
    ffn_out_second,
    mix_in_second,
    mix_out_second,
    vector_second,
):
    seq_count, length, channels = frames.shape
    me = lax.axis_index(AXES)
    paired = (lax.axis_size("dp"), lax.axis_size("fsdp")) == (4, 8)
    spots = jnp.asarray(SPOTS)[me] if paired else jnp.arange(32)
    table = jnp.asarray(TABLES)[me] if paired else jnp.arange(32)
    low = jnp.bfloat16

    def pack(parts):
        return jnp.concatenate([cut_columns(part.astype(low)) for part in parts])

    def gather(parts, extra=None):
        if paired:
            return gather_pieces(pack(parts), extra)
        gathered = [lax.all_gather(part.astype(low), AXES, axis=0, tiled=True) for part in parts]
        pieces = jnp.concatenate([pieces_of(matrix) for matrix in gathered], axis=1)
        return pieces[:16], pieces[16:], None if extra is None else lax.psum(extra, AXES)

    def reduce(matrices):
        pieces = jnp.concatenate([pieces_of(matrix.astype(low)) for matrix in matrices], axis=1)
        if paired:
            pieces = jnp.take(pieces, table, axis=0)
            return reduce_pieces(pieces[:16], pieces[16:])
        sums = [lax.psum_scatter(m, AXES, scatter_dimension=0, tiled=True) for m in matrices]
        return jnp.concatenate([cut_columns(part) for part in sums])

    total = sum_all if paired else lambda values: lax.psum(values, AXES)
    width = vector_master.shape[1]
    placed = lax.dynamic_update_slice(
        jnp.zeros((32, 512), low), vector_master.astype(low), (0, width * me)
    )
    own0, other0, placed = gather([ffn_in_master[0], ffn_out_master[0]], placed)
    own1, other1, _ = gather([mix_in_master[0], mix_out_master[0], mix_in_master[1], mix_out_master[1]])
    own2, other2, _ = gather([ffn_in_master[1], ffn_out_master[1]])

    def natural(own, other):
        return jnp.take(jnp.concatenate([own, other]), spots, axis=0)

    def whole(pieces, columns):
        return join_columns(pieces, columns).reshape(-1, 512 * columns)

    nat0, nat1, nat2 = natural(own0, other0), natural(own1, other1), natural(own2, other2)
    gathered = (
        (whole(nat0[:, :64], 4), whole(nat2[:, :64], 4)),
        (whole(nat0[:, 64:], 1), whole(nat2[:, 64:], 1)),
        (whole(nat1[:, :32], 2), whole(nat1[:, 48:80], 2)),
        (whole(nat1[:, 32:48], 1), whole(nat1[:, 80:96], 1)),
        placed[:30],
    )
    vectors = gathered[4].astype(jnp.float32)
    positions = jnp.arange(length, dtype=jnp.int32)
    valid = (positions[None, :] < seq_lengths[:, None]).astype(jnp.float32)[:, :, None]

    def silu_fn(projected, params):
        return jax.nn.silu(projected)

    def ssm_fn(projected, params):
        return ssm_piece(projected, valid, params)

    def conv_fn(projected, params):
        return conv_piece(projected, valid, params)

    local_fns = (silu_fn, ssm_fn, conv_fn, silu_fn)
    norm_indices = (0, 1, 2, 4)
    scales = (0.5, 1.0, 1.0, 0.5)
    stack_index = (0, 0, 1, 1)
    is_ffn = (True, False, False, True)

    def weight_pair(weights, module):
        which = stack_index[module]
        if is_ffn[module]:
            return (weights[0][which], weights[1][which])
        return (weights[2][which], weights[3][which])

    residual = frames.astype(jnp.float32)
    saved_all = []
    piece_outs = []
    for module in range(4):
        weight_in, weight_out = weight_pair(gathered, module)
        output, saved = run_branch(
            residual, norm_indices[module], weight_in, weight_out, local_fns[module], vectors
        )
        branch_part = scales[module] * output
        piece_outs.append(branch_part)
        saved_all.append(saved)
        residual = residual + branch_part
    activations, pull_final = jax.vjp(
        lambda values, params: layer_norm(values, params, 5), residual, vectors
    )
    piece_outs.append(residual)
    squares = [jnp.sum(valid * piece_out * piece_out) for piece_out in piece_outs]
    local_stats = jnp.stack(squares + [jnp.sum(valid)])
    global_stats = total(jnp.pad(local_stats, (0, 122))[None] * jnp.ones((8, 1)))[0]
    grad_residual, grad_vectors = pull_final(cotangent.astype(jnp.float32))
    back_weights = gathered
    grad_ins = [None, None, None, None]
    grad_outs = [None, None, None, None]
    for module in (3, 2, 1, 0):
        weight_in, weight_out = weight_pair(back_weights, module)
        grad_branch, grad_in_weight, grad_out_weight, grad_vec_more = back_branch(
            scales[module] * grad_residual, saved_all[module], weight_in, weight_out
        )
        grad_residual = grad_residual + grad_branch
        grad_vectors = grad_vectors + grad_vec_more
        grad_ins[module] = grad_in_weight
        grad_outs[module] = grad_out_weight
    sum2 = reduce([grad_ins[3], grad_outs[3]])
    sum1 = reduce([grad_ins[1], grad_outs[1], grad_ins[2], grad_outs[2]])
    sum0 = reduce([grad_ins[0], grad_outs[0]])
    all_vectors = total(jnp.pad(grad_vectors, ((0, 2), (0, 0))))
    n = ffn_in_master.shape[1]
    reduced = (
        jnp.stack([join_columns(sum0[: 4 * n], 4), join_columns(sum2[: 4 * n], 4)]),
        jnp.stack([sum0[4 * n :], sum2[4 * n :]]),
        jnp.stack([join_columns(sum1[: 2 * n], 2), join_columns(sum1[3 * n : 5 * n], 2)]),
        jnp.stack([sum1[2 * n : 3 * n], sum1[5 * n :]]),
        lax.dynamic_slice(all_vectors, (0, width * me), (30, width)),
    )
    sublayer_rms = jnp.sqrt(global_stats[:5] / (global_stats[5] * channels))
    masters = (ffn_in_master, ffn_out_master, mix_in_master, mix_out_master, vector_master)
    firsts = (ffn_in_first, ffn_out_first, mix_in_first, mix_out_first, vector_first)
    seconds = (ffn_in_second, ffn_out_second, mix_in_second, mix_out_second, vector_second)
    results = [
        adamw(
            masters[slot_index],
            firsts[slot_index],
            seconds[slot_index],
            reduced[slot_index],
            RATE_MATRIX if slot_index < 4 else RATE_VECTOR,
            WEIGHT_DECAY if slot_index < 4 else 0.0,
        )
        for slot_index in range(5)
    ]
    return (
        activations,
        grad_residual,
        results[0][0],
        results[1][0],
        results[2][0],
        results[3][0],
        results[4][0],
        results[0][1],
        results[1][1],
        results[2][1],
        results[3][1],
        results[4][1],
        results[0][2],
        results[1][2],
        results[2][2],
        results[3][2],
        results[4][2],
        results[0][3],
        results[1][3],
        results[2][3],
        results[3][3],
        results[4][3],
        sublayer_rms,
    )


def solution(mesh):
    return jax.shard_map(
        local,
        mesh=mesh,
        in_specs=(
            P(("dp", "fsdp"), None, None),
            P(("dp", "fsdp"), None, None),
            P(("dp", "fsdp")),
            P(None, ("dp", "fsdp"), None),
            P(None, ("dp", "fsdp"), None),
            P(None, ("dp", "fsdp"), None),
            P(None, ("dp", "fsdp"), None),
            P(None, ("dp", "fsdp")),
            P(None, ("dp", "fsdp"), None),
            P(None, ("dp", "fsdp"), None),
            P(None, ("dp", "fsdp"), None),
            P(None, ("dp", "fsdp"), None),
            P(None, ("dp", "fsdp")),
            P(None, ("dp", "fsdp"), None),
            P(None, ("dp", "fsdp"), None),
            P(None, ("dp", "fsdp"), None),
            P(None, ("dp", "fsdp"), None),
            P(None, ("dp", "fsdp")),
        ),
        out_specs=(
            P(("dp", "fsdp"), None, None),
            P(("dp", "fsdp"), None, None),
            P(None, ("dp", "fsdp"), None),
            P(None, ("dp", "fsdp"), None),
            P(None, ("dp", "fsdp"), None),
            P(None, ("dp", "fsdp"), None),
            P(None, ("dp", "fsdp")),
            P(None, ("dp", "fsdp"), None),
            P(None, ("dp", "fsdp"), None),
            P(None, ("dp", "fsdp"), None),
            P(None, ("dp", "fsdp"), None),
            P(None, ("dp", "fsdp")),
            P(None, ("dp", "fsdp"), None),
            P(None, ("dp", "fsdp"), None),
            P(None, ("dp", "fsdp"), None),
            P(None, ("dp", "fsdp"), None),
            P(None, ("dp", "fsdp")),
            P(None, ("dp", "fsdp"), None),
            P(None, ("dp", "fsdp"), None),
            P(None, ("dp", "fsdp"), None),
            P(None, ("dp", "fsdp"), None),
            P(None, ("dp", "fsdp")),
            P(),
        ),
        check_vma=False,
    )
```

```python
import jax
import numpy as np
import jax.numpy as jnp
from jax import lax
from jax.experimental import pallas as pl
from jax.experimental.pallas import tpu as pltpu
from jax.sharding import PartitionSpec as P

HEADS = 8
NSTATE = 32
KERNEL = 15
STEP_NUMBER = 5


NORM_EPS = 1e-05
BETA_FIRST = 0.5
BETA_SECOND = 0.6
ADAM_EPS = 1e-08
RATE_MATRIX = 0.02
RATE_VECTOR = 0.2
WEIGHT_DECAY = 0.01


def adamw(master, first, second, gradient, rate, decay):
    first_new = BETA_FIRST * first + (1.0 - BETA_FIRST) * gradient
    second_new = BETA_SECOND * second + (1.0 - BETA_SECOND) * gradient * gradient
    first_hat = first_new / (1.0 - BETA_FIRST**STEP_NUMBER)
    second_hat = second_new / (1.0 - BETA_SECOND**STEP_NUMBER)
    updated = master - rate * (first_hat / (jnp.sqrt(second_hat) + ADAM_EPS) + decay * master)
    return (updated, first_new, second_new, updated.astype(jnp.bfloat16))


def piece_tables():
    tables = []
    for me in range(32):
        core = (me >> 3) & 1
        pieces = []
        for side in (0, 1):
            base = me ^ (8 * side)
            across = ((16, 1), (1, 16))[core ^ side]
            for spot in range(16):
                rel = (across[0] if spot & 8 else 0) | (across[1] if spot & 4 else 0)
                rel |= (2 if spot & 2 else 0) | (4 if spot & 1 else 0)
                pieces.append(base ^ rel)
        tables.append(pieces)
    return np.array(tables, np.int32)


TABLES = piece_tables()
SPOTS = np.argsort(TABLES, axis=1).astype(np.int32)
AXES = ("dp", "fsdp")
CORE, Z_HIGH, Z_LOW = 8, 4, 2
STAGES = (Z_HIGH, Z_LOW, (1, 16), (16, 1))


def swap(values, mask):
    masks = mask if isinstance(mask, tuple) else (mask, mask)
    return lax.ppermute(values, AXES, [(i, i ^ masks[(i >> 3) & 1]) for i in range(32)])


def gather_pieces(shard, extra=None):
    rows = shard.shape[0]
    held = shard[None]
    for mask in STAGES + (CORE,):
        if extra is None:
            got = swap(held, mask)
        else:
            sent = jnp.concatenate([held.reshape(-1, 512), extra])
            got = swap(sent, mask)
            extra = extra + got[-extra.shape[0] :]
            got = got[: -extra.shape[0]].reshape(held.shape)
        if mask != CORE:
            held = jnp.concatenate([held, got])
    return held, got, extra


def reduce_pieces(kept, sent):
    got = swap(sent, CORE)
    half = 8
    for mask in STAGES[::-1]:
        sent = (kept[half:].astype(jnp.float32) + got[half:].astype(jnp.float32)).astype(jnp.bfloat16)
        new = swap(sent, mask)
        kept = (kept[:half].astype(jnp.float32) + got[:half].astype(jnp.float32)).astype(jnp.bfloat16)
        got = new
        half //= 2
    return (kept[0].astype(jnp.float32) + got[0].astype(jnp.float32))


def sum_all(values):
    for mask in (CORE,) + STAGES[::-1]:
        values = values + swap(values, mask)
    return values


def cut_columns(matrix):
    rows, columns = matrix.shape
    return matrix.reshape(rows, columns // 512, 512).transpose(1, 0, 2).reshape(-1, 512)


def pieces_of(matrix):
    by_piece = matrix.reshape(32, matrix.shape[0] // 32, -1, 512)
    return jnp.moveaxis(by_piece, 2, 1).reshape(32, -1, 512)


def join_columns(pieces, columns):
    lead = pieces.shape[:-2]
    rows = pieces.shape[-2] // columns
    moved = jnp.moveaxis(pieces.reshape(*lead, columns, rows, 512), -3, -2)
    return moved.reshape(*lead, rows, columns * 512)


TILE = 64
F32, LOW = jnp.float32, jnp.bfloat16
NN, NT, TN = ((1,), (0,)), ((1,), (1,)), ((0,), (0,))
VMEM_BYTES = 56 * 1024 * 1024


def mm(left, right, dims=NN):
    return lax.dot_general(left, right, (dims, ((), ())), preferred_element_type=F32)


def tiles(rows=512, step=TILE):
    return [pl.ds(start, step) for start in range(0, rows, step)]


def sigmoid(values):
    return 0.5 * jnp.tanh(0.5 * values) + 0.5


def standardize(values):
    centered = values - jnp.mean(values, axis=-1, keepdims=True)
    variance = jnp.mean(centered * centered, axis=-1, keepdims=True)
    spread = lax.rsqrt(variance + NORM_EPS)
    return centered * spread, spread


def standardize_back(grad, unit, spread):
    mean_grad = jnp.mean(grad, axis=-1, keepdims=True)
    mean_both = jnp.mean(grad * unit, axis=-1, keepdims=True)
    return spread * (grad - mean_grad - unit * mean_both)


def row(values):
    return jnp.sum(values, axis=0, keepdims=True)


def square(pieces):
    return pieces.reshape(512, 512)


def fetch(table, own, other, jobs, sem):
    def each(spot, what):
        device = table[spot]
        for side, source in ((0, own), (1, other)):
            for first, count, target in jobs:
                copy = pltpu.make_async_copy(
                    source.at[spot, pl.ds(first, count)], target(table[16 * side + spot]), sem
                )
                getattr(copy, what)()

    lax.fori_loop(0, 16, lambda spot, _: (each(spot, "start"), 0)[1], 0)
    return lambda: lax.fori_loop(0, 16, lambda spot, _: (each(spot, "wait"), 0)[1], 0)


def fetch_ffn(table, own, other, w_in, w_out, sem):
    return fetch(
        table,
        own,
        other,
        [(0, 4, lambda d: w_in.at[:, d]), (4, 4, lambda d: w_out.at[pl.ds(4 * d, 4)])],
        sem,
    )


def fetch_mix(table, own, other, first, w_in, w_out, sem):
    return fetch(
        table,
        own,
        other,
        [(first, 2, lambda d: w_in.at[:, d]), (first + 2, 1, lambda d: w_out.at[pl.ds(d, 1)])],
        sem,
    )


def fill_normed(h_ref, vec_ref, index, normed):
    gain = vec_ref[pl.ds(2 * index, 1)].astype(F32)
    shift = vec_ref[pl.ds(2 * index + 1, 1)].astype(F32)
    for part in tiles():
        unit, _ = standardize(h_ref[part].astype(F32))
        normed[part] = (unit * gain + shift).astype(LOW)


def order_rows(table, natural, ordered):
    def each(spot, _):
        ordered[spot] = natural[table[spot]]
        return 0

    lax.fori_loop(0, 32, each, 0)


def fill_transposed(source, natural):
    for part in tiles(step=128):
        turned = source[part].astype(F32).T.astype(LOW)
        natural[:, :, part] = turned.reshape(32, 16, 128)


def norm_back(h_ref, vec_ref, index, grad_normed, grad_in, grad_out):
    gain = vec_ref[pl.ds(2 * index, 1)].astype(F32)
    grad_gain, grad_shift = jnp.zeros((1, 512), F32), jnp.zeros((1, 512), F32)
    for part in tiles():
        unit, spread = standardize(h_ref[part].astype(F32))
        grad = grad_normed[part]
        grad_gain = grad_gain + row(grad * unit)
        grad_shift = grad_shift + row(grad)
        grad_out[part] = grad_in[part] + standardize_back(grad * gain, unit, spread)
    return grad_gain, grad_shift


def valid_rows(length, part):
    places = part.start + lax.broadcasted_iota(jnp.int32, (part.size, 1), 0)
    return (places < length).astype(F32)


def valid_lanes(length):
    return (lax.broadcasted_iota(jnp.int32, (1, 512), 1) < length).astype(F32)


def ffn_forward(length, h_ref, normed, w_in, w_out, pre, act, out, new_h, keep_pre):
    for j in range(4):
        pre_j = pre.at[j]
        pre_j[...] = mm(normed[...], square(w_in[j]))
        keep_pre(j)
        for part in tiles():
            values = pre_j[part]
            act[part] = (values * sigmoid(values)).astype(LOW)
        more = mm(act[...], square(w_out[pl.ds(32 * j, 32)]))
        out[...] = more if j == 0 else out[...] + more
    total = jnp.zeros((1, 512), F32)
    for part in tiles():
        half = 0.5 * out[part]
        new_h[part] = h_ref[part].astype(F32) + half
        total = total + row(valid_rows(length, part) * half * half)
    return total


def ffn_backward(spots, w_in, w_out, pre, grad_low, turned, act, grad_pre, grad_normed, grads):
    for j in range(4):
        pre_j = pre(j)
        grad_act = mm(grad_low[...], square(w_out[pl.ds(32 * j, 32)]), NT)
        grad_normed_more = None
        for part in tiles():
            values = pre_j[part]
            gate = sigmoid(values)
            lifted = values * gate
            act[part] = lifted.astype(LOW)
            slope = gate + lifted * (1.0 - gate)
            grad_pre[part] = (grad_act[part.start : part.start + part.size] * slope).astype(LOW)
        more = mm(grad_pre[...], square(w_in[j]), NT)
        grad_normed[...] = more if j == 0 else grad_normed[...] + more
        grads[:, j] = mm(square(turned[...]), grad_pre[...]).astype(LOW).reshape(32, 16, 512)
        grad_out_w = mm(act[...], grad_low[...], TN).astype(LOW).reshape(8, 4, 16, 512)
        for f in range(8):
            grads[spots[8 * j + f], pl.ds(4, 4)] = grad_out_w[f]


def first_kernel(
    table, length, h_ref, vec_ref, own, other, h1_ref, pre_hbm, stat_ref, w_in, w_out, normed, act, out, pre, sem, pre_sem
):
    finish = fetch_ffn(table, own, other, w_in, w_out, sem)
    fill_normed(h_ref, vec_ref, 0, normed)
    finish()

    def copy_of(j):
        return pltpu.make_async_copy(pre.at[j], pre_hbm.at[j], pre_sem.at[j])

    stat_ref[...] = ffn_forward(
        length[0], h_ref, normed, w_in, w_out, pre, act, out, h1_ref, lambda j: copy_of(j).start()
    )
    for j in range(4):
        copy_of(j).wait()


def last_kernel(
    table, spots, length, h_ref, vec_ref, cot_ref, own, other,
    top_ref, grad_ref, rows_ref, kept_hbm, sent_hbm,
    w_in, w_out, normed, act, out, pre, low, natural, turned, grads, sem, out_sem
):
    finish = fetch_ffn(table, own, other, w_in, w_out, sem)
    fill_normed(h_ref, vec_ref, 4, normed)
    fill_transposed(normed, natural)
    order_rows(table, natural, turned)
    finish()
    stat4 = ffn_forward(length[0], h_ref, normed, w_in, w_out, pre, act, out, grad_ref, lambda j: None)
    gain, shift = vec_ref[pl.ds(10, 1)].astype(F32), vec_ref[pl.ds(11, 1)].astype(F32)
    grad_gain, grad_shift = jnp.zeros((1, 512), F32), jnp.zeros((1, 512), F32)
    stat5 = jnp.zeros((1, 512), F32)
    for part in tiles():
        values = grad_ref[part]
        stat5 = stat5 + row(valid_rows(length[0], part) * values * values)
        unit, spread = standardize(values)
        top_ref[part] = unit * gain + shift
        grad = cot_ref[part].astype(F32)
        grad_gain = grad_gain + row(grad * unit)
        grad_shift = grad_shift + row(grad)
        back = standardize_back(grad * gain, unit, spread)
        grad_ref[part] = back
        low[part] = (0.5 * back).astype(LOW)
    ffn_backward(spots, w_in, w_out, lambda j: pre.at[j], low, turned, act, normed, out, grads)
    kept_copy = pltpu.make_async_copy(grads.at[pl.ds(0, 16)], kept_hbm, out_sem.at[0])
    sent_copy = pltpu.make_async_copy(grads.at[pl.ds(16, 16)], sent_hbm, out_sem.at[1])
    sent_copy.start()
    kept_copy.start()
    gain4, shift4 = norm_back(h_ref, vec_ref, 4, out, grad_ref, grad_ref)
    rows_ref[...] = jnp.concatenate(
        [gain4, shift4, grad_gain, grad_shift, stat4, stat5, jnp.zeros((2, 512), F32)]
    )
    sent_copy.wait()
    kept_copy.wait()


def back_first_kernel(
    table, spots, length, h_ref, vec_ref, grad_in, own, other, pre_hbm, rows3, rows2, rows1, stat1,
    grad_ref, rows_ref, kept_hbm, sent_hbm,
    w_in, w_out, normed, act, out, pre, low, natural, turned, grads, sem, pre_sem, out_sem
):
    finish = fetch_ffn(table, own, other, w_in, w_out, sem)
    copies = [pltpu.make_async_copy(pre_hbm.at[j], pre.at[j], pre_sem.at[j]) for j in range(4)]
    for copy in copies:
        copy.start()
    fill_normed(h_ref, vec_ref, 0, normed)
    fill_transposed(normed, natural)
    order_rows(table, natural, turned)
    for part in tiles():
        low[part] = (0.5 * grad_in[part]).astype(LOW)
    finish()

    def pre_of(j):
        copies[j].wait()
        return pre.at[j]

    ffn_backward(spots, w_in, w_out, pre_of, low, turned, act, normed, out, grads)
    kept_copy = pltpu.make_async_copy(grads.at[pl.ds(0, 16)], kept_hbm, out_sem.at[0])
    sent_copy = pltpu.make_async_copy(grads.at[pl.ds(16, 16)], sent_hbm, out_sem.at[1])
    sent_copy.start()
    kept_copy.start()
    gain0, shift0 = norm_back(h_ref, vec_ref, 0, out, grad_in, grad_ref)
    lanes = lax.broadcasted_iota(jnp.int32, (1, 512), 1)
    sums = [stat1[...], rows1[4:5], rows2[20:21], rows3[4:5], rows3[5:6]]
    stats = jnp.where(lanes == 5, length[0].astype(F32), 0.0)
    for place, values in enumerate(sums):
        stats = stats + jnp.where(lanes == place, jnp.sum(values, axis=1, keepdims=True), 0.0)
    rows_ref[...] = jnp.concatenate(
        [gain0, shift0, rows1[0:2], rows2[0:4], rows3[0:4], rows1[2:4], rows2[4:20], stats, jnp.zeros((1, 512), F32)]
    )
    sent_copy.wait()
    kept_copy.wait()


def vector_columns(vec_ref, pad):
    pad[...] = jnp.zeros((128, 512), F32)
    pad[pl.ds(0, 32)] = vec_ref[...].astype(F32)
    return pad[...].T


def ssm_decays(columns):
    rates = jnp.exp(columns[0:256, 13:14])
    lags = lax.broadcasted_iota(jnp.int32, (1, 512), 1).astype(F32)
    return jnp.exp(-rates * lags), rates, columns[256:512, 13:14]


def head_matrix(kernels, head):
    line = jnp.concatenate([kernels[head : head + 1], jnp.zeros((1, 128), F32)], axis=1)
    skewed = pltpu.roll(jnp.broadcast_to(line, (128, 640)), 0, 1, stride=1, stride_axis=0)
    return skewed[:, :512].astype(LOW)


def blocks_of(rows):
    return jnp.concatenate([rows[:, 128 * b : 128 * (b + 1)] for b in range(4)], axis=0)


def ssm_kernel(
    table, length, h_ref, vec_ref, own, other, h2_ref, saved_hbm, stat_ref, w_in, w_out, normed, act, saved, pad, sem, save_sem
):
    finish = fetch_mix(table, own, other, 0, w_in, w_out, sem)
    fill_normed(h_ref, vec_ref, 1, normed)
    columns = vector_columns(vec_ref, pad)
    decays, _, coefs = ssm_decays(columns)
    kernels = jnp.sum((coefs * decays).reshape(8, 32, 512), axis=1)
    finish()
    mask = valid_lanes(length[0])
    signal, gate, mixed = saved.at[0], saved.at[1], saved.at[2]
    signal[...] = mm(square(w_in[0]), normed[...], ((0,), (1,))) * mask
    gate[...] = mm(square(w_in[1]), normed[...], ((0,), (1,)))
    copies = [pltpu.make_async_copy(saved.at[k], saved_hbm.at[k], save_sem.at[k]) for k in range(3)]
    copies[0].start()
    copies[1].start()
    for head in range(8):
        part = pl.ds(64 * head, 64)
        rows = signal[part]
        spread = mm(blocks_of(rows).astype(LOW), head_matrix(kernels, head))
        skip = columns[64 * head : 64 * head + 64, 12:13]
        for a in range(4):
            lanes = pl.ds(128 * a, 128)
            total = skip * rows[:, 128 * a : 128 * a + 128]
            for b in range(a + 1):
                total = total + spread[64 * b : 64 * b + 64, 128 * (a - b) : 128 * (a - b) + 128]
            mixed[part, lanes] = total
            gates = gate[part, lanes]
            act[part, lanes] = (total * gates * sigmoid(gates)).astype(LOW)
    copies[2].start()
    out = mm(act[...], square(w_out[...]), TN)
    total = jnp.zeros((1, 512), F32)
    for part in tiles():
        values = out[part.start : part.start + part.size]
        h2_ref[part] = h_ref[part] + values
        total = total + row(valid_rows(length[0], part) * values * values)
    stat_ref[...] = total
    for copy in copies:
        copy.wait()


def ssm_back_kernel(
    table, length, h_ref, vec_ref, grad_in, own, other, saved_hbm, stat_in,
    grad_ref, rows_ref, kept_hbm, sent_hbm,
    w_in, w_out, normed, saved, low, natural, turned, act, act_turned, grad_pre, out, grads, pad, kernel_grads,
    sem, save_sem, out_sem
):
    finish = fetch_mix(table, own, other, 0, w_in, w_out, sem)
    copies = [pltpu.make_async_copy(saved_hbm.at[k], saved.at[k], save_sem.at[k]) for k in range(3)]
    for copy in copies:
        copy.start()
    fill_normed(h_ref, vec_ref, 1, normed)
    fill_transposed(normed, natural)
    order_rows(table, natural, turned)
    for part in tiles():
        low[part] = grad_in[part].astype(LOW)
    columns = vector_columns(vec_ref, pad)
    decays, rates, coefs = ssm_decays(columns)
    kernels = jnp.sum((coefs * decays).reshape(8, 32, 512), axis=1)
    mask = valid_lanes(length[0])
    finish()
    for copy in copies:
        copy.wait()
    signal, gate, mixed = saved.at[0], saved.at[1], saved.at[2]
    out[...] = mm(square(w_out[...]), low[...], NT)
    flipped = lax.broadcasted_iota(jnp.int32, (128, 128), 0) + lax.broadcasted_iota(jnp.int32, (128, 128), 1)
    flip = (flipped == 127).astype(F32).astype(LOW)
    for head in range(8):
        part = pl.ds(64 * head, 64)
        rows, gates, mixes, grad_act = signal[part], gate[part], mixed[part], out[part]
        gating = sigmoid(gates)
        lifted = gates * gating
        act[pl.ds(4 * head, 4)] = (mixes * lifted).astype(LOW).reshape(4, 16, 512)
        grad_mixed = grad_act * lifted
        grad_pre[1, part] = (grad_act * mixes * (gating + lifted * (1.0 - gating))).astype(LOW)
        grad_low = grad_mixed.astype(LOW)
        shifted = jnp.concatenate(
            [grad_low]
            + [
                jnp.concatenate([grad_low[:, 128 * b :], jnp.zeros((64, 128 * b), LOW)], axis=1)
                for b in (1, 2, 3)
            ],
            axis=0,
        )
        back = mm(shifted, head_matrix(kernels, head), NT)
        mirrored = mm(blocks_of(rows).astype(LOW), flip).astype(LOW)
        lag_sums = mm(mirrored, shifted, TN)
        lag_sums = jnp.concatenate([lag_sums, jnp.zeros((128, 128), F32)], axis=1)
        lag_sums = row(pltpu.roll(lag_sums, 0, 1, stride=1, stride_axis=0))
        kernel_grads[pl.ds(head, 1)] = pltpu.roll(lag_sums, 640 - 127, 1)[:, :512]
        skip = columns[64 * head : 64 * head + 64, 12:13]
        pad_lane = jnp.sum(grad_mixed * rows, axis=1, keepdims=True)
        natural_grad = jnp.concatenate([back[64 * b : 64 * b + 64] for b in range(4)], axis=1)
        grad_pre[0, part] = ((natural_grad + skip * grad_mixed) * mask).astype(LOW)
        normed_f = jnp.broadcast_to(pad_lane, (64, 128))
        saved[0, part, pl.ds(0, 128)] = normed_f
    order_rows(table, act, act_turned)
    grads[:, 2] = mm(square(act_turned[...]), low[...]).astype(LOW).reshape(32, 16, 512)
    for q in range(2):
        more = mm(grad_pre[q], square(w_in[q]), ((0,), (1,)))
        out[...] = more if q == 0 else out[...] + more
        grads[:, q] = mm(square(turned[...]), grad_pre[q], NT).astype(LOW).reshape(32, 16, 512)
    kept_copy = pltpu.make_async_copy(grads.at[pl.ds(0, 16)], kept_hbm, out_sem.at[0])
    sent_copy = pltpu.make_async_copy(grads.at[pl.ds(16, 16)], sent_hbm, out_sem.at[1])
    sent_copy.start()
    kept_copy.start()
    gain1, shift1 = norm_back(h_ref, vec_ref, 1, out, grad_in, grad_ref)
    lag_grads = jnp.broadcast_to(kernel_grads[...].reshape(8, 1, 512), (8, 32, 512)).reshape(256, 512)
    lags = lax.broadcasted_iota(jnp.int32, (1, 512), 1).astype(F32)
    weighed = lag_grads * decays
    coef_grads = jnp.sum(weighed, axis=1, keepdims=True)
    rate_grads = -rates * coefs * jnp.sum(weighed * lags, axis=1, keepdims=True)
    lanes = lax.broadcasted_iota(jnp.int32, (1, 128), 1)
    ssm_column = jnp.concatenate([rate_grads, coef_grads], axis=0)
    both = jnp.where(lanes == 0, saved[0, :, pl.ds(0, 128)], 0.0) + jnp.where(lanes == 1, ssm_column, 0.0)
    turned_rows = both.T
    rows_ref[...] = jnp.concatenate(
        [gain1, shift1, turned_rows[0:2], stat_in[...], jnp.zeros((3, 512), F32)]
    )
    sent_copy.wait()
    kept_copy.wait()


PAD = 16


def conv_kernel(
    table, length, h_ref, vec_ref, own, other, h3_ref, saved_hbm, stat_ref, w_in, w_out, normed, act, saved, padded, sem, save_sem
):
    finish = fetch_mix(table, own, other, 3, w_in, w_out, sem)
    fill_normed(h_ref, vec_ref, 2, normed)
    finish()
    copies = [pltpu.make_async_copy(saved.at[k], saved_hbm.at[k], save_sem.at[k]) for k in range(3)]
    for q in range(2):
        saved[q] = mm(normed[...], square(w_in[q]))
        copies[q].start()
    for c in range(4):
        padded[c, pl.ds(0, PAD)] = jnp.zeros((PAD, 128), F32)
        padded[c, pl.ds(PAD + 512, PAD)] = jnp.zeros((PAD, 128), F32)
        lanes = pl.ds(128 * c, 128)
        for part in tiles():
            glu = saved[0, part, lanes] * sigmoid(saved[1, part, lanes]) * valid_rows(length[0], part)
            padded[c, pl.ds(PAD + part.start, part.size)] = glu
        taps = [vec_ref[pl.ds(14 + j, 1), lanes].astype(F32) for j in range(KERNEL + 1)]
        for part in tiles():
            total = jnp.broadcast_to(taps[KERNEL], (part.size, 128))
            for j in range(KERNEL):
                total = total + padded[c, pl.ds(PAD + part.start + j - 7, part.size)] * taps[j]
            saved[2, part, lanes] = total
    copies[2].start()
    gain, shift = vec_ref[pl.ds(6, 1)].astype(F32), vec_ref[pl.ds(7, 1)].astype(F32)
    for part in tiles():
        unit, _ = standardize(saved[2, part])
        values = unit * gain + shift
        act[part] = (values * sigmoid(values)).astype(LOW)
    out = mm(act[...], square(w_out[...]))
    total = jnp.zeros((1, 512), F32)
    for part in tiles():
        values = out[part.start : part.start + part.size]
        h3_ref[part] = h_ref[part] + values
        total = total + row(valid_rows(length[0], part) * values * values)
    stat_ref[...] = total
    for copy in copies:
        copy.wait()


def conv_back_kernel(
    table, length, h_ref, vec_ref, grad_in, own, other, saved_hbm, stat_in,
    grad_ref, rows_ref, kept_hbm, sent_hbm,
    w_in, w_out, normed, saved, low, natural, turned, act, act_turned, grad_pre, out, grads, padded, padded_grad,
    sem, save_sem, out_sem
):
    finish = fetch_mix(table, own, other, 3, w_in, w_out, sem)
    copies = [pltpu.make_async_copy(saved_hbm.at[k], saved.at[k], save_sem.at[k]) for k in range(3)]
    for copy in copies:
        copy.start()
    fill_normed(h_ref, vec_ref, 2, normed)
    fill_transposed(normed, natural)
    order_rows(table, natural, turned)
    for part in tiles():
        low[part] = grad_in[part].astype(LOW)
    finish()
    for copy in copies:
        copy.wait()
    out[...] = mm(low[...], square(w_out[...]), NT)
    gain, shift = vec_ref[pl.ds(6, 1)].astype(F32), vec_ref[pl.ds(7, 1)].astype(F32)
    gain3, shift3, bias = (jnp.zeros((1, 512), F32) for _ in range(3))
    for part in tiles():
        unit, spread = standardize(saved[2, part])
        values = unit * gain + shift
        gating = sigmoid(values)
        lifted = values * gating
        normed[part] = lifted.astype(LOW)
        grad = out[part] * (gating + lifted * (1.0 - gating))
        gain3 = gain3 + row(grad * unit)
        shift3 = shift3 + row(grad)
        back = standardize_back(grad * gain, unit, spread)
        bias = bias + row(back)
        for c in range(4):
            padded_grad[c, pl.ds(PAD + part.start, part.size)] = back[:, 128 * c : 128 * c + 128]
    fill_transposed(normed, act)
    order_rows(table, act, act_turned)
    grads[:, 2] = mm(square(act_turned[...]), low[...]).astype(LOW).reshape(32, 16, 512)
    tap_rows = []
    for c in range(4):
        lanes = pl.ds(128 * c, 128)
        for ref in (padded, padded_grad):
            ref[c, pl.ds(0, PAD)] = jnp.zeros((PAD, 128), F32)
            ref[c, pl.ds(PAD + 512, PAD)] = jnp.zeros((PAD, 128), F32)
        for part in tiles():
            glu = saved[0, part, lanes] * sigmoid(saved[1, part, lanes]) * valid_rows(length[0], part)
            padded[c, pl.ds(PAD + part.start, part.size)] = glu
        taps = [vec_ref[pl.ds(14 + j, 1), lanes].astype(F32) for j in range(KERNEL)]
        sums = [jnp.zeros((8, 128), F32) for _ in range(KERNEL)]
        for part in tiles():
            total = jnp.zeros((part.size, 128), F32)
            grad = padded_grad[c, pl.ds(PAD + part.start, part.size)]
            for j in range(KERNEL):
                total = total + padded_grad[c, pl.ds(PAD + part.start + 7 - j, part.size)] * taps[j]
                seen = padded[c, pl.ds(PAD + part.start + j - 7, part.size)]
                sums[j] = sums[j] + jnp.sum((grad * seen).reshape(part.size // 8, 8, 128), axis=0)
            total = total * valid_rows(length[0], part)
            gating = sigmoid(saved[1, part, lanes])
            first = total * gating
            grad_pre[0, part, lanes] = first.astype(LOW)
            grad_pre[1, part, lanes] = (first * saved[0, part, lanes] * (1.0 - gating)).astype(LOW)
        tap_rows.append(jnp.concatenate([row(values) for values in sums], axis=0))
    for q in range(2):
        more = mm(grad_pre[q], square(w_in[q]), NT)
        out[...] = more if q == 0 else out[...] + more
        grads[:, q] = mm(square(turned[...]), grad_pre[q]).astype(LOW).reshape(32, 16, 512)
    kept_copy = pltpu.make_async_copy(grads.at[pl.ds(0, 16)], kept_hbm, out_sem.at[0])
    sent_copy = pltpu.make_async_copy(grads.at[pl.ds(16, 16)], sent_hbm, out_sem.at[1])
    sent_copy.start()
    kept_copy.start()
    gain2, shift2 = norm_back(h_ref, vec_ref, 2, out, grad_in, grad_ref)
    rows_ref[...] = jnp.concatenate(
        [gain2, shift2, gain3, shift3, jnp.concatenate(tap_rows, axis=1), bias, stat_in[...], jnp.zeros((3, 512), F32)]
    )
    sent_copy.wait()
    kept_copy.wait()


def call(kernel, scalars, arrays, outs, scratch, flops=0):
    whole = pl.BlockSpec(memory_space=pltpu.VMEM)
    there = pl.BlockSpec(memory_space=pl.ANY)
    return pl.pallas_call(
        kernel,
        out_shape=[jax.ShapeDtypeStruct(shape, dtype) for shape, dtype, _ in outs],
        in_specs=[pl.BlockSpec(memory_space=pltpu.SMEM)] * len(scalars)
        + [there if stays else whole for _, stays in arrays],
        out_specs=[there if stays else whole for _, _, stays in outs],
        scratch_shapes=scratch,
        compiler_params=pltpu.CompilerParams(vmem_limit_bytes=VMEM_BYTES),
        cost_estimate=pl.CostEstimate(flops=flops, bytes_accessed=8 << 20, transcendentals=1 << 20),
    )(*scalars, *[array for array, _ in arrays])


SQUARE, PIECES = (512, 512), (32, 16, 512)
DMA = pltpu.SemaphoreType.DMA


def run_first(table, length, h, vectors, own, other):
    return call(
        first_kernel,
        [table, length],
        [(h, False), (vectors, False), (own, True), (other, True)],
        [(SQUARE, F32, False), ((4, 512, 512), F32, True), ((1, 512), F32, False)],
        [
            pltpu.VMEM((4, 32, 16, 512), LOW), pltpu.VMEM((128, 16, 512), LOW), pltpu.VMEM(SQUARE, LOW),
            pltpu.VMEM(SQUARE, LOW), pltpu.VMEM(SQUARE, F32), pltpu.VMEM((4, 512, 512), F32), DMA, DMA((4,)),
        ],
        2 * 2 * 512 * 512 * 2048,
    )


FFN_GRADS = ((16, 8, 16, 512), LOW, True)
MIX_GRADS = ((16, 3, 16, 512), LOW, True)


def run_last(table, spots, length, h, vectors, cotangent, own, other):
    return call(
        last_kernel,
        [table, spots, length],
        [(h, False), (vectors, False), (cotangent, False), (own, True), (other, True)],
        [(SQUARE, F32, False), (SQUARE, F32, False), ((8, 512), F32, False), FFN_GRADS, FFN_GRADS],
        [
            pltpu.VMEM((4, 32, 16, 512), LOW), pltpu.VMEM((128, 16, 512), LOW), pltpu.VMEM(SQUARE, LOW),
            pltpu.VMEM(SQUARE, LOW), pltpu.VMEM(SQUARE, F32), pltpu.VMEM((4, 512, 512), F32), pltpu.VMEM(SQUARE, LOW),
            pltpu.VMEM(PIECES, LOW), pltpu.VMEM(PIECES, LOW), pltpu.VMEM((32, 8, 16, 512), LOW), DMA, DMA((2,)),
        ],
        6 * 2 * 512 * 512 * 2048,
    )


def run_back_first(table, spots, length, h, vectors, grad, own, other, pre, rows3, rows2, rows1, stat1):
    return call(
        back_first_kernel,
        [table, spots, length],
        [(h, False), (vectors, False), (grad, False), (own, True), (other, True), (pre, True)]
        + [(rows3, False), (rows2, False), (rows1, False), (stat1, False)],
        [(SQUARE, F32, False), ((32, 512), F32, False), FFN_GRADS, FFN_GRADS],
        [
            pltpu.VMEM((4, 32, 16, 512), LOW), pltpu.VMEM((128, 16, 512), LOW), pltpu.VMEM(SQUARE, LOW),
            pltpu.VMEM(SQUARE, LOW), pltpu.VMEM(SQUARE, F32), pltpu.VMEM((4, 512, 512), F32), pltpu.VMEM(SQUARE, LOW),
            pltpu.VMEM(PIECES, LOW), pltpu.VMEM(PIECES, LOW), pltpu.VMEM((32, 8, 16, 512), LOW), DMA, DMA((4,)), DMA((2,)),
        ],
        4 * 2 * 512 * 512 * 2048,
    )


def run_mix(kernel, table, length, h, vectors, own, other, last_scratch):
    return call(
        kernel,
        [table, length],
        [(h, False), (vectors, False), (own, True), (other, True)],
        [(SQUARE, F32, False), ((3, 512, 512), F32, True), ((1, 512), F32, False)],
        [
            pltpu.VMEM((2, 32, 16, 512), LOW), pltpu.VMEM(PIECES, LOW), pltpu.VMEM(SQUARE, LOW),
            pltpu.VMEM(SQUARE, LOW), pltpu.VMEM((3, 512, 512), F32), last_scratch, DMA, DMA((3,)),
        ],
        4 * 2 * 512 * 512 * 512,
    )


def run_mix_back(kernel, table, length, h, vectors, grad, own, other, saved, stat, rows, last_scratch):
    return call(
        kernel,
        [table, length],
        [(h, False), (vectors, False), (grad, False), (own, True), (other, True), (saved, True), (stat, False)],
        [(SQUARE, F32, False), ((rows, 512), F32, False), MIX_GRADS, MIX_GRADS],
        [
            pltpu.VMEM((2, 32, 16, 512), LOW), pltpu.VMEM(PIECES, LOW), pltpu.VMEM(SQUARE, LOW),
            pltpu.VMEM((3, 512, 512), F32), pltpu.VMEM(SQUARE, LOW), pltpu.VMEM(PIECES, LOW), pltpu.VMEM(PIECES, LOW),
            pltpu.VMEM(PIECES, LOW), pltpu.VMEM(PIECES, LOW), pltpu.VMEM((2, 512, 512), LOW), pltpu.VMEM(SQUARE, F32),
            pltpu.VMEM((32, 3, 16, 512), LOW), *last_scratch, DMA, DMA((3,)), DMA((2,)),
        ],
        8 * 2 * 512 * 512 * 512,
    )


def local(
    frames,
    cotangent,
    seq_lengths,
    ffn_in_master,
    ffn_out_master,
    mix_in_master,
    mix_out_master,
    vector_master,
    ffn_in_first,
    ffn_out_first,
    mix_in_first,
    mix_out_first,
    vector_first,
    ffn_in_second,
    ffn_out_second,
    mix_in_second,
    mix_out_second,
    vector_second,
):
    me = lax.axis_index(AXES)
    paired = (lax.axis_size("dp"), lax.axis_size("fsdp")) == (4, 8)
    spots = jnp.asarray(SPOTS)[me] if paired else jnp.arange(32, dtype=jnp.int32)
    table = jnp.asarray(TABLES)[me] if paired else jnp.arange(32, dtype=jnp.int32)
    low = jnp.bfloat16

    def gather(parts, extra=None):
        if paired:
            return gather_pieces(jnp.concatenate([cut_columns(part.astype(low)) for part in parts]), extra)
        gathered = [lax.all_gather(part.astype(low), AXES, axis=0, tiled=True) for part in parts]
        pieces = jnp.concatenate([pieces_of(matrix) for matrix in gathered], axis=1)
        return pieces[:16], pieces[16:], None if extra is None else lax.psum(extra, AXES)

    def reduce(kept, sent, columns):
        kept, sent = (pieces.reshape(16, -1, 512) for pieces in (kept, sent))
        if paired:
            return reduce_pieces(kept, sent)
        pieces, sums, start = jnp.concatenate([kept, sent]), [], 0
        for count, tall in columns:
            rows = 16 * count * tall
            matrix = join_columns(pieces[:, start : start + rows], count).reshape(512 * tall, -1)
            total_of = lax.psum_scatter(matrix.astype(jnp.float32), AXES, scatter_dimension=0, tiled=True)
            sums.append(cut_columns(total_of))
            start += rows
        return jnp.concatenate(sums)

    total = sum_all if paired else lambda values: lax.psum(values, AXES)
    width = vector_master.shape[1]
    placed = lax.dynamic_update_slice(
        jnp.zeros((32, 512), low), vector_master.astype(low), (0, width * me)
    )
    own0, other0, vectors = gather([ffn_in_master[0], ffn_out_master[0]], placed)
    own1, other1, _ = gather([mix_in_master[0], mix_out_master[0], mix_in_master[1], mix_out_master[1]])
    own2, other2, _ = gather([ffn_in_master[1], ffn_out_master[1]])
    own0, other0, own1, other1, own2, other2 = (
        pieces.reshape(16, -1, 16, 512) for pieces in (own0, other0, own1, other1, own2, other2)
    )

    h0, length = frames[0], seq_lengths
    h1, pre0, stat1 = run_first(table, length, h0, vectors, own0, other0)
    h2, saved1, stat2 = run_mix(
        ssm_kernel, table, length, h1, vectors, own1, other1, pltpu.VMEM((128, 512), F32)
    )
    h3, saved2, stat3 = run_mix(
        conv_kernel, table, length, h2, vectors, own1, other1, pltpu.VMEM((4, 512 + 2 * PAD, 128), F32)
    )
    activations, grad3, rows3, kept3, sent3 = run_last(
        table, spots, length, h3, vectors, cotangent[0], own2, other2
    )
    sum2 = reduce(kept3, sent3, ((4, 1), (1, 4)))
    grad2, rows2, kept2, sent2 = run_mix_back(
        conv_back_kernel, table, length, h2, vectors, grad3, own1, other1, saved2, stat3, 24,
        [pltpu.VMEM((4, 512 + 2 * PAD, 128), F32)] * 2,
    )
    grad1, rows1, kept1, sent1 = run_mix_back(
        ssm_back_kernel, table, length, h1, vectors, grad2, own1, other1, saved1, stat2, 8,
        [pltpu.VMEM((128, 512), F32), pltpu.VMEM((8, 512), F32)],
    )
    sum1 = reduce(
        jnp.concatenate([kept1, kept2], axis=1), jnp.concatenate([sent1, sent2], axis=1), ((2, 1), (1, 1)) * 2
    )
    grad0, rows, kept0, sent0 = run_back_first(
        table, spots, length, h0, vectors, grad1, own0, other0, pre0, rows3, rows2, rows1, stat1
    )
    sum0 = reduce(kept0, sent0, ((4, 1), (1, 4)))
    rows = total(rows)
    n = ffn_in_master.shape[1]
    reduced = (
        jnp.stack([join_columns(sum0[: 4 * n], 4), join_columns(sum2[: 4 * n], 4)]),
        jnp.stack([sum0[4 * n :], sum2[4 * n :]]),
        jnp.stack([join_columns(sum1[: 2 * n], 2), join_columns(sum1[3 * n : 5 * n], 2)]),
        jnp.stack([sum1[2 * n : 3 * n], sum1[5 * n :]]),
        lax.dynamic_slice(rows, (0, width * me), (30, width)),
    )
    sublayer_rms = jnp.sqrt(rows[30, :5] / (rows[30, 5] * frames.shape[2]))
    masters = (ffn_in_master, ffn_out_master, mix_in_master, mix_out_master, vector_master)
    firsts = (ffn_in_first, ffn_out_first, mix_in_first, mix_out_first, vector_first)
    seconds = (ffn_in_second, ffn_out_second, mix_in_second, mix_out_second, vector_second)
    results = [
        adamw(
            masters[slot_index],
            firsts[slot_index],
            seconds[slot_index],
            reduced[slot_index],
            RATE_MATRIX if slot_index < 4 else RATE_VECTOR,
            WEIGHT_DECAY if slot_index < 4 else 0.0,
        )
        for slot_index in range(5)
    ]
    return (
        activations[None],
        grad0[None],
        results[0][0],
        results[1][0],
        results[2][0],
        results[3][0],
        results[4][0],
        results[0][1],
        results[1][1],
        results[2][1],
        results[3][1],
        results[4][1],
        results[0][2],
        results[1][2],
        results[2][2],
        results[3][2],
        results[4][2],
        results[0][3],
        results[1][3],
        results[2][3],
        results[3][3],
        results[4][3],
        sublayer_rms,
    )


def solution(mesh):
    return jax.shard_map(
        local,
        mesh=mesh,
        in_specs=(
            P(("dp", "fsdp"), None, None),
            P(("dp", "fsdp"), None, None),
            P(("dp", "fsdp")),
            P(None, ("dp", "fsdp"), None),
            P(None, ("dp", "fsdp"), None),
            P(None, ("dp", "fsdp"), None),
            P(None, ("dp", "fsdp"), None),
            P(None, ("dp", "fsdp")),
            P(None, ("dp", "fsdp"), None),
            P(None, ("dp", "fsdp"), None),
            P(None, ("dp", "fsdp"), None),
            P(None, ("dp", "fsdp"), None),
            P(None, ("dp", "fsdp")),
            P(None, ("dp", "fsdp"), None),
            P(None, ("dp", "fsdp"), None),
            P(None, ("dp", "fsdp"), None),
            P(None, ("dp", "fsdp"), None),
            P(None, ("dp", "fsdp")),
        ),
        out_specs=(
            P(("dp", "fsdp"), None, None),
            P(("dp", "fsdp"), None, None),
            P(None, ("dp", "fsdp"), None),
            P(None, ("dp", "fsdp"), None),
            P(None, ("dp", "fsdp"), None),
            P(None, ("dp", "fsdp"), None),
            P(None, ("dp", "fsdp")),
            P(None, ("dp", "fsdp"), None),
            P(None, ("dp", "fsdp"), None),
            P(None, ("dp", "fsdp"), None),
            P(None, ("dp", "fsdp"), None),
            P(None, ("dp", "fsdp")),
            P(None, ("dp", "fsdp"), None),
            P(None, ("dp", "fsdp"), None),
            P(None, ("dp", "fsdp"), None),
            P(None, ("dp", "fsdp"), None),
            P(None, ("dp", "fsdp")),
            P(None, ("dp", "fsdp"), None),
            P(None, ("dp", "fsdp"), None),
            P(None, ("dp", "fsdp"), None),
            P(None, ("dp", "fsdp"), None),
            P(None, ("dp", "fsdp")),
            P(),
        ),
        check_vma=False,
    )
```

```python
import jax
import numpy as np
import jax.numpy as jnp
from jax import lax
from jax.experimental import pallas as pl
from jax.experimental.pallas import tpu as pltpu
from jax.sharding import PartitionSpec as P

HEADS = 8
NSTATE = 32
KERNEL = 15
STEP_NUMBER = 5


NORM_EPS = 1e-05
BETA_FIRST = 0.5
BETA_SECOND = 0.6
ADAM_EPS = 1e-08
RATE_MATRIX = 0.02
RATE_VECTOR = 0.2
WEIGHT_DECAY = 0.01


def adamw(master, first, second, gradient, rate, decay):
    first_new = BETA_FIRST * first + (1.0 - BETA_FIRST) * gradient
    second_new = BETA_SECOND * second + (1.0 - BETA_SECOND) * gradient * gradient
    first_hat = first_new / (1.0 - BETA_FIRST**STEP_NUMBER)
    second_hat = second_new / (1.0 - BETA_SECOND**STEP_NUMBER)
    updated = master - rate * (first_hat / (jnp.sqrt(second_hat) + ADAM_EPS) + decay * master)
    return (updated, first_new, second_new, updated.astype(jnp.bfloat16))


def piece_tables():
    tables = []
    for me in range(32):
        core = (me >> 3) & 1
        pieces = []
        for side in (0, 1):
            base = me ^ (8 * side)
            across = ((16, 1), (1, 16))[core ^ side]
            for spot in range(16):
                rel = (across[0] if spot & 8 else 0) | (across[1] if spot & 4 else 0)
                rel |= (2 if spot & 2 else 0) | (4 if spot & 1 else 0)
                pieces.append(base ^ rel)
        tables.append(pieces)
    return np.array(tables, np.int32)


TABLES = piece_tables()
SPOTS = np.argsort(TABLES, axis=1).astype(np.int32)
AXES = ("dp", "fsdp")
CORE, Z_HIGH, Z_LOW = 8, 4, 2
STAGES = (Z_HIGH, Z_LOW, (1, 16), (16, 1))


def swap(values, mask):
    masks = mask if isinstance(mask, tuple) else (mask, mask)
    return lax.ppermute(values, AXES, [(i, i ^ masks[(i >> 3) & 1]) for i in range(32)])


def after(values, *earlier):
    return lax.optimization_barrier((values, *earlier))[0] if earlier else values


def add_low(left, right):
    return (left.astype(jnp.float32) + right.astype(jnp.float32)).astype(jnp.bfloat16)


def pack_rows(sums):
    low = lax.reduce_precision(sums, 8, 7)
    rest = jnp.pad(sums[30:31] - low[30:31], ((31, 0), (0, 0)))
    return (low + rest).astype(jnp.bfloat16).reshape(2, 16, 512)


def unpack_rows(message):
    rows = message.astype(jnp.float32).reshape(32, 512)
    return jnp.concatenate([rows[:30], rows[30:31] + rows[31:32], jnp.zeros((1, 512), jnp.float32)])


def cut_columns(matrix):
    rows, columns = matrix.shape
    return matrix.reshape(rows, columns // 512, 512).transpose(1, 0, 2).reshape(-1, 512)


def pieces_of(matrix):
    by_piece = matrix.reshape(32, matrix.shape[0] // 32, -1, 512)
    return jnp.moveaxis(by_piece, 2, 1).reshape(32, -1, 512)


def join_columns(pieces, columns):
    lead = pieces.shape[:-2]
    rows = pieces.shape[-2] // columns
    moved = jnp.moveaxis(pieces.reshape(*lead, columns, rows, 512), -3, -2)
    return moved.reshape(*lead, rows, columns * 512)


def sync(*arrays):
    return lax.optimization_barrier(arrays)


def join(*arrays):
    return jnp.concatenate(arrays)


def shard_of(parts):
    return join(*[cut_columns(part.astype(jnp.bfloat16)).reshape(-1, 16, 512) for part in parts])


def gather_all(first, middle, last, vectors):
    far, near, late, later = STAGES
    own, mid, end = shard_of(first), shard_of(middle), shard_of(last)
    size = own.shape[0]
    vectors = vectors + swap(vectors, CORE)
    got0, got1 = swap(own, far), swap(own, near)
    vectors = vectors + swap(after(vectors, own), far)
    own, mid, end, got0, got1, vectors = sync(own, mid, end, got0, got1, vectors)

    got1_late = swap(join(got0, vectors), near)
    two = join(own, got0)
    got2 = swap(two, late)
    mid_got = swap(mid, far)
    got1_late, two, got2, mid_got, vectors = sync(got1_late, two, got2, mid_got, vectors)

    vectors = vectors + got1_late[size:]
    other_two = join(got1, got1_late[:size], vectors)
    got2_late = swap(other_two, late)
    four = join(two, other_two[:-2])
    got3 = swap(four, later)
    mid = join(mid, mid_got)
    mid_got, end_got = swap(mid, near), swap(after(end, mid_got), far)
    got2_late, got3, mid_got, end_got, other_two = sync(got2_late, got3, mid_got, end_got, other_two)

    vectors = vectors + got2_late[2 * size :]
    other_four = join(got2, got2_late[: 2 * size], vectors)
    got3_late = swap(other_four, later)
    mid = join(mid, mid_got)
    end = join(end, end_got)
    mid_got, end_got = swap(mid, late), swap(end, near)
    far_pieces = [swap(four, CORE), swap(other_four, CORE), swap(got3, CORE)]
    got3_late, mid_got, end_got, vectors = sync(got3_late, mid_got, end_got, vectors)

    vectors = vectors + got3_late[4 * size :]
    far_pieces.append(swap(got3_late, CORE))
    mid = join(mid, mid_got)
    mid_got, mid_far = swap(mid, later), swap(mid, CORE)
    end = join(end, end_got)
    end_got = swap(end, late)
    return (four, other_four, got3, got3_late, *far_pieces), vectors, (mid, mid_got, mid_far), (end, end_got)


def gather_whole(parts):
    gathered = [lax.all_gather(part.astype(jnp.bfloat16), AXES, axis=0, tiled=True) for part in parts]
    pieces = join(*[pieces_of(matrix) for matrix in gathered]) if len(parts) == 1 else jnp.concatenate(
        [pieces_of(matrix) for matrix in gathered], axis=1
    )
    return tuple(pieces.reshape(4, -1, 16, 512))


class Reduce:
    def __init__(self, kept, sent, columns, paired, rows=None, pack=None, unpack=None):
        self.groups = kept.shape[1]
        self.kept, self.sent = kept.reshape(-1, 16, 512), sent.reshape(-1, 16, 512)
        self.columns, self.rows, self.pack, self.unpack, self.paired = columns, rows, pack, unpack, paired
        self.stage = 0

    def start(self, *earlier):
        if not self.paired:
            return
        if self.stage == 0:
            self.got = swap(self.sent, CORE)
            if self.rows is not None:
                self.more = swap(self.pack(self.rows), CORE)
        else:
            count = self.kept.shape[0] // 2
            self.got = after(self.got, *earlier)
            sent = add_low(self.kept[count:], self.got[count : 2 * count])
            if self.rows is not None:
                more = after(self.more, *earlier) if self.stage == 1 else self.got[2 * count :]
                self.rows = self.rows + self.unpack(more)
                sent = jnp.concatenate([sent, self.pack(self.rows)])
            kept, got = after(self.kept, sent), after(self.got, sent)
            self.got = swap(sent, STAGES[4 - self.stage])
            self.kept = add_low(kept[:count], got[:count])
            self.sent = sent
        self.stage += 1

    def arrived(self):
        return (self.got,) if self.paired else ()

    def finish(self, *earlier):
        if not self.paired:
            return self.scatter()
        self.got = after(self.got, *earlier)
        total = self.kept.astype(jnp.float32) + self.got[: self.groups].astype(jnp.float32)
        rows = None if self.rows is None else self.rows + self.unpack(self.got[self.groups :])
        return total.reshape(-1, 512), rows

    def scatter(self):
        pieces = jnp.concatenate([self.kept, self.sent]).reshape(32, -1, 512)
        sums, start = [], 0
        for count, tall in self.columns:
            rows = 16 * count * tall
            matrix = join_columns(pieces[:, start : start + rows], count).reshape(512 * tall, -1)
            matrix = lax.psum_scatter(matrix.astype(jnp.float32), AXES, scatter_dimension=0, tiled=True)
            sums.append(cut_columns(matrix))
            start += rows
        return jnp.concatenate(sums), None if self.rows is None else lax.psum(self.rows, AXES)


def pack_pair(sums):
    low = lax.reduce_precision(sums[:2], 8, 7)
    parts = [low, sums[:2] - low, jnp.zeros((12, 512), jnp.float32)]
    return jnp.concatenate(parts).astype(jnp.bfloat16)[None]


def unpack_pair(message):
    rows = message[0].astype(jnp.float32)
    return jnp.concatenate([rows[0:2] + rows[2:4], jnp.zeros((6, 512), jnp.float32)])


TILE = 64
F32, LOW = jnp.float32, jnp.bfloat16
NN, NT, TN = ((1,), (0,)), ((1,), (1,)), ((0,), (0,))
VMEM_BYTES = 32 * 1024 * 1024


def mm(left, right, dims=NN):
    return lax.dot_general(left, right, (dims, ((), ())), preferred_element_type=F32)


def tiles(rows=512, step=TILE):
    return [pl.ds(start, step) for start in range(0, rows, step)]


def sigmoid(values):
    return 0.5 * jnp.tanh(0.5 * values) + 0.5


def standardize(values):
    centered = values - jnp.mean(values, axis=-1, keepdims=True)
    variance = jnp.mean(centered * centered, axis=-1, keepdims=True)
    spread = lax.rsqrt(variance + NORM_EPS)
    return centered * spread, spread


def standardize_back(grad, unit, spread):
    mean_grad = jnp.mean(grad, axis=-1, keepdims=True)
    mean_both = jnp.mean(grad * unit, axis=-1, keepdims=True)
    return spread * (grad - mean_grad - unit * mean_both)


def row(values):
    return jnp.sum(values, axis=0, keepdims=True)


def square(pieces):
    return pieces.reshape(512, 512)


def fetch(table, sources, groups, jobs, sem):
    each_has = 32 // len(sources)

    def each(spot, what):
        for side, source in enumerate(sources):
            for first, count, target in jobs:
                copy = pltpu.make_async_copy(
                    source.at[pl.ds(groups * spot + first, count)], target(table[each_has * side + spot]), sem
                )
                getattr(copy, what)()

    lax.fori_loop(0, each_has, lambda spot, _: (each(spot, "start"), 0)[1], 0)
    return lambda: lax.fori_loop(0, each_has, lambda spot, _: (each(spot, "wait"), 0)[1], 0)


def fetch_ffn(table, sources, w_in, w_out, sem):
    return fetch(
        table,
        sources,
        8,
        [(0, 4, lambda d: w_in.at[:, d]), (4, 4, lambda d: w_out.at[pl.ds(4 * d, 4)])],
        sem,
    )


def fetch_mix(table, sources, first, w_in, w_out, sem):
    return fetch(
        table,
        sources,
        6,
        [(first, 2, lambda d: w_in.at[:, d]), (first + 2, 1, lambda d: w_out.at[pl.ds(d, 1)])],
        sem,
    )


def weight_copies(w_in, w_out, in_hbm, out_hbm, sems, load=False):
    pairs = [(w_in, in_hbm), (w_out, out_hbm)]
    return [
        pltpu.make_async_copy(*(pair[::-1] if load else pair), sems.at[place])
        for place, pair in enumerate(pairs)
    ]


def start_all(copies):
    for copy in copies:
        copy.start()


def wait_all(copies):
    for copy in copies:
        copy.wait()


def fill_normed(h_ref, vec_ref, index, normed):
    gain = vec_ref[pl.ds(2 * index, 1)].astype(F32)
    shift = vec_ref[pl.ds(2 * index + 1, 1)].astype(F32)
    for part in tiles():
        unit, _ = standardize(h_ref[part].astype(F32))
        normed[part] = (unit * gain + shift).astype(LOW)


def order_rows(table, natural, ordered):
    def each(spot, _):
        ordered[spot] = natural[table[spot]]
        return 0

    lax.fori_loop(0, 32, each, 0)


def fill_transposed(source, natural):
    for part in tiles(step=128):
        turned = source[part].astype(F32).T.astype(LOW)
        natural[:, :, part] = turned.reshape(32, 16, 128)


def norm_back(h_ref, vec_ref, index, grad_normed, grad_in, grad_out):
    gain = vec_ref[pl.ds(2 * index, 1)].astype(F32)
    grad_gain, grad_shift = jnp.zeros((1, 512), F32), jnp.zeros((1, 512), F32)
    for part in tiles():
        unit, spread = standardize(h_ref[part].astype(F32))
        grad = grad_normed[part]
        grad_gain = grad_gain + row(grad * unit)
        grad_shift = grad_shift + row(grad)
        grad_out[part] = grad_in[part] + standardize_back(grad * gain, unit, spread)
    return grad_gain, grad_shift


def valid_rows(length, part):
    places = part.start + lax.broadcasted_iota(jnp.int32, (part.size, 1), 0)
    return (places < length).astype(F32)


def valid_lanes(length):
    return (lax.broadcasted_iota(jnp.int32, (1, 512), 1) < length).astype(F32)


def ffn_forward(length, h_ref, normed, w_in, w_out, pre, act, out, new_h, save):
    for j in range(4):
        pre_j, act_j = pre.at[j], act(j)
        pre_j[...] = mm(normed[...], square(w_in[j]))
        for part in tiles():
            values = pre_j[part]
            act_j[part] = (values * sigmoid(values)).astype(LOW)
        save(j)
        more = mm(act_j[...], square(w_out[pl.ds(32 * j, 32)]))
        out[...] = more if j == 0 else out[...] + more
    total = jnp.zeros((1, 512), F32)
    for part in tiles():
        half = 0.5 * out[part]
        new_h[part] = h_ref[part].astype(F32) + half
        total = total + row(valid_rows(length, part) * half * half)
    return total


def place_out_grads(spots, j, first, grads, act, grad_low):
    products = mm(act, grad_low, TN).astype(LOW).reshape(8, 4, 16, 512)
    for f in range(8):
        grads[spots[8 * j + f], pl.ds(first, 4)] = products[f]


def ffn_backward(spots, w_in, w_out, pre, grad_low, turned, act, grad_pre, grad_normed, grads):
    for j in range(4):
        pre_j = pre(j)
        grad_act = mm(grad_low[...], square(w_out[pl.ds(32 * j, 32)]), NT)
        for part in tiles():
            values = pre_j[part]
            gate = sigmoid(values)
            lifted = values * gate
            if act is not None:
                act[part] = lifted.astype(LOW)
            slope = gate + lifted * (1.0 - gate)
            grad_pre[part] = (grad_act[part.start : part.start + part.size] * slope).astype(LOW)
        more = mm(grad_pre[...], square(w_in[j]), NT)
        grad_normed[...] = more if j == 0 else grad_normed[...] + more
        grads[:, j] = mm(square(turned[...]), grad_pre[...]).astype(LOW).reshape(32, 16, 512)
        if act is not None:
            place_out_grads(spots, j, 4, grads, act[...], grad_low[...])


def first_kernel(table, length, h_ref, vec_ref, *refs):
    *pieces, h1_ref, pre_hbm, act_hbm, stat_ref, in_hbm, out_hbm = refs[:-10]
    w_in, w_out, normed, act, out, pre, sem, pre_sem, act_sem, w_sem = refs[-10:]
    finish = fetch_ffn(table, pieces, w_in, w_out, sem)
    fill_normed(h_ref, vec_ref, 0, normed)
    finish()
    weights = weight_copies(w_in, w_out, in_hbm, out_hbm, w_sem)
    start_all(weights)

    copies = [
        (
            pltpu.make_async_copy(pre.at[j], pre_hbm.at[j], pre_sem.at[j]),
            pltpu.make_async_copy(act.at[j], act_hbm.at[j], act_sem.at[j]),
        )
        for j in range(4)
    ]

    def save(j):
        start_all(copies[j])

    stat_ref[...] = ffn_forward(
        length[0], h_ref, normed, w_in, w_out, pre, lambda j: act.at[j], out, h1_ref, save
    )
    for j in range(4):
        wait_all(copies[j])
    wait_all(weights)


def last_kernel(
    table, spots, length, h_ref, vec_ref, cot_ref, held, got, held_far, got_far,
    top_ref, grad_ref, rows_ref, kept_hbm, sent_hbm,
    w_in, w_out, normed, act, out, pre, low, natural, turned, grads, sem, out_sem
):
    finish = fetch_ffn(table, (held, got, held_far, got_far), w_in, w_out, sem)
    fill_normed(h_ref, vec_ref, 4, normed)
    fill_transposed(normed, natural)
    order_rows(table, natural, turned)
    finish()
    stat4 = ffn_forward(length[0], h_ref, normed, w_in, w_out, pre, lambda j: act, out, grad_ref, lambda j: None)
    gain, shift = vec_ref[pl.ds(10, 1)].astype(F32), vec_ref[pl.ds(11, 1)].astype(F32)
    grad_gain, grad_shift = jnp.zeros((1, 512), F32), jnp.zeros((1, 512), F32)
    stat5 = jnp.zeros((1, 512), F32)
    for part in tiles():
        values = grad_ref[part]
        stat5 = stat5 + row(valid_rows(length[0], part) * values * values)
        unit, spread = standardize(values)
        top_ref[part] = unit * gain + shift
        grad = cot_ref[part].astype(F32)
        grad_gain = grad_gain + row(grad * unit)
        grad_shift = grad_shift + row(grad)
        back = standardize_back(grad * gain, unit, spread)
        grad_ref[part] = back
        low[part] = (0.5 * back).astype(LOW)
    ffn_backward(spots, w_in, w_out, lambda j: pre.at[j], low, turned, act, normed, out, grads)
    finish = hand_out(grads, kept_hbm, sent_hbm, out_sem)
    gain4, shift4 = norm_back(h_ref, vec_ref, 4, out, grad_ref, grad_ref)
    rows_ref[...] = jnp.concatenate(
        [gain4, shift4, grad_gain, grad_shift, stat4, stat5, jnp.zeros((2, 512), F32)]
    )
    finish()


def back_out_kernel(spots, grad_in, act, kept_hbm, sent_hbm, low, grads, out_sem):
    for part in tiles():
        low[part] = (0.5 * grad_in[part]).astype(LOW)
    for j in range(4):
        place_out_grads(spots, j, 0, grads, act[j], low[...])
    hand_out(grads, kept_hbm, sent_hbm, out_sem)()


def hand_out(grads, kept, sent, sem):
    copies = [
        pltpu.make_async_copy(grads.at[pl.ds(16, 16)], sent, sem.at[1]),
        pltpu.make_async_copy(grads.at[pl.ds(0, 16)], kept, sem.at[0]),
    ]
    for copy in copies:
        copy.start()

    def finish():
        for copy in copies:
            copy.wait()

    return finish


def back_first_kernel(table, spots, h_ref, vec_ref, grad_in, *refs):
    in_hbm, out_hbm, pre_hbm, grad_ref, rows_ref, kept_hbm, sent_hbm = refs[:-12]
    w_in, w_out, normed, out, pre, low, natural, turned, grads, w_sem, pre_sem, out_sem = refs[-12:]
    weights = weight_copies(w_in, w_out, in_hbm, out_hbm, w_sem, load=True)
    start_all(weights)
    copies = [pltpu.make_async_copy(pre_hbm.at[j], pre.at[j], pre_sem.at[j]) for j in range(4)]
    for copy in copies:
        copy.start()
    fill_normed(h_ref, vec_ref, 0, normed)
    fill_transposed(normed, natural)
    order_rows(table, natural, turned)
    for part in tiles():
        low[part] = (0.5 * grad_in[part]).astype(LOW)
    wait_all(weights)

    def pre_of(j):
        copies[j].wait()
        return pre.at[j]

    ffn_backward(spots, w_in, w_out, pre_of, low, turned, None, normed, out, grads)
    finish = hand_out(grads, kept_hbm, sent_hbm, out_sem)
    gain0, shift0 = norm_back(h_ref, vec_ref, 0, out, grad_in, grad_ref)
    rows_ref[...] = jnp.concatenate([gain0, shift0, jnp.zeros((6, 512), F32)])
    finish()


def vector_columns(vec_ref, pad):
    pad[...] = jnp.zeros((128, 512), F32)
    pad[pl.ds(0, 32)] = vec_ref[...].astype(F32)
    return pad[...].T


def ssm_decays(columns):
    rates = jnp.exp(columns[0:256, 13:14])
    lags = lax.broadcasted_iota(jnp.int32, (1, 512), 1).astype(F32)
    return jnp.exp(-rates * lags), rates, columns[256:512, 13:14]


def head_matrix(kernels, head):
    line = jnp.concatenate([kernels[head : head + 1], jnp.zeros((1, 128), F32)], axis=1)
    skewed = pltpu.roll(jnp.broadcast_to(line, (128, 640)), 0, 1, stride=1, stride_axis=0)
    return skewed[:, :512].astype(LOW)


def blocks_of(rows):
    return jnp.concatenate([rows[:, 128 * b : 128 * (b + 1)] for b in range(4)], axis=0)


def ssm_kernel(
    table, length, h_ref, vec_ref, held, got, held_far, got_far, h2_ref, saved_hbm, stat_ref, in_hbm, out_hbm,
    w_in, w_out, normed, act, saved, pad, sem, save_sem, w_sem
):
    finish = fetch_mix(table, (held, got, held_far, got_far), 0, w_in, w_out, sem)
    fill_normed(h_ref, vec_ref, 1, normed)
    columns = vector_columns(vec_ref, pad)
    decays, _, coefs = ssm_decays(columns)
    kernels = jnp.sum((coefs * decays).reshape(8, 32, 512), axis=1)
    finish()
    weights = weight_copies(w_in, w_out, in_hbm, out_hbm, w_sem)
    start_all(weights)
    mask = valid_lanes(length[0])
    signal, gate, mixed = saved.at[0], saved.at[1], saved.at[2]
    signal[...] = mm(square(w_in[0]), normed[...], ((0,), (1,))) * mask
    gate[...] = mm(square(w_in[1]), normed[...], ((0,), (1,)))
    copies = [pltpu.make_async_copy(saved.at[k], saved_hbm.at[k], save_sem.at[k]) for k in range(3)]
    copies[0].start()
    copies[1].start()
    for head in range(8):
        part = pl.ds(64 * head, 64)
        rows = signal[part]
        spread = mm(blocks_of(rows).astype(LOW), head_matrix(kernels, head))
        skip = columns[64 * head : 64 * head + 64, 12:13]
        for a in range(4):
            lanes = pl.ds(128 * a, 128)
            total = skip * rows[:, 128 * a : 128 * a + 128]
            for b in range(a + 1):
                total = total + spread[64 * b : 64 * b + 64, 128 * (a - b) : 128 * (a - b) + 128]
            mixed[part, lanes] = total
            gates = gate[part, lanes]
            act[part, lanes] = (total * gates * sigmoid(gates)).astype(LOW)
    copies[2].start()
    out = mm(act[...], square(w_out[...]), TN)
    total = jnp.zeros((1, 512), F32)
    for part in tiles():
        values = out[part.start : part.start + part.size]
        h2_ref[part] = h_ref[part] + values
        total = total + row(valid_rows(length[0], part) * values * values)
    stat_ref[...] = total
    wait_all(copies)
    wait_all(weights)


def ssm_back_kernel(
    table, length, h_ref, vec_ref, grad_in, in_hbm, out_hbm, saved_hbm, stat1, stat2, rows2, rows3,
    kept_before, sent_before, grad_ref, rows_ref, kept_hbm, sent_hbm,
    w_in, w_out, normed, saved, low, natural, turned, act, act_turned, grad_pre, out, grads, pad, kernel_grads,
    w_sem, save_sem, out_sem
):
    weights = weight_copies(w_in, w_out, in_hbm, out_hbm, w_sem, load=True)
    start_all(weights)
    copies = [pltpu.make_async_copy(saved_hbm.at[k], saved.at[k], save_sem.at[k]) for k in range(3)]
    for copy in copies:
        copy.start()
    fill_normed(h_ref, vec_ref, 1, normed)
    fill_transposed(normed, natural)
    order_rows(table, natural, turned)
    for part in tiles():
        low[part] = grad_in[part].astype(LOW)
    columns = vector_columns(vec_ref, pad)
    decays, rates, coefs = ssm_decays(columns)
    kernels = jnp.sum((coefs * decays).reshape(8, 32, 512), axis=1)
    mask = valid_lanes(length[0])
    wait_all(weights)
    for copy in copies:
        copy.wait()
    signal, gate, mixed = saved.at[0], saved.at[1], saved.at[2]
    out[...] = mm(square(w_out[...]), low[...], NT)
    flipped = lax.broadcasted_iota(jnp.int32, (128, 128), 0) + lax.broadcasted_iota(jnp.int32, (128, 128), 1)
    flip = (flipped == 127).astype(F32).astype(LOW)
    for head in range(8):
        part = pl.ds(64 * head, 64)
        rows, gates, mixes, grad_act = signal[part], gate[part], mixed[part], out[part]
        gating = sigmoid(gates)
        lifted = gates * gating
        act[pl.ds(4 * head, 4)] = (mixes * lifted).astype(LOW).reshape(4, 16, 512)
        grad_mixed = grad_act * lifted
        grad_pre[1, part] = (grad_act * mixes * (gating + lifted * (1.0 - gating))).astype(LOW)
        grad_low = grad_mixed.astype(LOW)
        shifted = jnp.concatenate(
            [grad_low]
            + [
                jnp.concatenate([grad_low[:, 128 * b :], jnp.zeros((64, 128 * b), LOW)], axis=1)
                for b in (1, 2, 3)
            ],
            axis=0,
        )
        back = mm(shifted, head_matrix(kernels, head), NT)
        mirrored = mm(blocks_of(rows).astype(LOW), flip).astype(LOW)
        lag_sums = mm(mirrored, shifted, TN)
        lag_sums = jnp.concatenate([lag_sums, jnp.zeros((128, 128), F32)], axis=1)
        lag_sums = row(pltpu.roll(lag_sums, 0, 1, stride=1, stride_axis=0))
        kernel_grads[pl.ds(head, 1)] = pltpu.roll(lag_sums, 640 - 127, 1)[:, :512]
        skip = columns[64 * head : 64 * head + 64, 12:13]
        pad_lane = jnp.sum(grad_mixed * rows, axis=1, keepdims=True)
        natural_grad = jnp.concatenate([back[64 * b : 64 * b + 64] for b in range(4)], axis=1)
        grad_pre[0, part] = ((natural_grad + skip * grad_mixed) * mask).astype(LOW)
        normed_f = jnp.broadcast_to(pad_lane, (64, 128))
        saved[0, part, pl.ds(0, 128)] = normed_f
    order_rows(table, act, act_turned)
    grads[:, 2] = mm(square(act_turned[...]), low[...]).astype(LOW).reshape(32, 16, 512)
    for q in range(2):
        more = mm(grad_pre[q], square(w_in[q]), ((0,), (1,)))
        out[...] = more if q == 0 else out[...] + more
        grads[:, q] = mm(square(turned[...]), grad_pre[q], NT).astype(LOW).reshape(32, 16, 512)
    finish = hand_out(grads, kept_hbm.at[:, pl.ds(0, 3)], sent_hbm.at[:, pl.ds(0, 3)], out_sem)
    gain1, shift1 = norm_back(h_ref, vec_ref, 1, out, grad_in, grad_ref)
    lag_grads = jnp.broadcast_to(kernel_grads[...].reshape(8, 1, 512), (8, 32, 512)).reshape(256, 512)
    lags = lax.broadcasted_iota(jnp.int32, (1, 512), 1).astype(F32)
    weighed = lag_grads * decays
    coef_grads = jnp.sum(weighed, axis=1, keepdims=True)
    rate_grads = -rates * coefs * jnp.sum(weighed * lags, axis=1, keepdims=True)
    lanes = lax.broadcasted_iota(jnp.int32, (1, 128), 1)
    ssm_column = jnp.concatenate([rate_grads, coef_grads], axis=0)
    both = jnp.where(lanes == 0, saved[0, :, pl.ds(0, 128)], 0.0) + jnp.where(lanes == 1, ssm_column, 0.0)
    turned_rows = both.T
    lanes = lax.broadcasted_iota(jnp.int32, (1, 512), 1)
    stats = jnp.where(lanes == 5, length[0].astype(F32), 0.0)
    for place, sums in enumerate([stat1[...], stat2[...], rows2[20:21], rows3[4:5], rows3[5:6]]):
        stats = stats + jnp.where(lanes == place, jnp.sum(sums, axis=1, keepdims=True), 0.0)
    nothing = jnp.zeros((2, 512), F32)
    rows_ref[...] = jnp.concatenate(
        [nothing, gain1, shift1, rows2[0:4], rows3[0:4], turned_rows[0:2], rows2[4:20], stats, nothing[0:1]]
    )
    finish()


PAD = 16


def conv_kernel(
    table, length, h_ref, vec_ref, held, got, held_far, got_far, h3_ref, saved_hbm, stat_ref, in_hbm, out_hbm,
    w_in, w_out, normed, act, saved, padded, sem, save_sem, w_sem
):
    finish = fetch_mix(table, (held, got, held_far, got_far), 3, w_in, w_out, sem)
    fill_normed(h_ref, vec_ref, 2, normed)
    finish()
    weights = weight_copies(w_in, w_out, in_hbm, out_hbm, w_sem)
    start_all(weights)
    copies = [pltpu.make_async_copy(saved.at[k], saved_hbm.at[k], save_sem.at[k]) for k in range(3)]
    for q in range(2):
        saved[q] = mm(normed[...], square(w_in[q]))
        copies[q].start()
    for c in range(4):
        padded[c, pl.ds(0, PAD)] = jnp.zeros((PAD, 128), F32)
        padded[c, pl.ds(PAD + 512, PAD)] = jnp.zeros((PAD, 128), F32)
        lanes = pl.ds(128 * c, 128)
        for part in tiles():
            glu = saved[0, part, lanes] * sigmoid(saved[1, part, lanes]) * valid_rows(length[0], part)
            padded[c, pl.ds(PAD + part.start, part.size)] = glu
        taps = [vec_ref[pl.ds(14 + j, 1), lanes].astype(F32) for j in range(KERNEL + 1)]
        for part in tiles():
            total = jnp.broadcast_to(taps[KERNEL], (part.size, 128))
            for j in range(KERNEL):
                total = total + padded[c, pl.ds(PAD + part.start + j - 7, part.size)] * taps[j]
            saved[2, part, lanes] = total
    copies[2].start()
    gain, shift = vec_ref[pl.ds(6, 1)].astype(F32), vec_ref[pl.ds(7, 1)].astype(F32)
    for part in tiles():
        unit, _ = standardize(saved[2, part])
        values = unit * gain + shift
        act[part] = (values * sigmoid(values)).astype(LOW)
    out = mm(act[...], square(w_out[...]))
    total = jnp.zeros((1, 512), F32)
    for part in tiles():
        values = out[part.start : part.start + part.size]
        h3_ref[part] = h_ref[part] + values
        total = total + row(valid_rows(length[0], part) * values * values)
    stat_ref[...] = total
    wait_all(copies)
    wait_all(weights)


def conv_back_kernel(
    table, length, h_ref, vec_ref, grad_in, in_hbm, out_hbm, saved_hbm, stat_in,
    grad_ref, rows_ref, kept_hbm, sent_hbm,
    w_in, w_out, normed, saved, low, natural, turned, act, act_turned, grad_pre, out, grads, padded, padded_grad,
    w_sem, save_sem, out_sem
):
    weights = weight_copies(w_in, w_out, in_hbm, out_hbm, w_sem, load=True)
    start_all(weights)
    copies = [pltpu.make_async_copy(saved_hbm.at[k], saved.at[k], save_sem.at[k]) for k in range(3)]
    for copy in copies:
        copy.start()
    fill_normed(h_ref, vec_ref, 2, normed)
    fill_transposed(normed, natural)
    order_rows(table, natural, turned)
    for part in tiles():
        low[part] = grad_in[part].astype(LOW)
    wait_all(weights)
    for copy in copies:
        copy.wait()
    out[...] = mm(low[...], square(w_out[...]), NT)
    gain, shift = vec_ref[pl.ds(6, 1)].astype(F32), vec_ref[pl.ds(7, 1)].astype(F32)
    gain3, shift3, bias = (jnp.zeros((1, 512), F32) for _ in range(3))
    for part in tiles():
        unit, spread = standardize(saved[2, part])
        values = unit * gain + shift
        gating = sigmoid(values)
        lifted = values * gating
        normed[part] = lifted.astype(LOW)
        grad = out[part] * (gating + lifted * (1.0 - gating))
        gain3 = gain3 + row(grad * unit)
        shift3 = shift3 + row(grad)
        back = standardize_back(grad * gain, unit, spread)
        bias = bias + row(back)
        for c in range(4):
            padded_grad[c, pl.ds(PAD + part.start, part.size)] = back[:, 128 * c : 128 * c + 128]
    fill_transposed(normed, act)
    order_rows(table, act, act_turned)
    grads[:, 2] = mm(square(act_turned[...]), low[...]).astype(LOW).reshape(32, 16, 512)
    tap_rows = []
    for c in range(4):
        lanes = pl.ds(128 * c, 128)
        for ref in (padded, padded_grad):
            ref[c, pl.ds(0, PAD)] = jnp.zeros((PAD, 128), F32)
            ref[c, pl.ds(PAD + 512, PAD)] = jnp.zeros((PAD, 128), F32)
        for part in tiles():
            glu = saved[0, part, lanes] * sigmoid(saved[1, part, lanes]) * valid_rows(length[0], part)
            padded[c, pl.ds(PAD + part.start, part.size)] = glu
        taps = [vec_ref[pl.ds(14 + j, 1), lanes].astype(F32) for j in range(KERNEL)]
        sums = [jnp.zeros((8, 128), F32) for _ in range(KERNEL)]
        for part in tiles():
            total = jnp.zeros((part.size, 128), F32)
            grad = padded_grad[c, pl.ds(PAD + part.start, part.size)]
            for j in range(KERNEL):
                total = total + padded_grad[c, pl.ds(PAD + part.start + 7 - j, part.size)] * taps[j]
                seen = padded[c, pl.ds(PAD + part.start + j - 7, part.size)]
                sums[j] = sums[j] + jnp.sum((grad * seen).reshape(part.size // 8, 8, 128), axis=0)
            total = total * valid_rows(length[0], part)
            gating = sigmoid(saved[1, part, lanes])
            first = total * gating
            grad_pre[0, part, lanes] = first.astype(LOW)
            grad_pre[1, part, lanes] = (first * saved[0, part, lanes] * (1.0 - gating)).astype(LOW)
        tap_rows.append(jnp.concatenate([row(values) for values in sums], axis=0))
    for q in range(2):
        more = mm(grad_pre[q], square(w_in[q]), NT)
        out[...] = more if q == 0 else out[...] + more
        grads[:, q] = mm(square(turned[...]), grad_pre[q]).astype(LOW).reshape(32, 16, 512)
    finish = hand_out(grads, kept_hbm.at[:, pl.ds(3, 3)], sent_hbm.at[:, pl.ds(3, 3)], out_sem)
    gain2, shift2 = norm_back(h_ref, vec_ref, 2, out, grad_in, grad_ref)
    rows_ref[...] = jnp.concatenate(
        [gain2, shift2, gain3, shift3, jnp.concatenate(tap_rows, axis=1), bias, stat_in[...], jnp.zeros((3, 512), F32)]
    )
    finish()


def call(kernel, scalars, arrays, outs, scratch, flops, aliases=None):
    in_place, in_vmem = pl.BlockSpec(memory_space=pl.ANY), pl.BlockSpec(memory_space=pltpu.VMEM)
    return pl.pallas_call(
        kernel,
        out_shape=[jax.ShapeDtypeStruct(shape, dtype) for shape, dtype, _ in outs],
        in_specs=[pl.BlockSpec(memory_space=pltpu.SMEM)] * len(scalars)
        + [in_place if stays else in_vmem for _, stays in arrays],
        out_specs=[in_place if stays else in_vmem for _, _, stays in outs],
        scratch_shapes=scratch,
        input_output_aliases=aliases or {},
        compiler_params=pltpu.CompilerParams(vmem_limit_bytes=VMEM_BYTES),
        cost_estimate=pl.CostEstimate(flops=40 * flops, bytes_accessed=64 << 20, transcendentals=1 << 24),
    )(*scalars, *[array for array, _ in arrays])


SQUARE, PIECES = (512, 512), (32, 16, 512)
DMA = pltpu.SemaphoreType.DMA
IN_FFN, OUT_FFN, IN_MIX = (4, 32, 16, 512), (128, 16, 512), (2, 32, 16, 512)
SMALL, LARGE = 512 * 512 * 512 * 2, 512 * 512 * 2048 * 2


def low_scratch(*shapes):
    return [pltpu.VMEM(shape, LOW) for shape in shapes]


def full_scratch(*shapes):
    return [pltpu.VMEM(shape, F32) for shape in shapes]


def here(*arrays):
    return [(array, False) for array in arrays]


def there(*arrays):
    return [(array, True) for array in arrays]


def run_first(table, length, h, vectors, pieces):
    return call(
        first_kernel,
        [table, length],
        here(h, vectors) + there(*pieces),
        [(SQUARE, F32, False), ((4, 512, 512), F32, True), ((4, 512, 512), LOW, True), ((1, 512), F32, False)]
        + [(IN_FFN, LOW, True), (OUT_FFN, LOW, True)],
        low_scratch(IN_FFN, OUT_FFN, SQUARE, (4, 512, 512))
        + full_scratch(SQUARE, (4, 512, 512))
        + [DMA, DMA((4,)), DMA((4,)), DMA((2,))],
        2 * LARGE,
    )


def grads_of(groups):
    return ((16, groups, 16, 512), LOW, True)


def run_last(table, spots, length, h, vectors, cotangent, pieces):
    return call(
        last_kernel,
        [table, spots, length],
        here(h, vectors, cotangent) + there(*pieces),
        [(SQUARE, F32, False), (SQUARE, F32, False), ((8, 512), F32, False), grads_of(8), grads_of(8)],
        low_scratch(IN_FFN, OUT_FFN, SQUARE, SQUARE)
        + full_scratch(SQUARE, (4, 512, 512))
        + low_scratch(SQUARE, PIECES, PIECES, (32, 8, 16, 512))
        + [DMA, DMA((2,))],
        6 * LARGE,
    )


def run_back_out(spots, grad, act):
    return call(
        back_out_kernel,
        [spots],
        here(grad, act),
        [grads_of(4), grads_of(4)],
        low_scratch(SQUARE, (32, 4, 16, 512)) + [DMA((2,))],
        LARGE,
    )


def run_back_first(table, spots, h, vectors, grad, pieces, pre):
    return call(
        back_first_kernel,
        [table, spots],
        here(h, vectors, grad) + there(*pieces, pre),
        [(SQUARE, F32, False), ((8, 512), F32, False), grads_of(4), grads_of(4)],
        low_scratch(IN_FFN, OUT_FFN, SQUARE)
        + full_scratch(SQUARE, (4, 512, 512))
        + low_scratch(SQUARE, PIECES, PIECES, (32, 4, 16, 512))
        + [DMA((2,)), DMA((4,)), DMA((2,))],
        3 * LARGE,
    )


def run_mix(kernel, table, length, h, vectors, pieces, last_scratch):
    return call(
        kernel,
        [table, length],
        here(h, vectors) + there(*pieces),
        [(SQUARE, F32, False), ((3, 512, 512), F32, True), ((1, 512), F32, False)]
        + [(IN_MIX, LOW, True), (PIECES, LOW, True)],
        low_scratch(IN_MIX, PIECES, SQUARE, SQUARE)
        + full_scratch((3, 512, 512), last_scratch)
        + [DMA, DMA((3,)), DMA((2,))],
        4 * SMALL,
    )


def run_mix_back(kernel, table, length, h, vectors, grad, pieces, saved, more, before, rows, last_scratch):
    first = 2 + 3 + len(pieces) + 1 + len(more)
    return call(
        kernel,
        [table, length],
        here(h, vectors, grad) + there(*pieces, saved) + here(*more) + there(*before),
        [(SQUARE, F32, False), ((rows, 512), F32, False), grads_of(6), grads_of(6)],
        low_scratch(IN_MIX, PIECES, SQUARE)
        + full_scratch((3, 512, 512))
        + low_scratch(SQUARE, PIECES, PIECES, PIECES, PIECES, (2, 512, 512))
        + full_scratch(SQUARE)
        + low_scratch((32, 3, 16, 512))
        + full_scratch(*last_scratch)
        + [DMA((2,)), DMA((3,)), DMA((2,))],
        8 * SMALL,
        {first: 2, first + 1: 3} if before else {},
    )


def local(
    frames,
    cotangent,
    seq_lengths,
    ffn_in_master,
    ffn_out_master,
    mix_in_master,
    mix_out_master,
    vector_master,
    ffn_in_first,
    ffn_out_first,
    mix_in_first,
    mix_out_first,
    vector_first,
    ffn_in_second,
    ffn_out_second,
    mix_in_second,
    mix_out_second,
    vector_second,
):
    me = lax.axis_index(AXES)
    paired = (lax.axis_size("dp"), lax.axis_size("fsdp")) == (4, 8)
    spots = jnp.asarray(SPOTS)[me] if paired else jnp.arange(32, dtype=jnp.int32)
    table = jnp.asarray(TABLES)[me] if paired else jnp.arange(32, dtype=jnp.int32)
    low = jnp.bfloat16
    width, n = vector_master.shape[1], ffn_in_master.shape[1]
    placed = lax.dynamic_update_slice(
        jnp.zeros((32, 512), low), vector_master.astype(low), (0, width * me)
    ).reshape(2, 16, 512)
    first = [ffn_in_master[0], ffn_out_master[0]]
    middle = [mix_in_master[0], mix_out_master[0], mix_in_master[1], mix_out_master[1]]
    last = [ffn_in_master[1], ffn_out_master[1]]
    h0, length = frames[0], seq_lengths
    if paired:
        first, vectors, (mid, mid_got, mid_far), (end, end_got) = gather_all(first, middle, last, placed)
    else:
        first, middle, last = gather_whole(first), gather_whole(middle), gather_whole(last)
        vectors = lax.psum(placed, AXES)
    vectors = vectors.reshape(32, 512)
    h1, pre0, act0, stat1, *weights0 = run_first(table, length, h0, vectors, first)
    if paired:
        mid_got, end_got, stat1 = sync(mid_got, end_got, stat1)
        end = join(end, end_got)
        end_got, end_far = swap(end, STAGES[3]), swap(end, CORE)
        middle = (mid, mid_got, mid_far, swap(mid_got, CORE))
    h2, saved1, stat2, *weights1 = run_mix(ssm_kernel, table, length, h1, vectors, middle, (128, 512))
    h3, saved2, stat3, *weights2 = run_mix(
        conv_kernel, table, length, h2, vectors, middle, (4, 512 + 2 * PAD, 128)
    )
    if paired:
        end_got, stat3 = sync(end_got, stat3)
        last = (end, end_got, end_far, swap(end_got, CORE))
    activations, grad3, rows3, kept3, sent3 = run_last(
        table, spots, length, h3, vectors, cotangent[0], last
    )
    sum3 = Reduce(kept3, sent3, ((4, 1), (1, 4)), paired)
    sum3.start()
    sum3.start()
    grad3 = after(grad3, sum3.sent)
    grad2, rows2, kept2, sent2 = run_mix_back(
        conv_back_kernel, table, length, h2, vectors, grad3, weights2, saved2, [stat3], [], 24,
        [(4, 512 + 2 * PAD, 128)] * 2,
    )
    sum3.start(rows2)
    grad2 = after(grad2, sum3.sent)
    grad1, rows, kept1, sent1 = run_mix_back(
        ssm_back_kernel, table, length, h1, vectors, grad2, weights1, saved1,
        [stat1, stat2, rows2, rows3], [kept2, sent2], 32, [(128, 512), (8, 512)],
    )
    sum1 = Reduce(kept1, sent1, ((2, 1), (1, 1)) * 2, paired, rows, pack_rows, unpack_rows)
    sum1.start()
    sum3.start(rows)
    grad1_out = after(grad1, sum3.sent)
    kept_out, sent_out = run_back_out(spots, grad1_out, act0)
    sum_out = Reduce(kept_out, sent_out, ((1, 4),), paired)
    sum_out.start()
    sum1.start(kept_out)
    grad1_in = after(grad1, sum1.sent)
    grad0, pair, kept_in, sent_in = run_back_first(
        table, spots, h0, vectors, grad1_in, weights0, pre0
    )
    sum_in = Reduce(kept_in, sent_in, ((4, 1),), paired, pair, pack_pair, unpack_pair)
    sum_in.start()
    sum1.start(pair)
    sum_out.start(pair)
    sum3.start(pair)
    sum_in.start(sum1.sent, sum_out.sent)
    sum1.start()
    sum_out.start(sum1.sent)
    sum1.start(sum_out.sent)
    sum_in.start(sum_out.sent)
    sum_out.start(sum1.sent)
    sum_in.start(sum_out.sent)
    sum_out.start(sum_in.sent)
    sum_in.start()
    whole3, _ = sum3.finish(sum_in.sent)
    whole1, rows = sum1.finish(sum_in.sent)
    whole_out, _ = sum_out.finish()
    whole_in, pair = sum_in.finish()
    rows = jnp.concatenate([pair[:2], rows[2:]])
    reduced = (
        jnp.stack([join_columns(whole_in, 4), join_columns(whole3[: 4 * n], 4)]),
        jnp.stack([whole_out, whole3[4 * n :]]),
        jnp.stack([join_columns(whole1[: 2 * n], 2), join_columns(whole1[3 * n : 5 * n], 2)]),
        jnp.stack([whole1[2 * n : 3 * n], whole1[5 * n :]]),
        lax.dynamic_slice(rows, (0, width * me), (30, width)).T,
    )
    sublayer_rms = jnp.sqrt(rows[30, :5] / (rows[30, 5] * frames.shape[2]))
    masters = (ffn_in_master, ffn_out_master, mix_in_master, mix_out_master, vector_master.T)
    firsts = (ffn_in_first, ffn_out_first, mix_in_first, mix_out_first, vector_first.T)
    seconds = (ffn_in_second, ffn_out_second, mix_in_second, mix_out_second, vector_second.T)
    results = [
        adamw(
            masters[slot_index],
            firsts[slot_index],
            seconds[slot_index],
            reduced[slot_index],
            RATE_MATRIX if slot_index < 4 else RATE_VECTOR,
            WEIGHT_DECAY if slot_index < 4 else 0.0,
        )
        for slot_index in range(5)
    ]
    results[4] = tuple(part.T for part in results[4])
    return (
        activations[None],
        grad0[None],
        results[0][0],
        results[1][0],
        results[2][0],
        results[3][0],
        results[4][0],
        results[0][1],
        results[1][1],
        results[2][1],
        results[3][1],
        results[4][1],
        results[0][2],
        results[1][2],
        results[2][2],
        results[3][2],
        results[4][2],
        results[0][3],
        results[1][3],
        results[2][3],
        results[3][3],
        results[4][3],
        sublayer_rms,
    )


def solution(mesh):
    return jax.shard_map(
        local,
        mesh=mesh,
        in_specs=(
            P(("dp", "fsdp"), None, None),
            P(("dp", "fsdp"), None, None),
            P(("dp", "fsdp")),
            P(None, ("dp", "fsdp"), None),
            P(None, ("dp", "fsdp"), None),
            P(None, ("dp", "fsdp"), None),
            P(None, ("dp", "fsdp"), None),
            P(None, ("dp", "fsdp")),
            P(None, ("dp", "fsdp"), None),
            P(None, ("dp", "fsdp"), None),
            P(None, ("dp", "fsdp"), None),
            P(None, ("dp", "fsdp"), None),
            P(None, ("dp", "fsdp")),
            P(None, ("dp", "fsdp"), None),
            P(None, ("dp", "fsdp"), None),
            P(None, ("dp", "fsdp"), None),
            P(None, ("dp", "fsdp"), None),
            P(None, ("dp", "fsdp")),
        ),
        out_specs=(
            P(("dp", "fsdp"), None, None),
            P(("dp", "fsdp"), None, None),
            P(None, ("dp", "fsdp"), None),
            P(None, ("dp", "fsdp"), None),
            P(None, ("dp", "fsdp"), None),
            P(None, ("dp", "fsdp"), None),
            P(None, ("dp", "fsdp")),
            P(None, ("dp", "fsdp"), None),
            P(None, ("dp", "fsdp"), None),
            P(None, ("dp", "fsdp"), None),
            P(None, ("dp", "fsdp"), None),
            P(None, ("dp", "fsdp")),
            P(None, ("dp", "fsdp"), None),
            P(None, ("dp", "fsdp"), None),
            P(None, ("dp", "fsdp"), None),
            P(None, ("dp", "fsdp"), None),
            P(None, ("dp", "fsdp")),
            P(None, ("dp", "fsdp"), None),
            P(None, ("dp", "fsdp"), None),
            P(None, ("dp", "fsdp"), None),
            P(None, ("dp", "fsdp"), None),
            P(None, ("dp", "fsdp")),
            P(),
        ),
        check_vma=False,
    )
```

```python
import functools

import jax

import jax.numpy as jnp
from jax import lax
from jax.experimental import pallas as pl
from jax.experimental.pallas import tpu as pltpu
from jax.sharding import PartitionSpec as P

HEADS = 8
NSTATE = 32
KERNEL = 15
STEP_NUMBER = 5


NORM_EPS = 1e-05
BETA_FIRST = 0.5
BETA_SECOND = 0.6
ADAM_EPS = 1e-08
RATE_MATRIX = 0.02
RATE_VECTOR = 0.2
WEIGHT_DECAY = 0.01


def adamw(master, first, second, gradient, rate, decay):
    first_new = BETA_FIRST * first + (1.0 - BETA_FIRST) * gradient
    second_new = BETA_SECOND * second + (1.0 - BETA_SECOND) * gradient * gradient
    first_hat = first_new / (1.0 - BETA_FIRST**STEP_NUMBER)
    second_hat = second_new / (1.0 - BETA_SECOND**STEP_NUMBER)
    updated = master - rate * (first_hat / (jnp.sqrt(second_hat) + ADAM_EPS) + decay * master)
    return (updated, first_new, second_new, updated.astype(jnp.bfloat16))


AXES = ("dp", "fsdp")
CORE, Z_HIGH, Z_LOW = 8, 4, 2
STAGES = (Z_HIGH, Z_LOW, (1, 16), (16, 1))


def swap(values, mask):
    masks = mask if isinstance(mask, tuple) else (mask, mask)
    return lax.ppermute(values, AXES, [(i, i ^ masks[(i >> 3) & 1]) for i in range(32)])


def after(values, *earlier):
    return lax.optimization_barrier((values, *earlier))[0] if earlier else values


def add_low(left, right):
    return (left.astype(jnp.float32) + right.astype(jnp.float32)).astype(jnp.bfloat16)


def pack_rows(sums):
    low = lax.reduce_precision(sums, 8, 7)
    rest = jnp.pad(sums[30:31] - low[30:31], ((31, 0), (0, 0)))
    return (low + rest).astype(jnp.bfloat16).reshape(2, 16, 512)


def unpack_rows(message):
    rows = message.astype(jnp.float32).reshape(32, 512)
    return jnp.concatenate([rows[:30], rows[30:31] + rows[31:32], jnp.zeros((1, 512), jnp.float32)])


def cut_columns(matrix):
    rows, columns = matrix.shape
    return matrix.reshape(rows, columns // 512, 512).transpose(1, 0, 2).reshape(-1, 512)


def pieces_of(matrix):
    by_piece = matrix.reshape(32, matrix.shape[0] // 32, -1, 512)
    return jnp.moveaxis(by_piece, 2, 1).reshape(32, -1, 512)


def join_columns(pieces, columns):
    lead = pieces.shape[:-2]
    rows = pieces.shape[-2] // columns
    moved = jnp.moveaxis(pieces.reshape(*lead, columns, rows, 512), -3, -2)
    return moved.reshape(*lead, rows, columns * 512)


def sync(*arrays):
    return lax.optimization_barrier(arrays)


def join(*arrays):
    return jnp.concatenate(arrays)


def shard_of(parts):
    return join(*[cut_columns(part.astype(jnp.bfloat16)).reshape(-1, 16, 512) for part in parts])


def gather_all(first, middle, last, vectors):
    far, near, late, later = STAGES
    own, mid, end = shard_of(first), shard_of(middle), shard_of(last)
    size = own.shape[0]
    vectors = vectors + swap(vectors, CORE)
    got0, got1 = swap(own, far), swap(own, near)
    vectors = vectors + swap(after(vectors, own), far)
    own, mid, end, got0, got1, vectors = sync(own, mid, end, got0, got1, vectors)

    got1_late = swap(join(got0, vectors), near)
    two = join(own, got0)
    got2 = swap(two, late)
    mid_got = swap(mid, far)
    got1_late, two, got2, mid_got, vectors = sync(got1_late, two, got2, mid_got, vectors)

    vectors = vectors + got1_late[size:]
    other_two = join(got1, got1_late[:size], vectors)
    got2_late = swap(other_two, late)
    four = join(two, other_two[:-2])
    got3 = swap(four, later)
    mid = join(mid, mid_got)
    mid_got, end_got = swap(mid, near), swap(after(end, mid_got), far)
    got2_late, got3, mid_got, end_got, other_two = sync(got2_late, got3, mid_got, end_got, other_two)

    vectors = vectors + got2_late[2 * size :]
    other_four = join(got2, got2_late[: 2 * size], vectors)
    got3_late = swap(other_four, later)
    mid = join(mid, mid_got)
    end = join(end, end_got)
    mid_got, end_got = swap(mid, late), swap(end, near)
    far_pieces = [swap(four, CORE), swap(other_four, CORE), swap(got3, CORE)]
    got3_late, mid_got, end_got, vectors = sync(got3_late, mid_got, end_got, vectors)

    vectors = vectors + got3_late[4 * size :]
    far_pieces.append(swap(got3_late, CORE))
    mid = join(mid, mid_got)
    mid_got, mid_far = swap(mid, later), swap(mid, CORE)
    end = join(end, end_got)
    end_got = swap(end, late)
    return (four, other_four, got3, got3_late, *far_pieces), vectors, (mid, mid_got, mid_far), (end, end_got)


def gather_whole(parts):
    gathered = [lax.all_gather(part.astype(jnp.bfloat16), AXES, axis=0, tiled=True) for part in parts]
    pieces = join(*[pieces_of(matrix) for matrix in gathered]) if len(parts) == 1 else jnp.concatenate(
        [pieces_of(matrix) for matrix in gathered], axis=1
    )
    return tuple(pieces.reshape(4, -1, 16, 512))


class Reduce:
    def __init__(self, columns, paired, rows=None, pack=None, unpack=None):
        self.columns, self.rows, self.pack, self.unpack, self.paired = columns, rows, pack, unpack, paired
        self.parts, self.stage, self.riding = [], 0, rows is not None
        if paired and rows is not None:
            self.more = swap(pack(rows), CORE)

    def add(self, kept, sent):
        self.parts.append((kept, swap(sent, CORE) if self.paired else sent))

    def start(self, *earlier):
        if not self.paired:
            return
        self.stage += 1
        if self.stage == 1:
            parts = [(kept, after(got, *earlier)) for kept, got in self.parts]
            count = 8 * sum(kept.shape[1] for kept, _ in parts)
            sent = jnp.concatenate([add_low(kept[8:], got[8:]) for kept, got in parts], axis=1)
            sent = sent.reshape(-1, 16, 512)
            more = after(self.more, *earlier) if self.riding else None
        else:
            count = self.kept.shape[0] // 2
            got = after(self.got, *earlier)
            sent = add_low(self.kept[count:], got[count : 2 * count])
            more = got[2 * count :]
        if self.riding:
            self.rows = self.rows + self.unpack(more)
        if self.rows is not None:
            sent = jnp.concatenate([sent, self.pack(self.rows)])
            self.riding = True
        new = swap(sent, STAGES[4 - self.stage])
        if self.stage == 1:
            parts = [(after(kept, sent)[:8], after(got, sent)[:8]) for kept, got in parts]
            kept = jnp.concatenate([add_low(kept, got) for kept, got in parts], axis=1)
            self.kept = kept.reshape(-1, 16, 512)
            self.groups = kept.shape[1]
        else:
            self.kept = add_low(after(self.kept, sent)[:count], after(got, sent)[:count])
        self.got, self.sent = new, sent

    def begun(self):
        if not self.paired:
            return ()
        return tuple(self.sent) if isinstance(self.sent, list) else (self.sent,)

    def attach(self, rows):
        if self.paired:
            rows = rows + self.unpack(swap(self.pack(rows), CORE))
            rows = rows + self.unpack(swap(self.pack(rows), STAGES[3]))
        self.rows = rows

    def spread(self, *earlier):
        got = after(self.got, *earlier)
        total = self.kept.astype(jnp.float32) + got[: 4 * self.groups].astype(jnp.float32)
        self.rows = self.rows + self.unpack(got[4 * self.groups :])
        total = total.reshape(4, self.groups, 16, 512)
        riders = self.pack(self.rows)
        self.sent = [jnp.concatenate([total[spot].astype(jnp.bfloat16), riders]) for spot in (2, 1, 3)]
        masks = (Z_LOW, Z_HIGH, Z_LOW | Z_HIGH)
        self.kept, self.got = total[0], [swap(sent, mask) for sent, mask in zip(self.sent, masks)]

    def finish(self, *earlier):
        if not self.paired:
            return self.scatter()
        if isinstance(self.got, list):
            pieces = [got[: self.groups].astype(jnp.float32) for got in self.got]
            total = (self.kept + pieces[0]) + (pieces[1] + pieces[2])
            return total.reshape(-1, 512), (self.rows, *[got[self.groups :] for got in self.got])
        self.got = after(self.got, *earlier)
        total = self.kept.astype(jnp.float32) + self.got[: self.groups].astype(jnp.float32)
        rows = None if self.rows is None else self.rows + self.unpack(self.got[self.groups :])
        return total.reshape(-1, 512), rows

    def scatter(self):
        pieces = jnp.concatenate([jnp.concatenate(part) for part in self.parts], axis=1).reshape(32, -1, 512)
        sums, start = [], 0
        for count, tall in self.columns:
            rows = 16 * count * tall
            matrix = join_columns(pieces[:, start : start + rows], count).reshape(512 * tall, -1)
            matrix = lax.psum_scatter(matrix.astype(jnp.float32), AXES, scatter_dimension=0, tiled=True)
            sums.append(cut_columns(matrix))
            start += rows
        rows = None if self.rows is None else lax.psum(self.rows, AXES)
        if rows is not None and rows.shape[0] == 8:
            rows = (rows, *[jnp.zeros((1, 16, 512), jnp.bfloat16)] * 3)
        return jnp.concatenate(sums), rows


def pack_pair(sums):
    low = lax.reduce_precision(sums[:2], 8, 7)
    parts = [low, sums[:2] - low, jnp.zeros((12, 512), jnp.float32)]
    return jnp.concatenate(parts).astype(jnp.bfloat16)[None]


def unpack_pair(message):
    rows = message[0].astype(jnp.float32)
    return jnp.concatenate([rows[0:2] + rows[2:4], jnp.zeros((6, 512), jnp.float32)])


TILE = 64
F32, LOW = jnp.float32, jnp.bfloat16
NN, NT, TN = ((1,), (0,)), ((1,), (1,)), ((0,), (0,))
VMEM_BYTES = 32 * 1024 * 1024


def mm(left, right, dims=NN):
    return lax.dot_general(left, right, (dims, ((), ())), preferred_element_type=F32)


def tiles(rows=512, step=TILE):
    return [pl.ds(start, step) for start in range(0, rows, step)]


def sigmoid(values):
    return 0.5 * jnp.tanh(0.5 * values) + 0.5


def standardize(values):
    centered = values - jnp.mean(values, axis=-1, keepdims=True)
    variance = jnp.mean(centered * centered, axis=-1, keepdims=True)
    spread = lax.rsqrt(variance + NORM_EPS)
    return centered * spread, spread


def standardize_back(grad, unit, spread):
    mean_grad = jnp.mean(grad, axis=-1, keepdims=True)
    mean_both = jnp.mean(grad * unit, axis=-1, keepdims=True)
    return spread * (grad - mean_grad - unit * mean_both)


def row(values):
    return jnp.sum(values, axis=0, keepdims=True)


def square(pieces):
    return pieces.reshape(512, 512)


class Place:
    def __init__(self, paired):
        self.paired = paired
        if paired:
            self.dp, self.fsdp = lax.axis_index("dp"), lax.axis_index("fsdp")
            self.core = self.dp & 1

    def device(self, spot):
        if not self.paired:
            return spot
        side, bits = spot // 16, [(spot >> place) & 1 for place in range(4)]
        first, second = 2 * bits[3] + side, bits[2]
        turned_first, turned_second = 2 * bits[2] + side, bits[3]
        around = 2 * bits[1] + 4 * bits[0]
        straight = self.core == side
        dp = self.dp ^ jnp.where(straight, first, turned_first)
        return 8 * dp + (self.fsdp ^ jnp.where(straight, second + around, turned_second + around))

    def chunk(self, step):
        return self.dp ^ (0, 2, 1, 3)[step] if self.paired else step

    def spot(self, step, f):
        if not self.paired:
            return 8 * (step % 2) + f
        rel = self.fsdp ^ f
        y_bit, z_spot = rel & 1, (rel & 2) + ((rel >> 2) & 1)
        straight = self.core == step // 2
        return z_spot + jnp.where(straight, 8 * (step % 2) + 4 * y_bit, 8 * y_bit + 4 * (step % 2))


def place_ffn(table, sources, w_in, w_out):
    each_has = 32 // len(sources)
    for side, source in enumerate(sources):
        for spot in range(each_has):
            device = table.device(each_has * side + spot)
            w_in[:, device] = source[pl.ds(8 * spot, 4)]
            w_out[pl.ds(4 * device, 4)] = source[pl.ds(8 * spot + 4, 4)]


def place_mix(table, sources, first, weights):
    each_has = 32 // len(sources)
    for side, source in enumerate(sources):
        for spot in range(each_has):
            weights[:, table.device(each_has * side + spot)] = source[pl.ds(6 * spot + first, 3)]


def start_all(copies):
    for copy in copies:
        copy.start()


def wait_all(copies):
    for copy in copies:
        copy.wait()


def fill_normed(h_ref, vec_ref, index, normed):
    gain = vec_ref[pl.ds(2 * index, 1)].astype(F32)
    shift = vec_ref[pl.ds(2 * index + 1, 1)].astype(F32)
    for part in tiles():
        unit, _ = standardize(h_ref[part].astype(F32))
        normed[part] = (unit * gain + shift).astype(LOW)


def order_rows(table, natural, ordered):
    for spot in range(32):
        ordered[spot] = natural[table.device(spot)]


def fill_transposed(source, natural):
    for part in tiles(step=128):
        turned = source[part].astype(F32).T.astype(LOW)
        natural[:, :, part] = turned.reshape(32, 16, 128)


def norm_back(h_ref, vec_ref, index, grad_normed, grad_in, grad_out):
    gain = vec_ref[pl.ds(2 * index, 1)].astype(F32)
    grad_gain, grad_shift = jnp.zeros((1, 512), F32), jnp.zeros((1, 512), F32)
    for part in tiles():
        unit, spread = standardize(h_ref[part].astype(F32))
        grad = grad_normed[part]
        grad_gain = grad_gain + row(grad * unit)
        grad_shift = grad_shift + row(grad)
        grad_out[part] = grad_in[part] + standardize_back(grad * gain, unit, spread)
    return grad_gain, grad_shift


def valid_rows(length, part):
    places = part.start + lax.broadcasted_iota(jnp.int32, (part.size, 1), 0)
    return (places < length).astype(F32)


def valid_lanes(length):
    return (lax.broadcasted_iota(jnp.int32, (1, 512), 1) < length).astype(F32)


def ffn_forward(length, h_ref, normed, w_in, w_out, pre, act, out, new_h, save):
    for j in range(4):
        pre_j, act_j = pre.at[j], act(j)
        pre_j[...] = mm(normed[...], square(w_in[j]))
        for part in tiles():
            values = pre_j[part]
            act_j[part] = (values * sigmoid(values)).astype(LOW)
        save(j)
        more = mm(act_j[...], square(w_out[pl.ds(32 * j, 32)]))
        out[...] = more if j == 0 else out[...] + more
    total = jnp.zeros((1, 512), F32)
    for part in tiles():
        half = 0.5 * out[part]
        new_h[part] = h_ref[part].astype(F32) + half
        total = total + row(valid_rows(length, part) * half * half)
    return total


def place_out_grads(table, step, first, kept, sent, act, grad_low):
    products = mm(act, grad_low, TN).astype(LOW).reshape(8, 4, 16, 512)
    for f in range(8):
        (kept, sent)[step // 2][table.spot(step, f), pl.ds(first, 4)] = products[f]


def place_rows(kept, sent, group, products):
    pieces = products.astype(LOW).reshape(32, 16, 512)
    kept[:, group] = pieces[:16]
    sent[:, group] = pieces[16:]


def ffn_backward(table, w_out, pre, grad_low, turned, act, grad_pre, kept, sent):
    for step in range(4):
        chunk = table.chunk(step)
        pre_j = pre.at[chunk]
        grad_act = mm(grad_low[...], square(w_out[pl.ds(32 * chunk, 32)]), NT)
        for part in tiles():
            values = pre_j[part]
            gate = sigmoid(values)
            lifted = values * gate
            if act is not None:
                act[part] = lifted.astype(LOW)
            slope = gate + lifted * (1.0 - gate)
            grad_pre[chunk, part] = (grad_act[part.start : part.start + part.size] * slope).astype(LOW)
        place_rows(kept, sent, chunk, mm(square(turned[...]), grad_pre[chunk]))
        if act is not None:
            place_out_grads(table, step, 4, kept, sent, act[...], grad_low[...])


def first_kernel(paired, length, h_ref, vec_ref, *refs):
    table = Place(paired)
    *pieces, h1_ref, pre_hbm, act_hbm, stat_ref, in_hbm, out_hbm = refs[:-9]
    w_in, w_out, normed, act, out, pre, pre_sem, act_sem, w_sem = refs[-9:]
    place_ffn(table, pieces, w_in, w_out)
    weights = [
        pltpu.make_async_copy(w_in, in_hbm, w_sem.at[0]),
        pltpu.make_async_copy(w_out, out_hbm, w_sem.at[1]),
    ]
    start_all(weights)
    fill_normed(h_ref, vec_ref, 0, normed)

    copies = [
        (
            pltpu.make_async_copy(pre.at[j], pre_hbm.at[j], pre_sem.at[j]),
            pltpu.make_async_copy(act.at[j], act_hbm.at[j], act_sem.at[j]),
        )
        for j in range(4)
    ]

    def save(j):
        start_all(copies[j])

    stat_ref[...] = ffn_forward(
        length[0], h_ref, normed, w_in, w_out, pre, lambda j: act.at[j], out, h1_ref, save
    )
    for j in range(4):
        wait_all(copies[j])
    wait_all(weights)


def last_kernel(
    paired, length, h_ref, vec_ref, cot_ref, held, got, held_far, got_far,
    top_ref, grad_ref, rows_ref, kept, sent, w_in, grad_pre,
    w_out, normed, act, out, pre, low, natural, turned
):
    table = Place(paired)
    place_ffn(table, (held, got, held_far, got_far), w_in, w_out)
    fill_normed(h_ref, vec_ref, 4, normed)
    fill_transposed(normed, natural)
    order_rows(table, natural, turned)
    stat4 = ffn_forward(length[0], h_ref, normed, w_in, w_out, pre, lambda j: act, out, grad_ref, lambda j: None)
    gain, shift = vec_ref[pl.ds(10, 1)].astype(F32), vec_ref[pl.ds(11, 1)].astype(F32)
    grad_gain, grad_shift = jnp.zeros((1, 512), F32), jnp.zeros((1, 512), F32)
    stat5 = jnp.zeros((1, 512), F32)
    for part in tiles():
        values = grad_ref[part]
        stat5 = stat5 + row(valid_rows(length[0], part) * values * values)
        unit, spread = standardize(values)
        top_ref[part] = unit * gain + shift
        grad = cot_ref[part].astype(F32)
        grad_gain = grad_gain + row(grad * unit)
        grad_shift = grad_shift + row(grad)
        back = standardize_back(grad * gain, unit, spread)
        grad_ref[part] = back
        low[part] = (0.5 * back).astype(LOW)
    ffn_backward(table, w_out, pre, low, turned, act, grad_pre, kept, sent)
    rows_ref[...] = jnp.concatenate([grad_gain, grad_shift, stat4, stat5, jnp.zeros((4, 512), F32)])


def back_out_kernel(paired, grad_in, act, kept, sent, low):
    table = Place(paired)
    for part in tiles():
        low[part] = (0.5 * grad_in[part]).astype(LOW)
    for step in range(4):
        place_out_grads(table, step, 0, kept, sent, act[table.chunk(step)], low[...])


def back_in_kernel(
    paired, h_ref, vec_ref, grad_in, w_out, pre, kept, sent, grad_pre, normed, low, natural, turned
):
    table = Place(paired)
    fill_normed(h_ref, vec_ref, 0, normed)
    fill_transposed(normed, natural)
    order_rows(table, natural, turned)
    for part in tiles():
        low[part] = (0.5 * grad_in[part]).astype(LOW)
    ffn_backward(table, w_out, pre, low, turned, None, grad_pre, kept, sent)


def ffn_grad_kernel(index, h_ref, vec_ref, grad_in, w_in, grad_pre, grad_ref, rows_ref, out):
    for j in range(4):
        more = mm(grad_pre[j], square(w_in[j]), NT)
        out[...] = more if j == 0 else out[...] + more
    gain, shift = norm_back(h_ref, vec_ref, index, out, grad_in, grad_ref)
    rows_ref[...] = jnp.concatenate([gain, shift, jnp.zeros((6, 512), F32)])


def vector_step_kernel(
    width, rows_ref, pair_ref, got0, got1, got2, master, first, second, new_ref, first_ref, second_ref, copy_ref
):
    pair = pair_ref[0:2]
    for got in (got0, got1, got2):
        message = got[0].astype(F32)
        pair = pair + (message[0:2] + message[2:4])
    rows = jnp.concatenate([pair, rows_ref[2:32]])
    me = lax.axis_index("dp") * lax.axis_size("fsdp") + lax.axis_index("fsdp")
    turned = pltpu.roll(rows, lax.rem(512 - width * me, 512), 1)[:, 0:128].T
    results = adamw(master[...], first[...], second[...], turned[0:width, 0:30], RATE_VECTOR, 0.0)
    for ref, values in zip((new_ref, first_ref, second_ref, copy_ref), results):
        ref[...] = values


def vector_columns(vec_ref, pad):
    pad[...] = jnp.zeros((128, 512), F32)
    pad[pl.ds(0, 32)] = vec_ref[...].astype(F32)
    return pad[...].T


def ssm_decays(columns):
    rates = jnp.exp(columns[0:256, 13:14])
    lags = lax.broadcasted_iota(jnp.int32, (1, 512), 1).astype(F32)
    return jnp.exp(-rates * lags), rates, columns[256:512, 13:14]


def head_matrix(kernels, head):
    line = jnp.concatenate([kernels[head : head + 1], jnp.zeros((1, 128), F32)], axis=1)
    skewed = pltpu.roll(jnp.broadcast_to(line, (128, 640)), 0, 1, stride=1, stride_axis=0)
    return skewed[:, :512].astype(LOW)


def blocks_of(rows):
    return jnp.concatenate([rows[:, 128 * b : 128 * (b + 1)] for b in range(4)], axis=0)


def ssm_kernel(
    paired, length, h_ref, vec_ref, held, got, held_far, got_far, h2_ref, saved_hbm, stat_ref, weights_hbm,
    weights, normed, act, saved, pad, save_sem, w_sem
):
    table = Place(paired)
    place_mix(table, (held, got, held_far, got_far), 0, weights)
    hand_on = pltpu.make_async_copy(weights, weights_hbm, w_sem)
    hand_on.start()
    fill_normed(h_ref, vec_ref, 1, normed)
    columns = vector_columns(vec_ref, pad)
    decays, _, coefs = ssm_decays(columns)
    kernels = jnp.sum((coefs * decays).reshape(8, 32, 512), axis=1)
    mask = valid_lanes(length[0])
    signal, gate, mixed = saved.at[0], saved.at[1], saved.at[2]
    signal[...] = mm(square(weights[0]), normed[...], ((0,), (1,))) * mask
    gate[...] = mm(square(weights[1]), normed[...], ((0,), (1,)))
    copies = [pltpu.make_async_copy(saved.at[k], saved_hbm.at[k], save_sem.at[k]) for k in range(3)]
    copies[0].start()
    copies[1].start()
    for head in range(8):
        part = pl.ds(64 * head, 64)
        rows = signal[part]
        spread = mm(blocks_of(rows).astype(LOW), head_matrix(kernels, head))
        skip = columns[64 * head : 64 * head + 64, 12:13]
        for a in range(4):
            lanes = pl.ds(128 * a, 128)
            total = skip * rows[:, 128 * a : 128 * a + 128]
            for b in range(a + 1):
                total = total + spread[64 * b : 64 * b + 64, 128 * (a - b) : 128 * (a - b) + 128]
            mixed[part, lanes] = total
            gates = gate[part, lanes]
            act[part, lanes] = (total * gates * sigmoid(gates)).astype(LOW)
    copies[2].start()
    out = mm(act[...], square(weights[2]), TN)
    total = jnp.zeros((1, 512), F32)
    for part in tiles():
        values = out[part.start : part.start + part.size]
        h2_ref[part] = h_ref[part] + values
        total = total + row(valid_rows(length[0], part) * values * values)
    stat_ref[...] = total
    wait_all(copies)
    hand_on.wait()


def ssm_back_kernel(
    paired, length, h_ref, vec_ref, grad_in, weights, saved, stat1, stat2, rows2, rows3, rows4,
    grad_ref, rows_ref, kept, sent,
    normed, low, natural, turned, act, act_turned, grad_pre, out, pad, kernel_grads, skip_grads
):
    table = Place(paired)
    fill_normed(h_ref, vec_ref, 1, normed)
    fill_transposed(normed, natural)
    order_rows(table, natural, turned)
    for part in tiles():
        low[part] = grad_in[part].astype(LOW)
    columns = vector_columns(vec_ref, pad)
    decays, rates, coefs = ssm_decays(columns)
    kernels = jnp.sum((coefs * decays).reshape(8, 32, 512), axis=1)
    mask = valid_lanes(length[0])
    signal, gate, mixed = saved.at[0], saved.at[1], saved.at[2]
    out[...] = mm(square(weights[2]), low[...], NT)
    flipped = lax.broadcasted_iota(jnp.int32, (128, 128), 0) + lax.broadcasted_iota(jnp.int32, (128, 128), 1)
    flip = (flipped == 127).astype(F32).astype(LOW)
    for head in range(8):
        part = pl.ds(64 * head, 64)
        rows, gates, mixes, grad_act = signal[part], gate[part], mixed[part], out[part]
        gating = sigmoid(gates)
        lifted = gates * gating
        act[pl.ds(4 * head, 4)] = (mixes * lifted).astype(LOW).reshape(4, 16, 512)
        grad_mixed = grad_act * lifted
        grad_pre[1, part] = (grad_act * mixes * (gating + lifted * (1.0 - gating))).astype(LOW)
        grad_low = grad_mixed.astype(LOW)
        shifted = jnp.concatenate(
            [grad_low]
            + [
                jnp.concatenate([grad_low[:, 128 * b :], jnp.zeros((64, 128 * b), LOW)], axis=1)
                for b in (1, 2, 3)
            ],
            axis=0,
        )
        back = mm(shifted, head_matrix(kernels, head), NT)
        mirrored = mm(blocks_of(rows).astype(LOW), flip).astype(LOW)
        lag_sums = mm(mirrored, shifted, TN)
        lag_sums = jnp.concatenate([lag_sums, jnp.zeros((128, 128), F32)], axis=1)
        lag_sums = row(pltpu.roll(lag_sums, 0, 1, stride=1, stride_axis=0))
        kernel_grads[pl.ds(head, 1)] = pltpu.roll(lag_sums, 640 - 127, 1)[:, :512]
        skip = columns[64 * head : 64 * head + 64, 12:13]
        pad_lane = jnp.sum(grad_mixed * rows, axis=1, keepdims=True)
        natural_grad = jnp.concatenate([back[64 * b : 64 * b + 64] for b in range(4)], axis=1)
        grad_pre[0, part] = ((natural_grad + skip * grad_mixed) * mask).astype(LOW)
        normed_f = jnp.broadcast_to(pad_lane, (64, 128))
        skip_grads[part] = normed_f
    order_rows(table, act, act_turned)
    place_rows(kept, sent, 2, mm(square(act_turned[...]), low[...]))
    for q in range(2):
        more = mm(grad_pre[q], square(weights[q]), ((0,), (1,)))
        out[...] = more if q == 0 else out[...] + more
        place_rows(kept, sent, q, mm(square(turned[...]), grad_pre[q], NT))
    gain1, shift1 = norm_back(h_ref, vec_ref, 1, out, grad_in, grad_ref)
    lag_grads = jnp.broadcast_to(kernel_grads[...].reshape(8, 1, 512), (8, 32, 512)).reshape(256, 512)
    lags = lax.broadcasted_iota(jnp.int32, (1, 512), 1).astype(F32)
    weighed = lag_grads * decays
    coef_grads = jnp.sum(weighed, axis=1, keepdims=True)
    rate_grads = -rates * coefs * jnp.sum(weighed * lags, axis=1, keepdims=True)
    lanes = lax.broadcasted_iota(jnp.int32, (1, 128), 1)
    ssm_column = jnp.concatenate([rate_grads, coef_grads], axis=0)
    both = jnp.where(lanes == 0, skip_grads[...], 0.0) + jnp.where(lanes == 1, ssm_column, 0.0)
    turned_rows = both.T
    lanes = lax.broadcasted_iota(jnp.int32, (1, 512), 1)
    stats = jnp.where(lanes == 5, length[0].astype(F32), 0.0)
    for place, sums in enumerate([stat1[...], stat2[...], rows2[20:21], rows3[2:3], rows3[3:4]]):
        stats = stats + jnp.where(lanes == place, jnp.sum(sums, axis=1, keepdims=True), 0.0)
    nothing = jnp.zeros((2, 512), F32)
    rows_ref[...] = jnp.concatenate(
        [nothing, gain1, shift1, rows2[0:4], rows4[0:2], rows3[0:2], turned_rows[0:2], rows2[4:20], stats, nothing[0:1]]
    )


PAD = 16


def conv_kernel(
    paired, length, h_ref, vec_ref, held, got, held_far, got_far, h3_ref, saved_hbm, stat_ref, weights_hbm,
    weights, normed, act, saved, padded, save_sem, w_sem
):
    table = Place(paired)
    place_mix(table, (held, got, held_far, got_far), 3, weights)
    hand_on = pltpu.make_async_copy(weights, weights_hbm, w_sem)
    hand_on.start()
    fill_normed(h_ref, vec_ref, 2, normed)
    copies = [pltpu.make_async_copy(saved.at[k], saved_hbm.at[k], save_sem.at[k]) for k in range(3)]
    for q in range(2):
        saved[q] = mm(normed[...], square(weights[q]))
        copies[q].start()
    for c in range(4):
        padded[c, pl.ds(0, PAD)] = jnp.zeros((PAD, 128), F32)
        padded[c, pl.ds(PAD + 512, PAD)] = jnp.zeros((PAD, 128), F32)
        lanes = pl.ds(128 * c, 128)
        for part in tiles():
            glu = saved[0, part, lanes] * sigmoid(saved[1, part, lanes]) * valid_rows(length[0], part)
            padded[c, pl.ds(PAD + part.start, part.size)] = glu
        taps = [vec_ref[pl.ds(14 + j, 1), lanes].astype(F32) for j in range(KERNEL + 1)]
        for part in tiles():
            total = jnp.broadcast_to(taps[KERNEL], (part.size, 128))
            for j in range(KERNEL):
                total = total + padded[c, pl.ds(PAD + part.start + j - 7, part.size)] * taps[j]
            saved[2, part, lanes] = total
    copies[2].start()
    gain, shift = vec_ref[pl.ds(6, 1)].astype(F32), vec_ref[pl.ds(7, 1)].astype(F32)
    for part in tiles():
        unit, _ = standardize(saved[2, part])
        values = unit * gain + shift
        act[part] = (values * sigmoid(values)).astype(LOW)
    out = mm(act[...], square(weights[2]))
    total = jnp.zeros((1, 512), F32)
    for part in tiles():
        values = out[part.start : part.start + part.size]
        h3_ref[part] = h_ref[part] + values
        total = total + row(valid_rows(length[0], part) * values * values)
    stat_ref[...] = total
    wait_all(copies)
    hand_on.wait()


def conv_back_kernel(
    paired, length, h_ref, vec_ref, grad_in, weights, saved, stat_in,
    grad_ref, rows_ref, kept, sent,
    normed, low, natural, turned, act, act_turned, grad_pre, out, padded, padded_grad
):
    table = Place(paired)
    fill_normed(h_ref, vec_ref, 2, normed)
    fill_transposed(normed, natural)
    order_rows(table, natural, turned)
    for part in tiles():
        low[part] = grad_in[part].astype(LOW)
    out[...] = mm(low[...], square(weights[2]), NT)
    gain, shift = vec_ref[pl.ds(6, 1)].astype(F32), vec_ref[pl.ds(7, 1)].astype(F32)
    gain3, shift3, bias = (jnp.zeros((1, 512), F32) for _ in range(3))
    for part in tiles():
        unit, spread = standardize(saved[2, part])
        values = unit * gain + shift
        gating = sigmoid(values)
        lifted = values * gating
        normed[part] = lifted.astype(LOW)
        grad = out[part] * (gating + lifted * (1.0 - gating))
        gain3 = gain3 + row(grad * unit)
        shift3 = shift3 + row(grad)
        back = standardize_back(grad * gain, unit, spread)
        bias = bias + row(back)
        for c in range(4):
            padded_grad[c, pl.ds(PAD + part.start, part.size)] = back[:, 128 * c : 128 * c + 128]
    fill_transposed(normed, act)
    order_rows(table, act, act_turned)
    place_rows(kept, sent, 2, mm(square(act_turned[...]), low[...]))
    tap_rows = []
    for c in range(4):
        lanes = pl.ds(128 * c, 128)
        for ref in (padded, padded_grad):
            ref[c, pl.ds(0, PAD)] = jnp.zeros((PAD, 128), F32)
            ref[c, pl.ds(PAD + 512, PAD)] = jnp.zeros((PAD, 128), F32)
        for part in tiles():
            glu = saved[0, part, lanes] * sigmoid(saved[1, part, lanes]) * valid_rows(length[0], part)
            padded[c, pl.ds(PAD + part.start, part.size)] = glu
        taps = [vec_ref[pl.ds(14 + j, 1), lanes].astype(F32) for j in range(KERNEL)]
        sums = [jnp.zeros((8, 128), F32) for _ in range(KERNEL)]
        for part in tiles():
            total = jnp.zeros((part.size, 128), F32)
            grad = padded_grad[c, pl.ds(PAD + part.start, part.size)]
            for j in range(KERNEL):
                total = total + padded_grad[c, pl.ds(PAD + part.start + 7 - j, part.size)] * taps[j]
                seen = padded[c, pl.ds(PAD + part.start + j - 7, part.size)]
                sums[j] = sums[j] + jnp.sum((grad * seen).reshape(part.size // 8, 8, 128), axis=0)
            total = total * valid_rows(length[0], part)
            gating = sigmoid(saved[1, part, lanes])
            first = total * gating
            grad_pre[0, part, lanes] = first.astype(LOW)
            grad_pre[1, part, lanes] = (first * saved[0, part, lanes] * (1.0 - gating)).astype(LOW)
        tap_rows.append(jnp.concatenate([row(values) for values in sums], axis=0))
    for q in range(2):
        more = mm(grad_pre[q], square(weights[q]), NT)
        out[...] = more if q == 0 else out[...] + more
        place_rows(kept, sent, q, mm(square(turned[...]), grad_pre[q]))
    gain2, shift2 = norm_back(h_ref, vec_ref, 2, out, grad_in, grad_ref)
    rows_ref[...] = jnp.concatenate(
        [gain2, shift2, gain3, shift3, jnp.concatenate(tap_rows, axis=1), bias, stat_in[...], jnp.zeros((3, 512), F32)]
    )


def call(kernel, scalars, arrays, outs, scratch, flops):
    in_vmem, in_hbm = pl.BlockSpec(memory_space=pltpu.VMEM), pl.BlockSpec(memory_space=pltpu.HBM)
    return pl.pallas_call(
        kernel,
        out_shape=[
            (pltpu.HBM if apart else jax.ShapeDtypeStruct)(shape, dtype) for shape, dtype, apart in outs
        ],
        in_specs=[pl.BlockSpec(memory_space=pltpu.SMEM)] * len(scalars) + [in_vmem] * len(arrays),
        out_specs=[in_hbm if apart else in_vmem for _, _, apart in outs],
        scratch_shapes=scratch,
        compiler_params=pltpu.CompilerParams(vmem_limit_bytes=VMEM_BYTES),
        cost_estimate=pl.CostEstimate(flops=40 * flops, bytes_accessed=64 << 20, transcendentals=1 << 24),
    )(*scalars, *arrays)


SQUARE, PIECES = (512, 512), (32, 16, 512)
DMA = pltpu.SemaphoreType.DMA
IN_FFN, OUT_FFN, MIX = (4, 32, 16, 512), (128, 16, 512), (3, 32, 16, 512)
SMALL, LARGE = 512 * 512 * 512 * 2, 512 * 512 * 2048 * 2


def low_scratch(*shapes):
    return [pltpu.VMEM(shape, LOW) for shape in shapes]


def full_scratch(*shapes):
    return [pltpu.VMEM(shape, F32) for shape in shapes]


def grads_of(groups):
    return [((16, groups, 16, 512), LOW, False)] * 2


def run_first(paired, length, h, vectors, pieces):
    return call(
        functools.partial(first_kernel, paired),
        [length],
        [h, vectors, *pieces],
        [(SQUARE, F32, False), ((4, 512, 512), F32, True), ((4, 512, 512), LOW, True), ((1, 512), F32, False)]
        + [(IN_FFN, LOW, True), (OUT_FFN, LOW, True)],
        low_scratch(IN_FFN, OUT_FFN, SQUARE, (4, 512, 512))
        + full_scratch(SQUARE, (4, 512, 512))
        + [DMA((4,)), DMA((4,)), DMA((2,))],
        2 * LARGE,
    )


def run_last(paired, length, h, vectors, cotangent, pieces):
    return call(
        functools.partial(last_kernel, paired),
        [length],
        [h, vectors, cotangent, *pieces],
        [(SQUARE, F32, False), (SQUARE, F32, False), ((8, 512), F32, False), *grads_of(8)]
        + [(IN_FFN, LOW, False), ((4, 512, 512), LOW, False)],
        low_scratch(OUT_FFN, SQUARE, SQUARE)
        + full_scratch(SQUARE, (4, 512, 512))
        + low_scratch(SQUARE, PIECES, PIECES),
        6 * LARGE,
    )


def run_back_out(paired, grad, act):
    return call(functools.partial(back_out_kernel, paired), [], [grad, act], grads_of(4), low_scratch(SQUARE), LARGE)


def run_back_in(paired, h, vectors, grad, w_out, pre):
    return call(
        functools.partial(back_in_kernel, paired),
        [],
        [h, vectors, grad, w_out, pre],
        [*grads_of(4), ((4, 512, 512), LOW, False)],
        low_scratch(SQUARE, SQUARE, PIECES, PIECES),
        2 * LARGE,
    )


def run_ffn_grad(index, h, vectors, grad, w_in, grad_pre):
    return call(
        functools.partial(ffn_grad_kernel, index),
        [],
        [h, vectors, grad, w_in, grad_pre],
        [(SQUARE, F32, False), ((8, 512), F32, False)],
        full_scratch(SQUARE),
        LARGE,
    )


def run_vector_step(rows, pair, master, first, second):
    shape = master.shape
    results = call(
        functools.partial(vector_step_kernel, shape[0]),
        [],
        [rows, *pair, master, first, second],
        [(shape, F32, False)] * 3 + [(shape, LOW, False)],
        [],
        SMALL // 40,
    )
    return tuple(part.T for part in results)


def run_mix(kernel, paired, length, h, vectors, pieces, last_scratch):
    return call(
        functools.partial(kernel, paired),
        [length],
        [h, vectors, *pieces],
        [(SQUARE, F32, False), ((3, 512, 512), F32, True), ((1, 512), F32, False), (MIX, LOW, True)],
        low_scratch(MIX, SQUARE, SQUARE) + full_scratch((3, 512, 512), last_scratch) + [DMA((3,)), DMA],
        4 * SMALL,
    )


def run_mix_back(kernel, paired, length, h, vectors, grad, weights, saved, more, rows, last_scratch):
    return call(
        functools.partial(kernel, paired),
        [length],
        [h, vectors, grad, *weights, saved, *more],
        [(SQUARE, F32, False), ((rows, 512), F32, False), *grads_of(3)],
        low_scratch(SQUARE, SQUARE, PIECES, PIECES, PIECES, PIECES, (2, 512, 512))
        + full_scratch(SQUARE, *last_scratch),
        8 * SMALL,
    )


def local(
    frames,
    cotangent,
    seq_lengths,
    ffn_in_master,
    ffn_out_master,
    mix_in_master,
    mix_out_master,
    vector_master,
    ffn_in_first,
    ffn_out_first,
    mix_in_first,
    mix_out_first,
    vector_first,
    ffn_in_second,
    ffn_out_second,
    mix_in_second,
    mix_out_second,
    vector_second,
):
    me = lax.axis_index(AXES)
    paired = (lax.axis_size("dp"), lax.axis_size("fsdp")) == (4, 8)
    low = jnp.bfloat16
    width, n = vector_master.shape[1], ffn_in_master.shape[1]
    placed = lax.dynamic_update_slice(
        jnp.zeros((32, 512), low), vector_master.astype(low), (0, width * me)
    ).reshape(2, 16, 512)
    first = [ffn_in_master[0], ffn_out_master[0]]
    middle = [mix_in_master[0], mix_out_master[0], mix_in_master[1], mix_out_master[1]]
    last = [ffn_in_master[1], ffn_out_master[1]]
    h0, length = frames[0], seq_lengths
    if paired:
        first, vectors, (mid, mid_got, mid_far), (end, end_got) = gather_all(first, middle, last, placed)
    else:
        first, middle, last = gather_whole(first), gather_whole(middle), gather_whole(last)
        vectors = lax.psum(placed, AXES)
    vectors = vectors.reshape(32, 512)
    h1, pre0, act0, stat1, *weights0 = run_first(paired, length, h0, vectors, first)
    if paired:
        mid_got, end_got, stat1 = sync(mid_got, end_got, stat1)
        end = join(end, end_got)
        end_got, end_far = swap(end, STAGES[3]), swap(end, CORE)
        middle = (mid, mid_got, mid_far, swap(mid_got, CORE))
    h2, saved1, stat2, *weights1 = run_mix(ssm_kernel, paired, length, h1, vectors, middle, (128, 512))
    h3, saved2, stat3, *weights2 = run_mix(
        conv_kernel, paired, length, h2, vectors, middle, (4, 512 + 2 * PAD, 128)
    )
    if paired:
        end_got, stat3 = sync(end_got, stat3)
        last = (end, end_got, end_far, swap(end_got, CORE))
    activations, grad4, rows3, kept3, sent3, w_in3, grad_pre3 = run_last(
        paired, length, h3, vectors, cotangent[0], last
    )
    sum3 = Reduce(((4, 1), (1, 4)), paired)
    sum3.add(kept3, sent3)
    grad3, rows4 = run_ffn_grad(4, h3, vectors, grad4, w_in3, grad_pre3)
    sum3.start(rows4)
    grad2, rows2, kept2, sent2 = run_mix_back(
        conv_back_kernel, paired, length, h2, vectors, after(grad3, *sum3.begun()), weights2, saved2, [stat3], 24,
        [(4, 512 + 2 * PAD, 128)] * 2,
    )
    grad1, rows, kept1, sent1 = run_mix_back(
        ssm_back_kernel, paired, length, h1, vectors, grad2, weights1, saved1,
        [stat1, stat2, rows2, rows3, rows4], 32, [(128, 512), (8, 512), (512, 128)],
    )
    sum1 = Reduce(((2, 1), (1, 1)) * 2, paired, rows, pack_rows, unpack_rows)
    sum1.add(kept1, sent1)
    sum1.add(kept2, sent2)
    sum3.start(rows)
    kept_out, sent_out = run_back_out(paired, after(grad1, *sum3.begun()), act0)
    sum_out = Reduce(((1, 4),), paired)
    sum_out.add(kept_out, sent_out)
    sum1.start(kept_out)
    grad1 = after(grad1, *sum1.begun())
    kept_in, sent_in, grad_pre0 = run_back_in(paired, h0, vectors, grad1, weights0[1], pre0)
    sum_in = Reduce(((4, 1),), paired, None, pack_pair, unpack_pair)
    sum_in.add(kept_in, sent_in)
    sum_out.start(kept_in)
    sum_in.start(*sum_out.begun())
    grad0, pair = run_ffn_grad(
        0, h0, vectors, after(grad1, *sum_in.begun()), weights0[0], grad_pre0
    )
    sum1.start(pair)
    sum3.start(pair)
    sum_in.attach(pair)
    sum_out.start(*sum1.begun())
    sum_in.start(*sum_out.begun())
    sum1.start(*sum_in.begun())
    sum3.start(*sum1.begun())
    sum_out.start(*sum3.begun())
    if paired:
        sum_in.spread(*sum_out.begun())
    sum1.start(*sum_in.begun())
    sum_out.start(*sum1.begun())
    whole3, _ = sum3.finish(*sum_out.begun())
    whole1, rows = sum1.finish(*sum_out.begun())
    whole_out, _ = sum_out.finish()
    whole_in, pair = sum_in.finish()
    reduced = (
        jnp.stack([join_columns(whole_in, 4), join_columns(whole3[: 4 * n], 4)]),
        jnp.stack([whole_out, whole3[4 * n :]]),
        jnp.stack([join_columns(whole1[: 2 * n], 2), join_columns(whole1[3 * n : 5 * n], 2)]),
        jnp.stack([whole1[2 * n : 3 * n], whole1[5 * n :]]),
    )
    sublayer_rms = jnp.sqrt(rows[30, :5] / (rows[30, 5] * frames.shape[2]))
    masters = (ffn_in_master, ffn_out_master, mix_in_master, mix_out_master)
    firsts = (ffn_in_first, ffn_out_first, mix_in_first, mix_out_first)
    seconds = (ffn_in_second, ffn_out_second, mix_in_second, mix_out_second)
    results = [
        adamw(
            masters[slot_index],
            firsts[slot_index],
            seconds[slot_index],
            reduced[slot_index],
            RATE_MATRIX,
            WEIGHT_DECAY,
        )
        for slot_index in range(4)
    ]
    results.append(run_vector_step(rows, pair, vector_master.T, vector_first.T, vector_second.T))
    return (
        activations[None],
        grad0[None],
        results[0][0],
        results[1][0],
        results[2][0],
        results[3][0],
        results[4][0],
        results[0][1],
        results[1][1],
        results[2][1],
        results[3][1],
        results[4][1],
        results[0][2],
        results[1][2],
        results[2][2],
        results[3][2],
        results[4][2],
        results[0][3],
        results[1][3],
        results[2][3],
        results[3][3],
        results[4][3],
        sublayer_rms,
    )


def solution(mesh):
    return jax.shard_map(
        local,
        mesh=mesh,
        in_specs=(
            P(("dp", "fsdp"), None, None),
            P(("dp", "fsdp"), None, None),
            P(("dp", "fsdp")),
            P(None, ("dp", "fsdp"), None),
            P(None, ("dp", "fsdp"), None),
            P(None, ("dp", "fsdp"), None),
            P(None, ("dp", "fsdp"), None),
            P(None, ("dp", "fsdp")),
            P(None, ("dp", "fsdp"), None),
            P(None, ("dp", "fsdp"), None),
            P(None, ("dp", "fsdp"), None),
            P(None, ("dp", "fsdp"), None),
            P(None, ("dp", "fsdp")),
            P(None, ("dp", "fsdp"), None),
            P(None, ("dp", "fsdp"), None),
            P(None, ("dp", "fsdp"), None),
            P(None, ("dp", "fsdp"), None),
            P(None, ("dp", "fsdp")),
        ),
        out_specs=(
            P(("dp", "fsdp"), None, None),
            P(("dp", "fsdp"), None, None),
            P(None, ("dp", "fsdp"), None),
            P(None, ("dp", "fsdp"), None),
            P(None, ("dp", "fsdp"), None),
            P(None, ("dp", "fsdp"), None),
            P(None, ("dp", "fsdp")),
            P(None, ("dp", "fsdp"), None),
            P(None, ("dp", "fsdp"), None),
            P(None, ("dp", "fsdp"), None),
            P(None, ("dp", "fsdp"), None),
            P(None, ("dp", "fsdp")),
            P(None, ("dp", "fsdp"), None),
            P(None, ("dp", "fsdp"), None),
            P(None, ("dp", "fsdp"), None),
            P(None, ("dp", "fsdp"), None),
            P(None, ("dp", "fsdp")),
            P(None, ("dp", "fsdp"), None),
            P(None, ("dp", "fsdp"), None),
            P(None, ("dp", "fsdp"), None),
            P(None, ("dp", "fsdp"), None),
            P(None, ("dp", "fsdp")),
            P(),
        ),
        check_vma=False,
    )
```

```python
import functools

import jax
import jax.numpy as jnp
from jax import lax
from jax.experimental import pallas as pl
from jax.experimental.pallas import tpu as pltpu
from jax.sharding import PartitionSpec as P

HEADS = 8
NSTATE = 32
KERNEL = 15
STEP_NUMBER = 5


NORM_EPS = 1e-05
BETA_FIRST = 0.5
BETA_SECOND = 0.6
ADAM_EPS = 1e-08
RATE_MATRIX = 0.02
RATE_VECTOR = 0.2
WEIGHT_DECAY = 0.01


def adamw(master, first, second, gradient, rate, decay):
    first_new = BETA_FIRST * first + (1.0 - BETA_FIRST) * gradient
    second_new = BETA_SECOND * second + (1.0 - BETA_SECOND) * gradient * gradient
    first_hat = first_new / (1.0 - BETA_FIRST**STEP_NUMBER)
    second_hat = second_new / (1.0 - BETA_SECOND**STEP_NUMBER)
    updated = master - rate * (first_hat / (jnp.sqrt(second_hat) + ADAM_EPS) + decay * master)
    return (updated, first_new, second_new, updated.astype(jnp.bfloat16))


AXES = ("dp", "fsdp")
CORE, Z_HIGH, Z_LOW = 8, 4, 2
STAGES = (Z_HIGH, Z_LOW, (1, 16), (16, 1))


def swap(values, mask):
    masks = mask if isinstance(mask, tuple) else (mask, mask)
    return lax.ppermute(values, AXES, [(i, i ^ masks[(i >> 3) & 1]) for i in range(32)])


def after(values, *earlier):
    return lax.optimization_barrier((values, *earlier))[0] if earlier else values


def add_low(left, right):
    return (left.astype(jnp.float32) + right.astype(jnp.float32)).astype(jnp.bfloat16)


def pack_rows(sums):
    low = lax.reduce_precision(sums, 8, 7)
    rest = jnp.pad(sums[30:31] - low[30:31], ((31, 0), (0, 0)))
    return (low + rest).astype(jnp.bfloat16).reshape(2, 16, 512)


def unpack_rows(message):
    rows = message.astype(jnp.float32).reshape(32, 512)
    return jnp.concatenate([rows[:30], rows[30:31] + rows[31:32], jnp.zeros((1, 512), jnp.float32)])


def cut_columns(matrix):
    rows, columns = matrix.shape
    return matrix.reshape(rows, columns // 512, 512).transpose(1, 0, 2).reshape(-1, 512)


def pieces_of(matrix):
    by_piece = matrix.reshape(32, matrix.shape[0] // 32, -1, 512)
    return jnp.moveaxis(by_piece, 2, 1).reshape(32, -1, 512)


def join_columns(pieces, columns):
    lead = pieces.shape[:-2]
    rows = pieces.shape[-2] // columns
    moved = jnp.moveaxis(pieces.reshape(*lead, columns, rows, 512), -3, -2)
    return moved.reshape(*lead, rows, columns * 512)


def sync(*arrays):
    return lax.optimization_barrier(arrays)


def join(*arrays):
    return jnp.concatenate(arrays)


def shard_of(parts):
    return join(*[cut_columns(part.astype(jnp.bfloat16)).reshape(-1, 16, 512) for part in parts])


def gather_all(first, middle, last, vectors):
    far, near, late, later = STAGES
    own, mid, end = shard_of(first), shard_of(middle), shard_of(last)
    size = own.shape[0]
    vectors = vectors + swap(vectors, CORE)
    got0, got1 = swap(own, far), swap(own, near)
    vectors = vectors + swap(after(vectors, own), far)
    own, mid, end, got0, got1, vectors = sync(own, mid, end, got0, got1, vectors)

    got1_late = swap(join(got0, vectors), near)
    two = join(own, got0)
    got2 = swap(two, late)
    mid_got = swap(mid, far)
    got1_late, two, got2, mid_got, vectors = sync(got1_late, two, got2, mid_got, vectors)

    vectors = vectors + got1_late[size:]
    other_two = join(got1, got1_late[:size], vectors)
    got2_late = swap(other_two, late)
    four = join(two, other_two[:-2])
    got3 = swap(four, later)
    mid = join(mid, mid_got)
    mid_got, end_got = swap(mid, near), swap(after(end, mid_got), far)
    got2_late, got3, mid_got, end_got, other_two = sync(got2_late, got3, mid_got, end_got, other_two)

    vectors = vectors + got2_late[2 * size :]
    other_four = join(got2, got2_late[: 2 * size], vectors)
    got3_late = swap(other_four, later)
    mid = join(mid, mid_got)
    end = join(end, end_got)
    mid_got, end_got = swap(mid, late), swap(end, near)
    far_pieces = [swap(four, CORE), swap(other_four, CORE), swap(got3, CORE)]
    got3_late, mid_got, end_got, vectors = sync(got3_late, mid_got, end_got, vectors)

    vectors = vectors + got3_late[4 * size :]
    far_pieces.append(swap(got3_late, CORE))
    mid = join(mid, mid_got)
    mid_got, mid_far = swap(mid, later), swap(mid, CORE)
    end = join(end, end_got)
    end_got = swap(end, late)
    return (four, other_four, got3, got3_late, *far_pieces), vectors, (mid, mid_got, mid_far), (end, end_got)


def gather_whole(parts):
    gathered = [lax.all_gather(part.astype(jnp.bfloat16), AXES, axis=0, tiled=True) for part in parts]
    pieces = join(*[pieces_of(matrix) for matrix in gathered]) if len(parts) == 1 else jnp.concatenate(
        [pieces_of(matrix) for matrix in gathered], axis=1
    )
    return tuple(pieces.reshape(4, -1, 16, 512))


class Reduce:
    def __init__(self, columns, paired, rows=None, pack=None, unpack=None, stages=STAGES[::-1]):
        self.stages = stages
        self.columns, self.rows, self.pack, self.unpack, self.paired = columns, rows, pack, unpack, paired
        self.parts, self.stage, self.riding = [], 0, rows is not None
        if paired and rows is not None:
            self.more = swap(pack(rows), CORE)

    def add(self, kept, sent):
        self.parts.append((kept, swap(sent, CORE) if self.paired else sent))

    def start(self, *earlier):
        if not self.paired:
            return
        self.stage += 1
        if self.stage == 1:
            parts = [(kept, after(got, *earlier)) for kept, got in self.parts]
            count = 8 * sum(kept.shape[1] for kept, _ in parts)
            sent = jnp.concatenate([add_low(kept[8:], got[8:]) for kept, got in parts], axis=1)
            sent = sent.reshape(-1, 16, 512)
            more = after(self.more, *earlier) if self.riding else None
        else:
            count = self.kept.shape[0] // 2
            got = after(self.got, *earlier)
            sent = add_low(self.kept[count:], got[count : 2 * count])
            more = got[2 * count :]
        if self.riding:
            self.rows = self.rows + self.unpack(more)
        if self.rows is not None:
            sent = jnp.concatenate([sent, self.pack(self.rows)])
            self.riding = True
        new = swap(sent, self.stages[self.stage - 1])
        if self.stage == 1:
            parts = [(after(kept, sent)[:8], after(got, sent)[:8]) for kept, got in parts]
            kept = jnp.concatenate([add_low(kept, got) for kept, got in parts], axis=1)
            self.kept = kept.reshape(-1, 16, 512)
            self.groups = kept.shape[1]
        else:
            self.kept = add_low(after(self.kept, sent)[:count], after(got, sent)[:count])
        self.got, self.sent = new, sent

    def begun(self):
        if not self.paired:
            return ()
        return tuple(self.sent) if isinstance(self.sent, list) else (self.sent,)

    def attach(self, rows):
        if self.paired:
            rows = rows + self.unpack(swap(self.pack(rows), CORE))
            self.late = swap(self.pack(rows), STAGES[3])
        self.rows = rows

    def catch_up(self):
        if self.paired:
            self.got, late = sync(self.got, self.late)
            self.rows = self.rows + self.unpack(late)

    def spread(self, *earlier):
        got = after(self.got, *earlier)
        total = self.kept.astype(jnp.float32) + got[: 4 * self.groups].astype(jnp.float32)
        self.rows = self.rows + self.unpack(got[4 * self.groups :])
        total = total.reshape(4, self.groups, 16, 512)
        riders = self.pack(self.rows)
        self.sent = [jnp.concatenate([total[spot].astype(jnp.bfloat16), riders]) for spot in (2, 1, 3)]
        masks = (Z_LOW, Z_HIGH, Z_LOW | Z_HIGH)
        self.kept, self.got = total[0], [swap(sent, mask) for sent, mask in zip(self.sent, masks)]

    def finish(self, *earlier):
        if not self.paired:
            return self.scatter()
        if isinstance(self.got, list):
            pieces = [got[: self.groups].astype(jnp.float32) for got in self.got]
            total = (self.kept + pieces[0]) + (pieces[1] + pieces[2])
            return total.reshape(-1, 512), (self.rows, *[got[self.groups :] for got in self.got])
        self.got = after(self.got, *earlier)
        total = self.kept.astype(jnp.float32) + self.got[: self.groups].astype(jnp.float32)
        rows = None if self.rows is None else self.rows + self.unpack(self.got[self.groups :])
        return total.reshape(-1, 512), rows

    def scatter(self):
        pieces = jnp.concatenate([jnp.concatenate(part) for part in self.parts], axis=1).reshape(32, -1, 512)
        sums, start = [], 0
        for count, tall in self.columns:
            rows = 16 * count * tall
            matrix = join_columns(pieces[:, start : start + rows], count).reshape(512 * tall, -1)
            matrix = lax.psum_scatter(matrix.astype(jnp.float32), AXES, scatter_dimension=0, tiled=True)
            sums.append(cut_columns(matrix))
            start += rows
        rows = None if self.rows is None else lax.psum(self.rows, AXES)
        if rows is not None and rows.shape[0] == 8:
            rows = (rows, *[jnp.zeros((1, 16, 512), jnp.bfloat16)] * 3)
        return jnp.concatenate(sums), rows


def pack_pair(sums):
    low = lax.reduce_precision(sums[:2], 8, 7)
    parts = [low, sums[:2] - low, jnp.zeros((12, 512), jnp.float32)]
    return jnp.concatenate(parts).astype(jnp.bfloat16)[None]


def unpack_pair(message):
    rows = message[0].astype(jnp.float32)
    return jnp.concatenate([rows[0:2] + rows[2:4], jnp.zeros((6, 512), jnp.float32)])


TILE = 64
F32, LOW = jnp.float32, jnp.bfloat16
NN, NT, TN = ((1,), (0,)), ((1,), (1,)), ((0,), (0,))
VMEM_BYTES = 32 * 1024 * 1024


def mm(left, right, dims=NN):
    return lax.dot_general(left, right, (dims, ((), ())), preferred_element_type=F32)


def tiles(rows=512, step=TILE):
    return [pl.ds(start, step) for start in range(0, rows, step)]


def sigmoid(values):
    return 0.5 * jnp.tanh(0.5 * values) + 0.5


def standardize(values):
    centered = values - jnp.mean(values, axis=-1, keepdims=True)
    variance = jnp.mean(centered * centered, axis=-1, keepdims=True)
    spread = lax.rsqrt(variance + NORM_EPS)
    return centered * spread, spread


def standardize_back(grad, unit, spread):
    mean_grad = jnp.mean(grad, axis=-1, keepdims=True)
    mean_both = jnp.mean(grad * unit, axis=-1, keepdims=True)
    return spread * (grad - mean_grad - unit * mean_both)


def row(values):
    return jnp.sum(values, axis=0, keepdims=True)


def square(pieces):
    return pieces.reshape(512, 512)


class Place:
    def __init__(self, paired, order=0):
        self.paired, self.order = paired, order
        if paired:
            self.dp, self.fsdp = lax.axis_index("dp"), lax.axis_index("fsdp")
            self.core = self.dp & 1

    def device(self, spot):
        if not self.paired:
            return spot
        side, bits = spot // 16, [(spot >> place) & 1 for place in range(4)]
        first, second = 2 * bits[3] + side, bits[2]
        turned_first, turned_second = 2 * bits[2] + side, bits[3]
        around = 2 * bits[1] + 4 * bits[0]
        straight = self.core == side
        dp = self.dp ^ jnp.where(straight, first, turned_first)
        return 8 * dp + (self.fsdp ^ jnp.where(straight, second + around, turned_second + around))

    def piece(self, spot):
        if self.paired and self.order == 1:
            spot = (spot & 24) + 4 * (spot & 1) + ((spot >> 1) & 3)
        if self.paired and self.order == 2:
            spot = (spot & 25) + 2 * (spot & 2) + ((spot & 4) >> 1)
        return self.device(spot)

    def chunk(self, step):
        return self.dp ^ (0, 2, 1, 3)[step] if self.paired else step

    def spot(self, step, f):
        if not self.paired:
            return 8 * (step % 2) + f
        rel = self.fsdp ^ f
        low, z_near, z_far = ((4, 2, 1), (1, 4, 2), (2, 4, 1))[self.order]
        y_bit, z_spot = rel & 1, z_near * ((rel >> 1) & 1) + z_far * ((rel >> 2) & 1)
        straight = self.core == step // 2
        return z_spot + jnp.where(straight, 8 * (step % 2) + low * y_bit, 8 * y_bit + low * (step % 2))


def place_ffn(table, sources, w_in, w_out):
    each_has = 32 // len(sources)
    for side, source in enumerate(sources):
        for spot in range(each_has):
            device = table.device(each_has * side + spot)
            w_in[:, device] = source[pl.ds(8 * spot, 4)]
            w_out[pl.ds(4 * device, 4)] = source[pl.ds(8 * spot + 4, 4)]


def place_mix(table, sources, first, weights):
    each_has = 32 // len(sources)
    for side, source in enumerate(sources):
        for spot in range(each_has):
            weights[:, table.device(each_has * side + spot)] = source[pl.ds(6 * spot + first, 3)]


def start_all(copies):
    for copy in copies:
        copy.start()


def wait_all(copies):
    for copy in copies:
        copy.wait()


def fill_normed(h_ref, vec_ref, index, normed):
    gain = vec_ref[pl.ds(2 * index, 1)].astype(F32)
    shift = vec_ref[pl.ds(2 * index + 1, 1)].astype(F32)
    for part in tiles():
        unit, _ = standardize(h_ref[part].astype(F32))
        normed[part] = (unit * gain + shift).astype(LOW)


def order_rows(table, natural, ordered):
    for spot in range(32):
        ordered[spot] = natural[table.piece(spot)]


def fill_transposed(source, natural):
    for part in tiles(step=128):
        turned = source[part].astype(F32).T.astype(LOW)
        natural[:, :, part] = turned.reshape(32, 16, 128)


def norm_back(h_ref, vec_ref, index, grad_normed, grad_in, grad_out):
    gain = vec_ref[pl.ds(2 * index, 1)].astype(F32)
    grad_gain, grad_shift = jnp.zeros((1, 512), F32), jnp.zeros((1, 512), F32)
    for part in tiles():
        unit, spread = standardize(h_ref[part].astype(F32))
        grad = grad_normed[part]
        grad_gain = grad_gain + row(grad * unit)
        grad_shift = grad_shift + row(grad)
        grad_out[part] = grad_in[part] + standardize_back(grad * gain, unit, spread)
    return grad_gain, grad_shift


def valid_rows(length, part):
    places = part.start + lax.broadcasted_iota(jnp.int32, (part.size, 1), 0)
    return (places < length).astype(F32)


def valid_lanes(length):
    return (lax.broadcasted_iota(jnp.int32, (1, 512), 1) < length).astype(F32)


def ffn_forward(length, h_ref, normed, w_in, w_out, pre, act, out, new_h, save):
    pre[0] = mm(normed[...], square(w_in[0]))
    for j in range(4):
        pre_j, act_j = pre.at[j], act(j)
        if j < 3:
            pre[j + 1] = mm(normed[...], square(w_in[j + 1]))
        for part in tiles():
            values = pre_j[part]
            act_j[part] = (values * sigmoid(values)).astype(LOW)
        save(j)
        more = mm(act_j[...], square(w_out[pl.ds(32 * j, 32)]))
        out[...] = more if j == 0 else out[...] + more
    total = jnp.zeros((1, 512), F32)
    for part in tiles():
        half = 0.5 * out[part]
        new_h[part] = h_ref[part].astype(F32) + half
        total = total + row(valid_rows(length, part) * half * half)
    return total


def place_out_grads(table, step, first, kept, sent, act, grad_low):
    products = mm(act, grad_low, TN).astype(LOW).reshape(8, 4, 16, 512)
    for f in range(8):
        (kept, sent)[step // 2][table.spot(step, f), pl.ds(first, 4)] = products[f]


def place_rows(kept, sent, group, products):
    pieces = products.astype(LOW).reshape(32, 16, 512)
    kept[:, group] = pieces[:16]
    sent[:, group] = pieces[16:]


def ffn_backward(table, w_out, pre, grad_low, turned, act, grad_pre, kept, sent):
    def first_product(step):
        return mm(grad_low[...], square(w_out[pl.ds(32 * table.chunk(step), 32)]), NT)

    following = first_product(0)
    for step in range(4):
        chunk = table.chunk(step)
        pre_j = pre.at[chunk]
        grad_act = following
        if step < 3:
            following = first_product(step + 1)
        for part in tiles():
            values = pre_j[part]
            gate = sigmoid(values)
            lifted = values * gate
            if act is not None:
                act[part] = lifted.astype(LOW)
            slope = gate + lifted * (1.0 - gate)
            grad_pre[chunk, part] = (grad_act[part.start : part.start + part.size] * slope).astype(LOW)
        place_rows(kept, sent, chunk, mm(square(turned[...]), grad_pre[chunk]))
        if act is not None:
            place_out_grads(table, step, 4, kept, sent, act[...], grad_low[...])


def first_kernel(paired, length, h_ref, vec_ref, *refs):
    table = Place(paired)
    *pieces, h1_ref, pre_hbm, act_hbm, stat_ref, in_hbm, out_hbm = refs[:-9]
    w_in, w_out, normed, act, out, pre, pre_sem, act_sem, w_sem = refs[-9:]
    place_ffn(table, pieces, w_in, w_out)
    weights = [
        pltpu.make_async_copy(w_in, in_hbm, w_sem.at[0]),
        pltpu.make_async_copy(w_out, out_hbm, w_sem.at[1]),
    ]
    start_all(weights)
    fill_normed(h_ref, vec_ref, 0, normed)

    copies = [
        (
            pltpu.make_async_copy(pre.at[j], pre_hbm.at[j], pre_sem.at[j]),
            pltpu.make_async_copy(act.at[j], act_hbm.at[j], act_sem.at[j]),
        )
        for j in range(4)
    ]

    def save(j):
        start_all(copies[j])

    stat_ref[...] = ffn_forward(
        length[0], h_ref, normed, w_in, w_out, pre, lambda j: act.at[j], out, h1_ref, save
    )
    for j in range(4):
        wait_all(copies[j])
    wait_all(weights)


def last_kernel(
    paired, length, h_ref, vec_ref, cot_ref, held, got, held_far, got_far,
    top_ref, grad_ref, rows_ref, kept, sent, w_in, grad_pre,
    w_out, normed, act, out, pre, low, natural, turned
):
    table = Place(paired, 1)
    place_ffn(table, (held, got, held_far, got_far), w_in, w_out)
    fill_normed(h_ref, vec_ref, 4, normed)
    fill_transposed(normed, natural)
    order_rows(table, natural, turned)
    stat4 = ffn_forward(length[0], h_ref, normed, w_in, w_out, pre, lambda j: act, out, grad_ref, lambda j: None)
    gain, shift = vec_ref[pl.ds(10, 1)].astype(F32), vec_ref[pl.ds(11, 1)].astype(F32)
    grad_gain, grad_shift = jnp.zeros((1, 512), F32), jnp.zeros((1, 512), F32)
    stat5 = jnp.zeros((1, 512), F32)
    for part in tiles():
        values = grad_ref[part]
        stat5 = stat5 + row(valid_rows(length[0], part) * values * values)
        unit, spread = standardize(values)
        top_ref[part] = unit * gain + shift
        grad = cot_ref[part].astype(F32)
        grad_gain = grad_gain + row(grad * unit)
        grad_shift = grad_shift + row(grad)
        back = standardize_back(grad * gain, unit, spread)
        grad_ref[part] = back
        low[part] = (0.5 * back).astype(LOW)
    ffn_backward(table, w_out, pre, low, turned, act, grad_pre, kept, sent)
    rows_ref[...] = jnp.concatenate([grad_gain, grad_shift, stat4, stat5, jnp.zeros((4, 512), F32)])


def back_out_kernel(paired, grad_in, act, kept, sent, low):
    table = Place(paired)
    for part in tiles():
        low[part] = (0.5 * grad_in[part]).astype(LOW)
    for step in range(4):
        place_out_grads(table, step, 0, kept, sent, act[table.chunk(step)], low[...])


def back_in_kernel(
    paired, h_ref, vec_ref, grad_in, w_out, pre, kept, sent, grad_pre, normed, low, natural, turned
):
    table = Place(paired)
    fill_normed(h_ref, vec_ref, 0, normed)
    fill_transposed(normed, natural)
    order_rows(table, natural, turned)
    for part in tiles():
        low[part] = (0.5 * grad_in[part]).astype(LOW)
    ffn_backward(table, w_out, pre, low, turned, None, grad_pre, kept, sent)


def ffn_grad_kernel(index, h_ref, vec_ref, grad_in, w_in, grad_pre, grad_ref, rows_ref, out):
    for j in range(4):
        more = mm(grad_pre[j], square(w_in[j]), NT)
        out[...] = more if j == 0 else out[...] + more
    gain, shift = norm_back(h_ref, vec_ref, index, out, grad_in, grad_ref)
    rows_ref[...] = jnp.concatenate([gain, shift, jnp.zeros((6, 512), F32)])


def vector_step_kernel(
    width, rows_ref, pair_ref, got0, got1, got2, master, first, second, new_ref, first_ref, second_ref, copy_ref
):
    pair = pair_ref[0:2]
    for got in (got0, got1, got2):
        message = got[0].astype(F32)
        pair = pair + (message[0:2] + message[2:4])
    rows = jnp.concatenate([pair, rows_ref[2:32]])
    me = lax.axis_index("dp") * lax.axis_size("fsdp") + lax.axis_index("fsdp")
    turned = pltpu.roll(rows, lax.rem(512 - width * me, 512), 1)[:, 0:128].T
    results = adamw(master[...], first[...], second[...], turned[0:width, 0:30], RATE_VECTOR, 0.0)
    for ref, values in zip((new_ref, first_ref, second_ref, copy_ref), results):
        ref[...] = values


def vector_columns(vec_ref, pad):
    pad[...] = jnp.zeros((128, 512), F32)
    pad[pl.ds(0, 32)] = vec_ref[...].astype(F32)
    return pad[...].T


def ssm_decays(columns):
    rates = jnp.exp(columns[0:256, 13:14])
    lags = lax.broadcasted_iota(jnp.int32, (1, 512), 1).astype(F32)
    return jnp.exp(-rates * lags), rates, columns[256:512, 13:14]


def head_matrix(kernels, head):
    line = jnp.concatenate([kernels[head : head + 1], jnp.zeros((1, 128), F32)], axis=1)
    skewed = pltpu.roll(jnp.broadcast_to(line, (128, 640)), 0, 1, stride=1, stride_axis=0)
    return skewed[:, :512].astype(LOW)


def blocks_of(rows):
    return jnp.concatenate([rows[:, 128 * b : 128 * (b + 1)] for b in range(4)], axis=0)


def ssm_kernel(
    paired, length, h_ref, vec_ref, held, got, held_far, got_far, h2_ref, saved_hbm, stat_ref, weights_hbm,
    weights, normed, act, saved, pad, save_sem, w_sem
):
    table = Place(paired)
    place_mix(table, (held, got, held_far, got_far), 0, weights)
    hand_on = pltpu.make_async_copy(weights, weights_hbm, w_sem)
    hand_on.start()
    fill_normed(h_ref, vec_ref, 1, normed)
    columns = vector_columns(vec_ref, pad)
    decays, _, coefs = ssm_decays(columns)
    kernels = jnp.sum((coefs * decays).reshape(8, 32, 512), axis=1)
    mask = valid_lanes(length[0])
    signal, gate, mixed = saved.at[0], saved.at[1], saved.at[2]
    signal[...] = mm(square(weights[0]), normed[...], ((0,), (1,))) * mask
    gate[...] = mm(square(weights[1]), normed[...], ((0,), (1,)))
    copies = [pltpu.make_async_copy(saved.at[k], saved_hbm.at[k], save_sem.at[k]) for k in range(3)]
    copies[0].start()
    copies[1].start()
    for head in range(8):
        part = pl.ds(64 * head, 64)
        rows = signal[part]
        spread = mm(blocks_of(rows).astype(LOW), head_matrix(kernels, head))
        skip = columns[64 * head : 64 * head + 64, 12:13]
        for a in range(4):
            lanes = pl.ds(128 * a, 128)
            total = skip * rows[:, 128 * a : 128 * a + 128]
            for b in range(a + 1):
                total = total + spread[64 * b : 64 * b + 64, 128 * (a - b) : 128 * (a - b) + 128]
            mixed[part, lanes] = total
            gates = gate[part, lanes]
            act[part, lanes] = (total * gates * sigmoid(gates)).astype(LOW)
    copies[2].start()
    out = mm(act[...], square(weights[2]), TN)
    total = jnp.zeros((1, 512), F32)
    for part in tiles():
        values = out[part.start : part.start + part.size]
        h2_ref[part] = h_ref[part] + values
        total = total + row(valid_rows(length[0], part) * values * values)
    stat_ref[...] = total
    wait_all(copies)
    hand_on.wait()


def ssm_back_kernel(
    paired, length, h_ref, vec_ref, grad_in, weights, saved, stat1, stat2, rows2, rows3, rows4,
    grad_ref, rows_ref, kept, sent,
    normed, low, natural, turned, act, act_turned, grad_pre, out, pad, kernel_grads, skip_grads
):
    table = Place(paired, 2)
    fill_normed(h_ref, vec_ref, 1, normed)
    fill_transposed(normed, natural)
    order_rows(table, natural, turned)
    for part in tiles():
        low[part] = grad_in[part].astype(LOW)
    columns = vector_columns(vec_ref, pad)
    decays, rates, coefs = ssm_decays(columns)
    kernels = jnp.sum((coefs * decays).reshape(8, 32, 512), axis=1)
    mask = valid_lanes(length[0])
    signal, gate, mixed = saved.at[0], saved.at[1], saved.at[2]
    out[...] = mm(square(weights[2]), low[...], NT)
    flipped = lax.broadcasted_iota(jnp.int32, (128, 128), 0) + lax.broadcasted_iota(jnp.int32, (128, 128), 1)
    flip = (flipped == 127).astype(F32).astype(LOW)
    for head in range(8):
        part = pl.ds(64 * head, 64)
        rows, gates, mixes, grad_act = signal[part], gate[part], mixed[part], out[part]
        gating = sigmoid(gates)
        lifted = gates * gating
        act[pl.ds(4 * head, 4)] = (mixes * lifted).astype(LOW).reshape(4, 16, 512)
        grad_mixed = grad_act * lifted
        grad_pre[1, part] = (grad_act * mixes * (gating + lifted * (1.0 - gating))).astype(LOW)
        grad_low = grad_mixed.astype(LOW)
        shifted = jnp.concatenate(
            [grad_low]
            + [
                jnp.concatenate([grad_low[:, 128 * b :], jnp.zeros((64, 128 * b), LOW)], axis=1)
                for b in (1, 2, 3)
            ],
            axis=0,
        )
        back = mm(shifted, head_matrix(kernels, head), NT)
        mirrored = mm(blocks_of(rows).astype(LOW), flip).astype(LOW)
        lag_sums = mm(mirrored, shifted, TN)
        lag_sums = jnp.concatenate([lag_sums, jnp.zeros((128, 128), F32)], axis=1)
        lag_sums = row(pltpu.roll(lag_sums, 0, 1, stride=1, stride_axis=0))
        kernel_grads[pl.ds(head, 1)] = pltpu.roll(lag_sums, 640 - 127, 1)[:, :512]
        skip = columns[64 * head : 64 * head + 64, 12:13]
        pad_lane = jnp.sum(grad_mixed * rows, axis=1, keepdims=True)
        natural_grad = jnp.concatenate([back[64 * b : 64 * b + 64] for b in range(4)], axis=1)
        grad_pre[0, part] = ((natural_grad + skip * grad_mixed) * mask).astype(LOW)
        normed_f = jnp.broadcast_to(pad_lane, (64, 128))
        skip_grads[part] = normed_f
    order_rows(table, act, act_turned)
    place_rows(kept, sent, 2, mm(square(act_turned[...]), low[...]))
    for q in range(2):
        more = mm(grad_pre[q], square(weights[q]), ((0,), (1,)))
        out[...] = more if q == 0 else out[...] + more
        place_rows(kept, sent, q, mm(square(turned[...]), grad_pre[q], NT))
    gain1, shift1 = norm_back(h_ref, vec_ref, 1, out, grad_in, grad_ref)
    lag_grads = jnp.broadcast_to(kernel_grads[...].reshape(8, 1, 512), (8, 32, 512)).reshape(256, 512)
    lags = lax.broadcasted_iota(jnp.int32, (1, 512), 1).astype(F32)
    weighed = lag_grads * decays
    coef_grads = jnp.sum(weighed, axis=1, keepdims=True)
    rate_grads = -rates * coefs * jnp.sum(weighed * lags, axis=1, keepdims=True)
    lanes = lax.broadcasted_iota(jnp.int32, (1, 128), 1)
    ssm_column = jnp.concatenate([rate_grads, coef_grads], axis=0)
    both = jnp.where(lanes == 0, skip_grads[...], 0.0) + jnp.where(lanes == 1, ssm_column, 0.0)
    turned_rows = both.T
    lanes = lax.broadcasted_iota(jnp.int32, (1, 512), 1)
    stats = jnp.where(lanes == 5, length[0].astype(F32), 0.0)
    for place, sums in enumerate([stat1[...], stat2[...], rows2[20:21], rows3[2:3], rows3[3:4]]):
        stats = stats + jnp.where(lanes == place, jnp.sum(sums, axis=1, keepdims=True), 0.0)
    nothing = jnp.zeros((2, 512), F32)
    rows_ref[...] = jnp.concatenate(
        [nothing, gain1, shift1, rows2[0:4], rows4[0:2], rows3[0:2], turned_rows[0:2], rows2[4:20], stats, nothing[0:1]]
    )


PAD = 16


def conv_kernel(
    paired, length, h_ref, vec_ref, held, got, held_far, got_far, h3_ref, saved_hbm, stat_ref, weights_hbm,
    weights, normed, act, saved, padded, save_sem, w_sem
):
    table = Place(paired)
    place_mix(table, (held, got, held_far, got_far), 3, weights)
    hand_on = pltpu.make_async_copy(weights, weights_hbm, w_sem)
    hand_on.start()
    fill_normed(h_ref, vec_ref, 2, normed)
    copies = [pltpu.make_async_copy(saved.at[k], saved_hbm.at[k], save_sem.at[k]) for k in range(3)]
    for q in range(2):
        saved[q] = mm(normed[...], square(weights[q]))
        copies[q].start()
    for c in range(4):
        padded[c, pl.ds(0, PAD)] = jnp.zeros((PAD, 128), F32)
        padded[c, pl.ds(PAD + 512, PAD)] = jnp.zeros((PAD, 128), F32)
        lanes = pl.ds(128 * c, 128)
        for part in tiles():
            glu = saved[0, part, lanes] * sigmoid(saved[1, part, lanes]) * valid_rows(length[0], part)
            padded[c, pl.ds(PAD + part.start, part.size)] = glu
        taps = [vec_ref[pl.ds(14 + j, 1), lanes].astype(F32) for j in range(KERNEL + 1)]
        for part in tiles():
            total = jnp.broadcast_to(taps[KERNEL], (part.size, 128))
            for j in range(KERNEL):
                total = total + padded[c, pl.ds(PAD + part.start + j - 7, part.size)] * taps[j]
            saved[2, part, lanes] = total
    copies[2].start()
    gain, shift = vec_ref[pl.ds(6, 1)].astype(F32), vec_ref[pl.ds(7, 1)].astype(F32)
    for part in tiles():
        unit, _ = standardize(saved[2, part])
        values = unit * gain + shift
        act[part] = (values * sigmoid(values)).astype(LOW)
    out = mm(act[...], square(weights[2]))
    total = jnp.zeros((1, 512), F32)
    for part in tiles():
        values = out[part.start : part.start + part.size]
        h3_ref[part] = h_ref[part] + values
        total = total + row(valid_rows(length[0], part) * values * values)
    stat_ref[...] = total
    wait_all(copies)
    hand_on.wait()


def conv_back_kernel(
    paired, length, h_ref, vec_ref, grad_in, weights, saved, stat_in,
    grad_ref, rows_ref, kept, sent,
    normed, low, natural, turned, act, act_turned, grad_pre, out, padded, padded_grad
):
    table = Place(paired, 2)
    fill_normed(h_ref, vec_ref, 2, normed)
    fill_transposed(normed, natural)
    order_rows(table, natural, turned)
    for part in tiles():
        low[part] = grad_in[part].astype(LOW)
    out[...] = mm(low[...], square(weights[2]), NT)
    gain, shift = vec_ref[pl.ds(6, 1)].astype(F32), vec_ref[pl.ds(7, 1)].astype(F32)
    gain3, shift3, bias = (jnp.zeros((1, 512), F32) for _ in range(3))
    for part in tiles():
        unit, spread = standardize(saved[2, part])
        values = unit * gain + shift
        gating = sigmoid(values)
        lifted = values * gating
        normed[part] = lifted.astype(LOW)
        grad = out[part] * (gating + lifted * (1.0 - gating))
        gain3 = gain3 + row(grad * unit)
        shift3 = shift3 + row(grad)
        back = standardize_back(grad * gain, unit, spread)
        bias = bias + row(back)
        for c in range(4):
            padded_grad[c, pl.ds(PAD + part.start, part.size)] = back[:, 128 * c : 128 * c + 128]
    fill_transposed(normed, act)
    order_rows(table, act, act_turned)
    place_rows(kept, sent, 2, mm(square(act_turned[...]), low[...]))
    tap_rows = []
    for c in range(4):
        lanes = pl.ds(128 * c, 128)
        for ref in (padded, padded_grad):
            ref[c, pl.ds(0, PAD)] = jnp.zeros((PAD, 128), F32)
            ref[c, pl.ds(PAD + 512, PAD)] = jnp.zeros((PAD, 128), F32)
        for part in tiles():
            glu = saved[0, part, lanes] * sigmoid(saved[1, part, lanes]) * valid_rows(length[0], part)
            padded[c, pl.ds(PAD + part.start, part.size)] = glu
        taps = [vec_ref[pl.ds(14 + j, 1), lanes].astype(F32) for j in range(KERNEL)]
        sums = [jnp.zeros((8, 128), F32) for _ in range(KERNEL)]
        for part in tiles():
            total = jnp.zeros((part.size, 128), F32)
            grad = padded_grad[c, pl.ds(PAD + part.start, part.size)]
            for j in range(KERNEL):
                total = total + padded_grad[c, pl.ds(PAD + part.start + 7 - j, part.size)] * taps[j]
                seen = padded[c, pl.ds(PAD + part.start + j - 7, part.size)]
                sums[j] = sums[j] + jnp.sum((grad * seen).reshape(part.size // 8, 8, 128), axis=0)
            total = total * valid_rows(length[0], part)
            gating = sigmoid(saved[1, part, lanes])
            first = total * gating
            grad_pre[0, part, lanes] = first.astype(LOW)
            grad_pre[1, part, lanes] = (first * saved[0, part, lanes] * (1.0 - gating)).astype(LOW)
        tap_rows.append(jnp.concatenate([row(values) for values in sums], axis=0))
    for q in range(2):
        more = mm(grad_pre[q], square(weights[q]), NT)
        out[...] = more if q == 0 else out[...] + more
        place_rows(kept, sent, q, mm(square(turned[...]), grad_pre[q]))
    gain2, shift2 = norm_back(h_ref, vec_ref, 2, out, grad_in, grad_ref)
    rows_ref[...] = jnp.concatenate(
        [gain2, shift2, gain3, shift3, jnp.concatenate(tap_rows, axis=1), bias, stat_in[...], jnp.zeros((3, 512), F32)]
    )


def call(kernel, scalars, arrays, outs, scratch, flops):
    in_vmem, in_hbm = pl.BlockSpec(memory_space=pltpu.VMEM), pl.BlockSpec(memory_space=pltpu.HBM)
    return pl.pallas_call(
        kernel,
        out_shape=[
            (pltpu.HBM if apart else jax.ShapeDtypeStruct)(shape, dtype) for shape, dtype, apart in outs
        ],
        in_specs=[pl.BlockSpec(memory_space=pltpu.SMEM)] * len(scalars) + [in_vmem] * len(arrays),
        out_specs=[in_hbm if apart else in_vmem for _, _, apart in outs],
        scratch_shapes=scratch,
        compiler_params=pltpu.CompilerParams(vmem_limit_bytes=VMEM_BYTES),
        cost_estimate=pl.CostEstimate(flops=10 * flops, bytes_accessed=10 << 20, transcendentals=0),
    )(*scalars, *arrays)


SQUARE, PIECES = (512, 512), (32, 16, 512)
DMA = pltpu.SemaphoreType.DMA
IN_FFN, OUT_FFN, MIX = (4, 32, 16, 512), (128, 16, 512), (3, 32, 16, 512)
SMALL, LARGE = 512 * 512 * 512 * 2, 512 * 512 * 2048 * 2


def low_scratch(*shapes):
    return [pltpu.VMEM(shape, LOW) for shape in shapes]


def full_scratch(*shapes):
    return [pltpu.VMEM(shape, F32) for shape in shapes]


def grads_of(groups):
    return [((16, groups, 16, 512), LOW, False)] * 2


def run_first(paired, length, h, vectors, pieces):
    return call(
        functools.partial(first_kernel, paired),
        [length],
        [h, vectors, *pieces],
        [(SQUARE, F32, False), ((4, 512, 512), F32, True), ((4, 512, 512), LOW, True), ((1, 512), F32, False)]
        + [(IN_FFN, LOW, True), (OUT_FFN, LOW, True)],
        low_scratch(IN_FFN, OUT_FFN, SQUARE, (4, 512, 512))
        + full_scratch(SQUARE, (4, 512, 512))
        + [DMA((4,)), DMA((4,)), DMA((2,))],
        2 * LARGE,
    )


def run_last(paired, length, h, vectors, cotangent, pieces):
    return call(
        functools.partial(last_kernel, paired),
        [length],
        [h, vectors, cotangent, *pieces],
        [(SQUARE, F32, False), (SQUARE, F32, False), ((8, 512), F32, False), *grads_of(8)]
        + [(IN_FFN, LOW, False), ((4, 512, 512), LOW, False)],
        low_scratch(OUT_FFN, SQUARE, SQUARE)
        + full_scratch(SQUARE, (4, 512, 512))
        + low_scratch(SQUARE, PIECES, PIECES),
        6 * LARGE,
    )


def run_back_out(paired, grad, act):
    return call(functools.partial(back_out_kernel, paired), [], [grad, act], grads_of(4), low_scratch(SQUARE), LARGE)


def run_back_in(paired, h, vectors, grad, w_out, pre):
    return call(
        functools.partial(back_in_kernel, paired),
        [],
        [h, vectors, grad, w_out, pre],
        [*grads_of(4), ((4, 512, 512), LOW, False)],
        low_scratch(SQUARE, SQUARE, PIECES, PIECES),
        2 * LARGE,
    )


def run_ffn_grad(index, h, vectors, grad, w_in, grad_pre):
    return call(
        functools.partial(ffn_grad_kernel, index),
        [],
        [h, vectors, grad, w_in, grad_pre],
        [(SQUARE, F32, False), ((8, 512), F32, False)],
        full_scratch(SQUARE),
        LARGE,
    )


def run_vector_step(rows, pair, master, first, second):
    shape = master.shape
    results = call(
        functools.partial(vector_step_kernel, shape[0]),
        [],
        [rows, *pair, master, first, second],
        [(shape, F32, False)] * 3 + [(shape, LOW, False)],
        [],
        SMALL // 40,
    )
    return tuple(part.T for part in results)


def run_mix(kernel, paired, length, h, vectors, pieces, last_scratch):
    return call(
        functools.partial(kernel, paired),
        [length],
        [h, vectors, *pieces],
        [(SQUARE, F32, False), ((3, 512, 512), F32, True), ((1, 512), F32, False), (MIX, LOW, True)],
        low_scratch(MIX, SQUARE, SQUARE) + full_scratch((3, 512, 512), last_scratch) + [DMA((3,)), DMA],
        4 * SMALL,
    )


def run_mix_back(kernel, paired, length, h, vectors, grad, weights, saved, more, rows, last_scratch):
    return call(
        functools.partial(kernel, paired),
        [length],
        [h, vectors, grad, *weights, saved, *more],
        [(SQUARE, F32, False), ((rows, 512), F32, False), *grads_of(3)],
        low_scratch(SQUARE, SQUARE, PIECES, PIECES, PIECES, PIECES, (2, 512, 512))
        + full_scratch(SQUARE, *last_scratch),
        8 * SMALL,
    )


def local(
    frames,
    cotangent,
    seq_lengths,
    ffn_in_master,
    ffn_out_master,
    mix_in_master,
    mix_out_master,
    vector_master,
    ffn_in_first,
    ffn_out_first,
    mix_in_first,
    mix_out_first,
    vector_first,
    ffn_in_second,
    ffn_out_second,
    mix_in_second,
    mix_out_second,
    vector_second,
):
    me = lax.axis_index(AXES)
    paired = (lax.axis_size("dp"), lax.axis_size("fsdp")) == (4, 8)
    low = jnp.bfloat16
    width, n = vector_master.shape[1], ffn_in_master.shape[1]
    placed = lax.dynamic_update_slice(
        jnp.zeros((32, 512), low), vector_master.astype(low), (0, width * me)
    ).reshape(2, 16, 512)
    first = [ffn_in_master[0], ffn_out_master[0]]
    middle = [mix_in_master[0], mix_out_master[0], mix_in_master[1], mix_out_master[1]]
    last = [ffn_in_master[1], ffn_out_master[1]]
    h0, length = frames[0], seq_lengths
    if paired:
        first, vectors, (mid, mid_got, mid_far), (end, end_got) = gather_all(first, middle, last, placed)
    else:
        first, middle, last = gather_whole(first), gather_whole(middle), gather_whole(last)
        vectors = lax.psum(placed, AXES)
    vectors = vectors.reshape(32, 512)
    h1, pre0, act0, stat1, *weights0 = run_first(paired, length, h0, vectors, first)
    if paired:
        mid_got, end_got, stat1 = sync(mid_got, end_got, stat1)
        end = join(end, end_got)
        end_got, end_far = swap(end, STAGES[3]), swap(end, CORE)
        middle = (mid, mid_got, mid_far, swap(mid_got, CORE))
    h2, saved1, stat2, *weights1 = run_mix(ssm_kernel, paired, length, h1, vectors, middle, (128, 512))
    h3, saved2, stat3, *weights2 = run_mix(
        conv_kernel, paired, length, h2, vectors, middle, (4, 512 + 2 * PAD, 128)
    )
    if paired:
        end_got, stat3 = sync(end_got, stat3)
        last = (end, end_got, end_far, swap(end_got, CORE))
    activations, grad4, rows3, kept3, sent3, w_in3, grad_pre3 = run_last(
        paired, length, h3, vectors, cotangent[0], last
    )
    sum3 = Reduce(((4, 1), (1, 4)), paired, stages=(STAGES[3], Z_LOW, Z_HIGH, STAGES[2]))
    sum3.add(kept3, sent3)
    grad3, rows4 = run_ffn_grad(4, h3, vectors, grad4, w_in3, grad_pre3)
    sum3.start(rows4)
    grad2, rows2, kept2, sent2 = run_mix_back(
        conv_back_kernel, paired, length, h2, vectors, after(grad3, *sum3.begun()), weights2, saved2, [stat3], 24,
        [(4, 512 + 2 * PAD, 128)] * 2,
    )
    grad1, rows, kept1, sent1 = run_mix_back(
        ssm_back_kernel, paired, length, h1, vectors, grad2, weights1, saved1,
        [stat1, stat2, rows2, rows3, rows4], 32, [(128, 512), (8, 512), (512, 128)],
    )
    sum1 = Reduce(
        ((2, 1), (1, 1)) * 2, paired, rows, pack_rows, unpack_rows, (STAGES[3], Z_LOW, STAGES[2], Z_HIGH)
    )
    sum1.add(kept1, sent1)
    sum1.add(kept2, sent2)
    sum3.start(rows)
    kept_out, sent_out = run_back_out(paired, after(grad1, *sum3.begun()), act0)
    sum_out = Reduce(((1, 4),), paired)
    sum_out.add(kept_out, sent_out)
    sum1.start(kept_out)
    grad1 = after(grad1, *sum1.begun())
    kept_in, sent_in, grad_pre0 = run_back_in(paired, h0, vectors, grad1, weights0[1], pre0)
    sum_in = Reduce(((4, 1),), paired, None, pack_pair, unpack_pair)
    sum_in.add(kept_in, sent_in)
    sum_out.start(kept_in)
    sum_in.start(*sum_out.begun())
    grad0, pair = run_ffn_grad(
        0, h0, vectors, after(grad1, *sum_in.begun()), weights0[0], grad_pre0
    )
    sum1.start(pair)
    sum3.start(pair)
    sum_in.attach(pair)
    sum_out.start(*sum1.begun())
    sum_in.catch_up()
    sum_in.start(*sum_out.begun())
    sum1.start(*sum_in.begun())
    sum3.start(*sum1.begun())
    sum_out.start(*sum3.begun())
    if paired:
        sum_in.spread(*sum_out.begun())
        sum_in.kept, sum1.got, sum_out.got = sync(sum_in.kept, sum1.got, sum_out.got)
    sum1.start(*sum_in.begun())
    sum_out.start(*sum1.begun())
    if paired:
        sum_out.kept, sum1.kept, *sum_in.got = sync(sum_out.kept, sum1.kept, *sum_in.got)
    whole3, _ = sum3.finish(*sum_out.begun())
    whole1, rows = sum1.finish(*sum_out.begun())
    whole_out, _ = sum_out.finish()
    whole_in, pair = sum_in.finish()
    reduced = (
        jnp.stack([join_columns(whole_in, 4), join_columns(whole3[: 4 * n], 4)]),
        jnp.stack([whole_out, whole3[4 * n :]]),
        jnp.stack([join_columns(whole1[: 2 * n], 2), join_columns(whole1[3 * n : 5 * n], 2)]),
        jnp.stack([whole1[2 * n : 3 * n], whole1[5 * n :]]),
    )
    sublayer_rms = jnp.sqrt(rows[30, :5] / (rows[30, 5] * frames.shape[2]))
    masters = (ffn_in_master, ffn_out_master, mix_in_master, mix_out_master)
    firsts = (ffn_in_first, ffn_out_first, mix_in_first, mix_out_first)
    seconds = (ffn_in_second, ffn_out_second, mix_in_second, mix_out_second)
    results = [
        adamw(
            masters[slot_index],
            firsts[slot_index],
            seconds[slot_index],
            reduced[slot_index],
            RATE_MATRIX,
            WEIGHT_DECAY,
        )
        for slot_index in range(4)
    ]
    results.append(run_vector_step(rows, pair, vector_master.T, vector_first.T, vector_second.T))
    return (
        activations[None],
        grad0[None],
        results[0][0],
        results[1][0],
        results[2][0],
        results[3][0],
        results[4][0],
        results[0][1],
        results[1][1],
        results[2][1],
        results[3][1],
        results[4][1],
        results[0][2],
        results[1][2],
        results[2][2],
        results[3][2],
        results[4][2],
        results[0][3],
        results[1][3],
        results[2][3],
        results[3][3],
        results[4][3],
        sublayer_rms,
    )


def solution(mesh):
    return jax.shard_map(
        local,
        mesh=mesh,
        in_specs=(
            P(("dp", "fsdp"), None, None),
            P(("dp", "fsdp"), None, None),
            P(("dp", "fsdp")),
            P(None, ("dp", "fsdp"), None),
            P(None, ("dp", "fsdp"), None),
            P(None, ("dp", "fsdp"), None),
            P(None, ("dp", "fsdp"), None),
            P(None, ("dp", "fsdp")),
            P(None, ("dp", "fsdp"), None),
            P(None, ("dp", "fsdp"), None),
            P(None, ("dp", "fsdp"), None),
            P(None, ("dp", "fsdp"), None),
            P(None, ("dp", "fsdp")),
            P(None, ("dp", "fsdp"), None),
            P(None, ("dp", "fsdp"), None),
            P(None, ("dp", "fsdp"), None),
            P(None, ("dp", "fsdp"), None),
            P(None, ("dp", "fsdp")),
        ),
        out_specs=(
            P(("dp", "fsdp"), None, None),
            P(("dp", "fsdp"), None, None),
            P(None, ("dp", "fsdp"), None),
            P(None, ("dp", "fsdp"), None),
            P(None, ("dp", "fsdp"), None),
            P(None, ("dp", "fsdp"), None),
            P(None, ("dp", "fsdp")),
            P(None, ("dp", "fsdp"), None),
            P(None, ("dp", "fsdp"), None),
            P(None, ("dp", "fsdp"), None),
            P(None, ("dp", "fsdp"), None),
            P(None, ("dp", "fsdp")),
            P(None, ("dp", "fsdp"), None),
            P(None, ("dp", "fsdp"), None),
            P(None, ("dp", "fsdp"), None),
            P(None, ("dp", "fsdp"), None),
            P(None, ("dp", "fsdp")),
            P(None, ("dp", "fsdp"), None),
            P(None, ("dp", "fsdp"), None),
            P(None, ("dp", "fsdp"), None),
            P(None, ("dp", "fsdp"), None),
            P(None, ("dp", "fsdp")),
            P(),
        ),
        check_vma=False,
    )
```

```python
import functools

import jax
import jax.numpy as jnp
from jax import lax
from jax.experimental import pallas as pl
from jax.experimental.pallas import tpu as pltpu
from jax.sharding import PartitionSpec as P

HEADS = 8
NSTATE = 32
KERNEL = 15
STEP_NUMBER = 5


NORM_EPS = 1e-05
BETA_FIRST = 0.5
BETA_SECOND = 0.6
ADAM_EPS = 1e-08
RATE_MATRIX = 0.02
RATE_VECTOR = 0.2
WEIGHT_DECAY = 0.01


def adamw(master, first, second, gradient, rate, decay):
    first_new = BETA_FIRST * first + (1.0 - BETA_FIRST) * gradient
    second_new = BETA_SECOND * second + (1.0 - BETA_SECOND) * gradient * gradient
    first_hat = first_new / (1.0 - BETA_FIRST**STEP_NUMBER)
    second_hat = second_new / (1.0 - BETA_SECOND**STEP_NUMBER)
    updated = master - rate * (first_hat / (jnp.sqrt(second_hat) + ADAM_EPS) + decay * master)
    return (updated, first_new, second_new, updated.astype(jnp.bfloat16))


AXES = ("dp", "fsdp")
CORE, Z_HIGH, Z_LOW = 8, 4, 2
STAGES = (Z_HIGH, Z_LOW, (1, 16), (16, 1))


def swap(values, mask):
    masks = mask if isinstance(mask, tuple) else (mask, mask)
    return lax.ppermute(values, AXES, [(i, i ^ masks[(i >> 3) & 1]) for i in range(32)])


def after(values, *earlier):
    return lax.optimization_barrier((values, *earlier))[0] if earlier else values


def add_low(left, right):
    return (left.astype(jnp.float32) + right.astype(jnp.float32)).astype(jnp.bfloat16)


def pack_rows(sums):
    low = lax.reduce_precision(sums, 8, 7)
    rest = jnp.pad(sums[30:31] - low[30:31], ((31, 0), (0, 0)))
    return (low + rest).astype(jnp.bfloat16).reshape(2, 16, 512)


def unpack_rows(message):
    rows = message.astype(jnp.float32).reshape(32, 512)
    return jnp.concatenate([rows[:30], rows[30:31] + rows[31:32], jnp.zeros((1, 512), jnp.float32)])


def cut_columns(matrix):
    rows, columns = matrix.shape
    return matrix.reshape(rows, columns // 512, 512).transpose(1, 0, 2).reshape(-1, 512)


def pieces_of(matrix):
    by_piece = matrix.reshape(32, matrix.shape[0] // 32, -1, 512)
    return jnp.moveaxis(by_piece, 2, 1).reshape(32, -1, 512)


def join_columns(pieces, columns):
    lead = pieces.shape[:-2]
    rows = pieces.shape[-2] // columns
    moved = jnp.moveaxis(pieces.reshape(*lead, columns, rows, 512), -3, -2)
    return moved.reshape(*lead, rows, columns * 512)


def sync(*arrays):
    return lax.optimization_barrier(arrays)


def join(*arrays):
    return jnp.concatenate(arrays)


def shard_of(parts):
    return join(*[cut_columns(part.astype(jnp.bfloat16)).reshape(-1, 16, 512) for part in parts])


def gather_all(first, middle, last, vectors):
    far, near, late, later = STAGES
    own, mid, end = shard_of(first), shard_of(middle), shard_of(last)
    size = own.shape[0]
    vectors = vectors + swap(vectors, CORE)
    got0, got1 = swap(own, far), swap(own, near)
    vectors = vectors + swap(after(vectors, own), far)
    own, mid, end, got0, got1, vectors = sync(own, mid, end, got0, got1, vectors)

    got1_late = swap(join(got0, vectors), near)
    two = join(own, got0)
    got2 = swap(two, late)
    mid_got = swap(mid, far)
    got1_late, two, got2, mid_got, vectors = sync(got1_late, two, got2, mid_got, vectors)

    vectors = vectors + got1_late[size:]
    other_two = join(got1, got1_late[:size], vectors)
    got2_late = swap(other_two, late)
    four = join(two, other_two[:-2])
    got3 = swap(four, later)
    mid = join(mid, mid_got)
    mid_got, end_got = swap(mid, near), swap(after(end, mid_got), far)
    got2_late, got3, mid_got, end_got, other_two = sync(got2_late, got3, mid_got, end_got, other_two)

    vectors = vectors + got2_late[2 * size :]
    other_four = join(got2, got2_late[: 2 * size], vectors)
    got3_late = swap(other_four, later)
    mid = join(mid, mid_got)
    end = join(end, end_got)
    mid_got, end_got = swap(mid, late), swap(end, near)
    far_pieces = [swap(four, CORE), swap(other_four, CORE), swap(got3, CORE)]
    got3_late, mid_got, end_got, vectors = sync(got3_late, mid_got, end_got, vectors)

    vectors = vectors + got3_late[4 * size :]
    far_pieces.append(swap(got3_late, CORE))
    mid = join(mid, mid_got)
    mid_got, mid_far = swap(mid, later), swap(mid, CORE)
    end = join(end, end_got)
    end_got = swap(end, late)
    return (four, other_four, got3, got3_late, *far_pieces), vectors, (mid, mid_got, mid_far), (end, end_got)


def gather_whole(parts):
    gathered = [lax.all_gather(part.astype(jnp.bfloat16), AXES, axis=0, tiled=True) for part in parts]
    pieces = join(*[pieces_of(matrix) for matrix in gathered]) if len(parts) == 1 else jnp.concatenate(
        [pieces_of(matrix) for matrix in gathered], axis=1
    )
    return tuple(pieces.reshape(4, -1, 16, 512))


class Reduce:
    def __init__(self, columns, paired, rows=None, pack=None, unpack=None, stages=STAGES[::-1]):
        self.stages = stages
        self.columns, self.rows, self.pack, self.unpack, self.paired = columns, rows, pack, unpack, paired
        self.parts, self.stage, self.riding = [], 0, rows is not None
        if paired and rows is not None:
            self.more = swap(pack(rows), CORE)

    def add(self, kept, sent):
        self.parts.append((kept, swap(sent, CORE) if self.paired else sent))

    def start(self, *earlier):
        if not self.paired:
            return
        self.stage += 1
        if self.stage == 1:
            parts = [(kept, after(got, *earlier)) for kept, got in self.parts]
            count = 8 * sum(kept.shape[1] for kept, _ in parts)
            sent = jnp.concatenate([add_low(kept[8:], got[8:]) for kept, got in parts], axis=1)
            sent = sent.reshape(-1, 16, 512)
            more = after(self.more, *earlier) if self.riding else None
        else:
            count = self.kept.shape[0] // 2
            got = after(self.got, *earlier)
            sent = add_low(self.kept[count:], got[count : 2 * count])
            more = got[2 * count :]
        if self.riding:
            self.rows = self.rows + self.unpack(more)
        if self.rows is not None:
            sent = jnp.concatenate([sent, self.pack(self.rows)])
            self.riding = True
        new = swap(sent, self.stages[self.stage - 1])
        if self.stage == 1:
            parts = [(after(kept, sent)[:8], after(got, sent)[:8]) for kept, got in parts]
            kept = jnp.concatenate([add_low(kept, got) for kept, got in parts], axis=1)
            self.kept = kept.reshape(-1, 16, 512)
            self.groups = kept.shape[1]
        else:
            self.kept = add_low(after(self.kept, sent)[:count], after(got, sent)[:count])
        self.got, self.sent = new, sent

    def begun(self):
        if not self.paired:
            return ()
        return tuple(self.sent) if isinstance(self.sent, list) else (self.sent,)

    def attach(self, rows):
        if self.paired:
            rows = rows + self.unpack(swap(self.pack(rows), CORE))
            self.late = swap(self.pack(rows), STAGES[3])
        self.rows = rows

    def catch_up(self):
        if self.paired:
            self.got, late = sync(self.got, self.late)
            self.rows = self.rows + self.unpack(late)

    def spread(self, *earlier):
        got = after(self.got, *earlier)
        total = self.kept.astype(jnp.float32) + got[: 4 * self.groups].astype(jnp.float32)
        self.rows = self.rows + self.unpack(got[4 * self.groups :])
        total = total.reshape(4, self.groups, 16, 512)
        riders = self.pack(self.rows)
        self.sent = [jnp.concatenate([total[spot].astype(jnp.bfloat16), riders]) for spot in (2, 1, 3)]
        masks = (Z_LOW, Z_HIGH, Z_LOW | Z_HIGH)
        self.kept, self.got = total[0], [swap(sent, mask) for sent, mask in zip(self.sent, masks)]

    def finish(self, *earlier):
        if not self.paired:
            return self.scatter()
        if isinstance(self.got, list):
            pieces = [got[: self.groups].astype(jnp.float32) for got in self.got]
            total = (self.kept + pieces[0]) + (pieces[1] + pieces[2])
            return total.reshape(-1, 512), (self.rows, *[got[self.groups :] for got in self.got])
        self.got = after(self.got, *earlier)
        total = self.kept.astype(jnp.float32) + self.got[: self.groups].astype(jnp.float32)
        rows = None if self.rows is None else self.rows + self.unpack(self.got[self.groups :])
        return total.reshape(-1, 512), rows

    def scatter(self):
        pieces = jnp.concatenate([jnp.concatenate(part) for part in self.parts], axis=1).reshape(32, -1, 512)
        sums, start = [], 0
        for count, tall in self.columns:
            rows = 16 * count * tall
            matrix = join_columns(pieces[:, start : start + rows], count).reshape(512 * tall, -1)
            matrix = lax.psum_scatter(matrix.astype(jnp.float32), AXES, scatter_dimension=0, tiled=True)
            sums.append(cut_columns(matrix))
            start += rows
        rows = None if self.rows is None else lax.psum(self.rows, AXES)
        if rows is not None and rows.shape[0] == 8:
            rows = (rows, *[jnp.zeros((1, 16, 512), jnp.bfloat16)] * 3)
        return jnp.concatenate(sums), rows


def pack_pair(sums):
    low = lax.reduce_precision(sums[:2], 8, 7)
    parts = [low, sums[:2] - low, jnp.zeros((12, 512), jnp.float32)]
    return jnp.concatenate(parts).astype(jnp.bfloat16)[None]


def unpack_pair(message):
    rows = message[0].astype(jnp.float32)
    return jnp.concatenate([rows[0:2] + rows[2:4], jnp.zeros((6, 512), jnp.float32)])


TILE = 64
F32, LOW = jnp.float32, jnp.bfloat16
NN, NT, TN = ((1,), (0,)), ((1,), (1,)), ((0,), (0,))
VMEM_BYTES = 32 * 1024 * 1024


def mm(left, right, dims=NN):
    return lax.dot_general(left, right, (dims, ((), ())), preferred_element_type=F32)


def tiles(rows=512, step=TILE):
    return [pl.ds(start, step) for start in range(0, rows, step)]


def sigmoid(values):
    return 0.5 * jnp.tanh(0.5 * values) + 0.5


def standardize(values):
    centered = values - jnp.mean(values, axis=-1, keepdims=True)
    variance = jnp.mean(centered * centered, axis=-1, keepdims=True)
    spread = lax.rsqrt(variance + NORM_EPS)
    return centered * spread, spread


def standardize_back(grad, unit, spread):
    mean_grad = jnp.mean(grad, axis=-1, keepdims=True)
    mean_both = jnp.mean(grad * unit, axis=-1, keepdims=True)
    return spread * (grad - mean_grad - unit * mean_both)


def row(values):
    return jnp.sum(values, axis=0, keepdims=True)


def square(pieces):
    return pieces.reshape(512, 512)


class Place:
    def __init__(self, paired, order=0):
        self.paired, self.order = paired, order
        if paired:
            self.dp, self.fsdp = lax.axis_index("dp"), lax.axis_index("fsdp")
            self.core = self.dp & 1

    def device(self, spot):
        if not self.paired:
            return spot
        side, bits = spot // 16, [(spot >> place) & 1 for place in range(4)]
        first, second = 2 * bits[3] + side, bits[2]
        turned_first, turned_second = 2 * bits[2] + side, bits[3]
        around = 2 * bits[1] + 4 * bits[0]
        straight = self.core == side
        dp = self.dp ^ jnp.where(straight, first, turned_first)
        return 8 * dp + (self.fsdp ^ jnp.where(straight, second + around, turned_second + around))

    def piece(self, spot):
        if self.paired and self.order == 1:
            spot = (spot & 24) + 4 * (spot & 1) + ((spot >> 1) & 3)
        if self.paired and self.order == 2:
            spot = (spot & 25) + 2 * (spot & 2) + ((spot & 4) >> 1)
        return self.device(spot)

    def chunk(self, step):
        return self.dp ^ (0, 2, 1, 3)[step] if self.paired else step

    def spot(self, step, f):
        if not self.paired:
            return 8 * (step % 2) + f
        rel = self.fsdp ^ f
        low, z_near, z_far = ((4, 2, 1), (1, 4, 2), (2, 4, 1))[self.order]
        y_bit, z_spot = rel & 1, z_near * ((rel >> 1) & 1) + z_far * ((rel >> 2) & 1)
        straight = self.core == step // 2
        return z_spot + jnp.where(straight, 8 * (step % 2) + low * y_bit, 8 * y_bit + low * (step % 2))


def place_ffn(table, sources, w_in, w_out):
    each_has = 32 // len(sources)
    for side, source in enumerate(sources):
        for spot in range(each_has):
            device = table.device(each_has * side + spot)
            w_in[:, device] = source[pl.ds(8 * spot, 4)]
            w_out[pl.ds(4 * device, 4)] = source[pl.ds(8 * spot + 4, 4)]


def place_mix(table, sources, first, weights):
    each_has = 32 // len(sources)
    for side, source in enumerate(sources):
        for spot in range(each_has):
            weights[:, table.device(each_has * side + spot)] = source[pl.ds(6 * spot + first, 3)]


def start_all(copies):
    for copy in copies:
        copy.start()


def wait_all(copies):
    for copy in copies:
        copy.wait()


def fill_normed(h_ref, vec_ref, index, normed):
    gain = vec_ref[pl.ds(2 * index, 1)].astype(F32)
    shift = vec_ref[pl.ds(2 * index + 1, 1)].astype(F32)
    for part in tiles():
        unit, _ = standardize(h_ref[part].astype(F32))
        normed[part] = (unit * gain + shift).astype(LOW)


def order_rows(table, natural, ordered):
    for spot in range(32):
        ordered[spot] = natural[table.piece(spot)]


def fill_transposed(source, natural):
    for part in tiles(step=128):
        turned = source[part].astype(F32).T.astype(LOW)
        natural[:, :, part] = turned.reshape(32, 16, 128)


def norm_back(h_ref, vec_ref, index, grad_normed, grad_in, grad_out):
    gain = vec_ref[pl.ds(2 * index, 1)].astype(F32)
    grad_gain, grad_shift = jnp.zeros((1, 512), F32), jnp.zeros((1, 512), F32)
    for part in tiles():
        unit, spread = standardize(h_ref[part].astype(F32))
        grad = grad_normed[part]
        grad_gain = grad_gain + row(grad * unit)
        grad_shift = grad_shift + row(grad)
        grad_out[part] = grad_in[part] + standardize_back(grad * gain, unit, spread)
    return grad_gain, grad_shift


def valid_rows(length, part):
    places = part.start + lax.broadcasted_iota(jnp.int32, (part.size, 1), 0)
    return (places < length).astype(F32)


def valid_lanes(length):
    return (lax.broadcasted_iota(jnp.int32, (1, 512), 1) < length).astype(F32)


def ffn_forward(length, h_ref, normed, w_in, w_out, pre, act, out, new_h, save):
    pre[0] = mm(normed[...], square(w_in[0]))
    for j in range(4):
        pre_j, act_j = pre.at[j], act(j)
        if j < 3:
            pre[j + 1] = mm(normed[...], square(w_in[j + 1]))
        for part in tiles():
            values = pre_j[part]
            act_j[part] = (values * sigmoid(values)).astype(LOW)
        save(j)
        more = mm(act_j[...], square(w_out[pl.ds(32 * j, 32)]))
        out[...] = more if j == 0 else out[...] + more
    total = jnp.zeros((1, 512), F32)
    for part in tiles():
        half = 0.5 * out[part]
        new_h[part] = h_ref[part].astype(F32) + half
        total = total + row(valid_rows(length, part) * half * half)
    return total


def place_out_grads(table, step, first, kept, sent, act, grad_low):
    products = mm(act, grad_low, TN).astype(LOW).reshape(8, 4, 16, 512)
    for f in range(8):
        (kept, sent)[step // 2][table.spot(step, f), pl.ds(first, 4)] = products[f]


def place_rows(kept, sent, group, products):
    pieces = products.astype(LOW).reshape(32, 16, 512)
    kept[:, group] = pieces[:16]
    sent[:, group] = pieces[16:]


def ffn_backward(table, w_out, pre, grad_low, turned, act, grad_pre, kept, sent):
    def first_product(step):
        return mm(grad_low[...], square(w_out[pl.ds(32 * table.chunk(step), 32)]), NT)

    following = first_product(0)
    for step in range(4):
        chunk = table.chunk(step)
        pre_j = pre.at[chunk]
        grad_act = following
        if step < 3:
            following = first_product(step + 1)
        for part in tiles():
            values = pre_j[part]
            gate = sigmoid(values)
            lifted = values * gate
            if act is not None:
                act[part] = lifted.astype(LOW)
            slope = gate + lifted * (1.0 - gate)
            grad_pre[chunk, part] = (grad_act[part.start : part.start + part.size] * slope).astype(LOW)
        place_rows(kept, sent, chunk, mm(square(turned[...]), grad_pre[chunk]))
        if act is not None:
            place_out_grads(table, step, 4, kept, sent, act[...], grad_low[...])


def first_kernel(paired, length, h_ref, vec_ref, *refs):
    table = Place(paired)
    *pieces, h1_ref, pre_hbm, act_hbm, stat_ref, in_hbm, out_hbm = refs[:-9]
    w_in, w_out, normed, act, out, pre, pre_sem, act_sem, w_sem = refs[-9:]
    place_ffn(table, pieces, w_in, w_out)
    weights = [
        pltpu.make_async_copy(w_in, in_hbm, w_sem.at[0]),
        pltpu.make_async_copy(w_out, out_hbm, w_sem.at[1]),
    ]
    start_all(weights)
    fill_normed(h_ref, vec_ref, 0, normed)

    copies = [
        (
            pltpu.make_async_copy(pre.at[j], pre_hbm.at[j], pre_sem.at[j]),
            pltpu.make_async_copy(act.at[j], act_hbm.at[j], act_sem.at[j]),
        )
        for j in range(4)
    ]

    def save(j):
        start_all(copies[j])

    stat_ref[...] = ffn_forward(
        length[0], h_ref, normed, w_in, w_out, pre, lambda j: act.at[j], out, h1_ref, save
    )
    for j in range(4):
        wait_all(copies[j])
    wait_all(weights)


def last_kernel(
    paired, length, h_ref, vec_ref, cot_ref, held, got, held_far, got_far,
    top_ref, grad_ref, rows_ref, kept, sent, w_in, grad_pre,
    w_out, normed, act, out, pre, low, natural, turned
):
    table = Place(paired, 1)
    place_ffn(table, (held, got, held_far, got_far), w_in, w_out)
    fill_normed(h_ref, vec_ref, 4, normed)
    fill_transposed(normed, natural)
    order_rows(table, natural, turned)
    stat4 = ffn_forward(length[0], h_ref, normed, w_in, w_out, pre, lambda j: act, out, grad_ref, lambda j: None)
    gain, shift = vec_ref[pl.ds(10, 1)].astype(F32), vec_ref[pl.ds(11, 1)].astype(F32)
    grad_gain, grad_shift = jnp.zeros((1, 512), F32), jnp.zeros((1, 512), F32)
    stat5 = jnp.zeros((1, 512), F32)
    for part in tiles():
        values = grad_ref[part]
        stat5 = stat5 + row(valid_rows(length[0], part) * values * values)
        unit, spread = standardize(values)
        top_ref[part] = unit * gain + shift
        grad = cot_ref[part].astype(F32)
        grad_gain = grad_gain + row(grad * unit)
        grad_shift = grad_shift + row(grad)
        back = standardize_back(grad * gain, unit, spread)
        grad_ref[part] = back
        low[part] = (0.5 * back).astype(LOW)
    ffn_backward(table, w_out, pre, low, turned, act, grad_pre, kept, sent)
    rows_ref[...] = jnp.concatenate([grad_gain, grad_shift, stat4, stat5, jnp.zeros((4, 512), F32)])


def back_out_kernel(paired, grad_in, act, kept, sent, low):
    table = Place(paired)
    for part in tiles():
        low[part] = (0.5 * grad_in[part]).astype(LOW)
    for step in range(4):
        place_out_grads(table, step, 0, kept, sent, act[table.chunk(step)], low[...])


def back_in_kernel(
    paired, h_ref, vec_ref, grad_in, w_out, pre, kept, sent, grad_pre, normed, low, natural, turned
):
    table = Place(paired)
    fill_normed(h_ref, vec_ref, 0, normed)
    fill_transposed(normed, natural)
    order_rows(table, natural, turned)
    for part in tiles():
        low[part] = (0.5 * grad_in[part]).astype(LOW)
    ffn_backward(table, w_out, pre, low, turned, None, grad_pre, kept, sent)


def ffn_grad_kernel(index, h_ref, vec_ref, grad_in, w_in, grad_pre, grad_ref, rows_ref, out):
    for j in range(4):
        more = mm(grad_pre[j], square(w_in[j]), NT)
        out[...] = more if j == 0 else out[...] + more
    gain, shift = norm_back(h_ref, vec_ref, index, out, grad_in, grad_ref)
    rows_ref[...] = jnp.concatenate([gain, shift, jnp.zeros((6, 512), F32)])


def vector_step_kernel(
    width, rows_ref, pair_ref, got0, got1, got2, master, first, second, new_ref, first_ref, second_ref, copy_ref
):
    pair = pair_ref[0:2]
    for got in (got0, got1, got2):
        message = got[0].astype(F32)
        pair = pair + (message[0:2] + message[2:4])
    rows = jnp.concatenate([pair, rows_ref[2:32]])
    me = lax.axis_index("dp") * lax.axis_size("fsdp") + lax.axis_index("fsdp")
    turned = pltpu.roll(rows, lax.rem(512 - width * me, 512), 1)[:, 0:128].T
    results = adamw(master[...], first[...], second[...], turned[0:width, 0:30], RATE_VECTOR, 0.0)
    for ref, values in zip((new_ref, first_ref, second_ref, copy_ref), results):
        ref[...] = values


def mix_step_kernel(kept, got, *refs):
    sums = [kept[group].astype(F32) + got[group].astype(F32) for group in range(6)]
    inputs, outputs = refs[:6], refs[6:]
    for k in range(2):
        for which, part, group in ((0, pl.ds(0, 512), 0), (0, pl.ds(512, 512), 1), (1, pl.ds(0, 512), 2)):
            parts = [ref[k, :, part] for ref in inputs[3 * which : 3 * which + 3]]
            results = adamw(*parts, sums[3 * k + group], RATE_MATRIX, WEIGHT_DECAY)
            for ref, values in zip(outputs[4 * which : 4 * which + 4], results):
                ref[k, :, part] = values


def vector_columns(vec_ref, pad):
    pad[...] = jnp.zeros((128, 512), F32)
    pad[pl.ds(0, 32)] = vec_ref[...].astype(F32)
    return pad[...].T


def ssm_decays(columns):
    rates = jnp.exp(columns[0:256, 13:14])
    lags = lax.broadcasted_iota(jnp.int32, (1, 512), 1).astype(F32)
    return jnp.exp(-rates * lags), rates, columns[256:512, 13:14]


def head_matrix(kernels, head):
    line = jnp.concatenate([kernels[head : head + 1], jnp.zeros((1, 128), F32)], axis=1)
    skewed = pltpu.roll(jnp.broadcast_to(line, (128, 640)), 0, 1, stride=1, stride_axis=0)
    return skewed[:, :512].astype(LOW)


def blocks_of(rows):
    return jnp.concatenate([rows[:, 128 * b : 128 * (b + 1)] for b in range(4)], axis=0)


def ssm_kernel(
    paired, length, h_ref, vec_ref, held, got, held_far, got_far, h2_ref, saved_hbm, stat_ref, weights_hbm,
    weights, normed, act, saved, pad, save_sem, w_sem
):
    table = Place(paired)
    place_mix(table, (held, got, held_far, got_far), 0, weights)
    hand_on = pltpu.make_async_copy(weights, weights_hbm, w_sem)
    hand_on.start()
    fill_normed(h_ref, vec_ref, 1, normed)
    columns = vector_columns(vec_ref, pad)
    decays, _, coefs = ssm_decays(columns)
    kernels = jnp.sum((coefs * decays).reshape(8, 32, 512), axis=1)
    mask = valid_lanes(length[0])
    signal, gate, mixed = saved.at[0], saved.at[1], saved.at[2]
    signal[...] = mm(square(weights[0]), normed[...], ((0,), (1,))) * mask
    gate[...] = mm(square(weights[1]), normed[...], ((0,), (1,)))
    copies = [pltpu.make_async_copy(saved.at[k], saved_hbm.at[k], save_sem.at[k]) for k in range(3)]
    copies[0].start()
    copies[1].start()
    for head in range(8):
        part = pl.ds(64 * head, 64)
        rows = signal[part]
        spread = mm(blocks_of(rows).astype(LOW), head_matrix(kernels, head))
        skip = columns[64 * head : 64 * head + 64, 12:13]
        for a in range(4):
            lanes = pl.ds(128 * a, 128)
            total = skip * rows[:, 128 * a : 128 * a + 128]
            for b in range(a + 1):
                total = total + spread[64 * b : 64 * b + 64, 128 * (a - b) : 128 * (a - b) + 128]
            mixed[part, lanes] = total
            gates = gate[part, lanes]
            act[part, lanes] = (total * gates * sigmoid(gates)).astype(LOW)
    copies[2].start()
    out = mm(act[...], square(weights[2]), TN)
    total = jnp.zeros((1, 512), F32)
    for part in tiles():
        values = out[part.start : part.start + part.size]
        h2_ref[part] = h_ref[part] + values
        total = total + row(valid_rows(length[0], part) * values * values)
    stat_ref[...] = total
    wait_all(copies)
    hand_on.wait()


def ssm_back_kernel(
    paired, length, h_ref, vec_ref, grad_in, weights, saved, stat1, stat2, rows2, rows3, rows4,
    grad_ref, rows_ref, kept, sent,
    normed, low, natural, turned, act, act_turned, grad_pre, out, pad, kernel_grads, skip_grads
):
    table = Place(paired, 2)
    fill_normed(h_ref, vec_ref, 1, normed)
    fill_transposed(normed, natural)
    order_rows(table, natural, turned)
    for part in tiles():
        low[part] = grad_in[part].astype(LOW)
    columns = vector_columns(vec_ref, pad)
    decays, rates, coefs = ssm_decays(columns)
    kernels = jnp.sum((coefs * decays).reshape(8, 32, 512), axis=1)
    mask = valid_lanes(length[0])
    signal, gate, mixed = saved.at[0], saved.at[1], saved.at[2]
    out[...] = mm(square(weights[2]), low[...], NT)
    flipped = lax.broadcasted_iota(jnp.int32, (128, 128), 0) + lax.broadcasted_iota(jnp.int32, (128, 128), 1)
    flip = (flipped == 127).astype(F32).astype(LOW)
    for head in range(8):
        part = pl.ds(64 * head, 64)
        rows, gates, mixes, grad_act = signal[part], gate[part], mixed[part], out[part]
        gating = sigmoid(gates)
        lifted = gates * gating
        act[pl.ds(4 * head, 4)] = (mixes * lifted).astype(LOW).reshape(4, 16, 512)
        grad_mixed = grad_act * lifted
        grad_pre[1, part] = (grad_act * mixes * (gating + lifted * (1.0 - gating))).astype(LOW)
        grad_low = grad_mixed.astype(LOW)
        shifted = jnp.concatenate(
            [grad_low]
            + [
                jnp.concatenate([grad_low[:, 128 * b :], jnp.zeros((64, 128 * b), LOW)], axis=1)
                for b in (1, 2, 3)
            ],
            axis=0,
        )
        back = mm(shifted, head_matrix(kernels, head), NT)
        mirrored = mm(blocks_of(rows).astype(LOW), flip).astype(LOW)
        lag_sums = mm(mirrored, shifted, TN)
        lag_sums = jnp.concatenate([lag_sums, jnp.zeros((128, 128), F32)], axis=1)
        lag_sums = row(pltpu.roll(lag_sums, 0, 1, stride=1, stride_axis=0))
        kernel_grads[pl.ds(head, 1)] = pltpu.roll(lag_sums, 640 - 127, 1)[:, :512]
        skip = columns[64 * head : 64 * head + 64, 12:13]
        pad_lane = jnp.sum(grad_mixed * rows, axis=1, keepdims=True)
        natural_grad = jnp.concatenate([back[64 * b : 64 * b + 64] for b in range(4)], axis=1)
        grad_pre[0, part] = ((natural_grad + skip * grad_mixed) * mask).astype(LOW)
        normed_f = jnp.broadcast_to(pad_lane, (64, 128))
        skip_grads[part] = normed_f
    order_rows(table, act, act_turned)
    place_rows(kept, sent, 2, mm(square(act_turned[...]), low[...]))
    for q in range(2):
        more = mm(grad_pre[q], square(weights[q]), ((0,), (1,)))
        out[...] = more if q == 0 else out[...] + more
        place_rows(kept, sent, q, mm(square(turned[...]), grad_pre[q], NT))
    gain1, shift1 = norm_back(h_ref, vec_ref, 1, out, grad_in, grad_ref)
    lag_grads = jnp.broadcast_to(kernel_grads[...].reshape(8, 1, 512), (8, 32, 512)).reshape(256, 512)
    lags = lax.broadcasted_iota(jnp.int32, (1, 512), 1).astype(F32)
    weighed = lag_grads * decays
    coef_grads = jnp.sum(weighed, axis=1, keepdims=True)
    rate_grads = -rates * coefs * jnp.sum(weighed * lags, axis=1, keepdims=True)
    lanes = lax.broadcasted_iota(jnp.int32, (1, 128), 1)
    ssm_column = jnp.concatenate([rate_grads, coef_grads], axis=0)
    both = jnp.where(lanes == 0, skip_grads[...], 0.0) + jnp.where(lanes == 1, ssm_column, 0.0)
    turned_rows = both.T
    lanes = lax.broadcasted_iota(jnp.int32, (1, 512), 1)
    stats = jnp.where(lanes == 5, length[0].astype(F32), 0.0)
    for place, sums in enumerate([stat1[...], stat2[...], rows2[20:21], rows3[2:3], rows3[3:4]]):
        stats = stats + jnp.where(lanes == place, jnp.sum(sums, axis=1, keepdims=True), 0.0)
    nothing = jnp.zeros((2, 512), F32)
    rows_ref[...] = jnp.concatenate(
        [nothing, gain1, shift1, rows2[0:4], rows4[0:2], rows3[0:2], turned_rows[0:2], rows2[4:20], stats, nothing[0:1]]
    )


PAD = 16


def conv_kernel(
    paired, length, h_ref, vec_ref, held, got, held_far, got_far, h3_ref, saved_hbm, stat_ref, weights_hbm,
    weights, normed, act, saved, padded, save_sem, w_sem
):
    table = Place(paired)
    place_mix(table, (held, got, held_far, got_far), 3, weights)
    hand_on = pltpu.make_async_copy(weights, weights_hbm, w_sem)
    hand_on.start()
    fill_normed(h_ref, vec_ref, 2, normed)
    copies = [pltpu.make_async_copy(saved.at[k], saved_hbm.at[k], save_sem.at[k]) for k in range(3)]
    for q in range(2):
        saved[q] = mm(normed[...], square(weights[q]))
        copies[q].start()
    for c in range(4):
        padded[c, pl.ds(0, PAD)] = jnp.zeros((PAD, 128), F32)
        padded[c, pl.ds(PAD + 512, PAD)] = jnp.zeros((PAD, 128), F32)
        lanes = pl.ds(128 * c, 128)
        for part in tiles():
            glu = saved[0, part, lanes] * sigmoid(saved[1, part, lanes]) * valid_rows(length[0], part)
            padded[c, pl.ds(PAD + part.start, part.size)] = glu
        taps = [vec_ref[pl.ds(14 + j, 1), lanes].astype(F32) for j in range(KERNEL + 1)]
        for part in tiles():
            total = jnp.broadcast_to(taps[KERNEL], (part.size, 128))
            for j in range(KERNEL):
                total = total + padded[c, pl.ds(PAD + part.start + j - 7, part.size)] * taps[j]
            saved[2, part, lanes] = total
    copies[2].start()
    gain, shift = vec_ref[pl.ds(6, 1)].astype(F32), vec_ref[pl.ds(7, 1)].astype(F32)
    for part in tiles():
        unit, _ = standardize(saved[2, part])
        values = unit * gain + shift
        act[part] = (values * sigmoid(values)).astype(LOW)
    out = mm(act[...], square(weights[2]))
    total = jnp.zeros((1, 512), F32)
    for part in tiles():
        values = out[part.start : part.start + part.size]
        h3_ref[part] = h_ref[part] + values
        total = total + row(valid_rows(length[0], part) * values * values)
    stat_ref[...] = total
    wait_all(copies)
    hand_on.wait()


def conv_back_kernel(
    paired, length, h_ref, vec_ref, grad_in, weights, saved, stat_in,
    grad_ref, rows_ref, kept, sent,
    normed, low, natural, turned, act, act_turned, grad_pre, out, padded, padded_grad
):
    table = Place(paired, 2)
    fill_normed(h_ref, vec_ref, 2, normed)
    fill_transposed(normed, natural)
    order_rows(table, natural, turned)
    for part in tiles():
        low[part] = grad_in[part].astype(LOW)
    out[...] = mm(low[...], square(weights[2]), NT)
    gain, shift = vec_ref[pl.ds(6, 1)].astype(F32), vec_ref[pl.ds(7, 1)].astype(F32)
    gain3, shift3, bias = (jnp.zeros((1, 512), F32) for _ in range(3))
    for part in tiles():
        unit, spread = standardize(saved[2, part])
        values = unit * gain + shift
        gating = sigmoid(values)
        lifted = values * gating
        normed[part] = lifted.astype(LOW)
        grad = out[part] * (gating + lifted * (1.0 - gating))
        gain3 = gain3 + row(grad * unit)
        shift3 = shift3 + row(grad)
        back = standardize_back(grad * gain, unit, spread)
        bias = bias + row(back)
        for c in range(4):
            padded_grad[c, pl.ds(PAD + part.start, part.size)] = back[:, 128 * c : 128 * c + 128]
    fill_transposed(normed, act)
    order_rows(table, act, act_turned)
    place_rows(kept, sent, 2, mm(square(act_turned[...]), low[...]))
    tap_rows = []
    for c in range(4):
        lanes = pl.ds(128 * c, 128)
        for ref in (padded, padded_grad):
            ref[c, pl.ds(0, PAD)] = jnp.zeros((PAD, 128), F32)
            ref[c, pl.ds(PAD + 512, PAD)] = jnp.zeros((PAD, 128), F32)
        for part in tiles():
            glu = saved[0, part, lanes] * sigmoid(saved[1, part, lanes]) * valid_rows(length[0], part)
            padded[c, pl.ds(PAD + part.start, part.size)] = glu
        taps = [vec_ref[pl.ds(14 + j, 1), lanes].astype(F32) for j in range(KERNEL)]
        sums = [jnp.zeros((8, 128), F32) for _ in range(KERNEL)]
        for part in tiles():
            total = jnp.zeros((part.size, 128), F32)
            grad = padded_grad[c, pl.ds(PAD + part.start, part.size)]
            for j in range(KERNEL):
                total = total + padded_grad[c, pl.ds(PAD + part.start + 7 - j, part.size)] * taps[j]
                seen = padded[c, pl.ds(PAD + part.start + j - 7, part.size)]
                sums[j] = sums[j] + jnp.sum((grad * seen).reshape(part.size // 8, 8, 128), axis=0)
            total = total * valid_rows(length[0], part)
            gating = sigmoid(saved[1, part, lanes])
            first = total * gating
            grad_pre[0, part, lanes] = first.astype(LOW)
            grad_pre[1, part, lanes] = (first * saved[0, part, lanes] * (1.0 - gating)).astype(LOW)
        tap_rows.append(jnp.concatenate([row(values) for values in sums], axis=0))
    for q in range(2):
        more = mm(grad_pre[q], square(weights[q]), NT)
        out[...] = more if q == 0 else out[...] + more
        place_rows(kept, sent, q, mm(square(turned[...]), grad_pre[q]))
    gain2, shift2 = norm_back(h_ref, vec_ref, 2, out, grad_in, grad_ref)
    rows_ref[...] = jnp.concatenate(
        [gain2, shift2, gain3, shift3, jnp.concatenate(tap_rows, axis=1), bias, stat_in[...], jnp.zeros((3, 512), F32)]
    )


def call(kernel, scalars, arrays, outs, scratch, flops):
    in_vmem, in_hbm = pl.BlockSpec(memory_space=pltpu.VMEM), pl.BlockSpec(memory_space=pltpu.HBM)
    return pl.pallas_call(
        kernel,
        out_shape=[
            (pltpu.HBM if apart else jax.ShapeDtypeStruct)(shape, dtype) for shape, dtype, apart in outs
        ],
        in_specs=[pl.BlockSpec(memory_space=pltpu.SMEM)] * len(scalars) + [in_vmem] * len(arrays),
        out_specs=[in_hbm if apart else in_vmem for _, _, apart in outs],
        scratch_shapes=scratch,
        compiler_params=pltpu.CompilerParams(vmem_limit_bytes=VMEM_BYTES),
        cost_estimate=pl.CostEstimate(flops=10 * flops, bytes_accessed=10 << 20, transcendentals=0),
    )(*scalars, *arrays)


SQUARE, PIECES = (512, 512), (32, 16, 512)
DMA = pltpu.SemaphoreType.DMA
IN_FFN, OUT_FFN, MIX = (4, 32, 16, 512), (128, 16, 512), (3, 32, 16, 512)
SMALL, LARGE = 512 * 512 * 512 * 2, 512 * 512 * 2048 * 2


def low_scratch(*shapes):
    return [pltpu.VMEM(shape, LOW) for shape in shapes]


def full_scratch(*shapes):
    return [pltpu.VMEM(shape, F32) for shape in shapes]


def grads_of(groups):
    return [((16, groups, 16, 512), LOW, False)] * 2


def run_first(paired, length, h, vectors, pieces):
    return call(
        functools.partial(first_kernel, paired),
        [length],
        [h, vectors, *pieces],
        [(SQUARE, F32, False), ((4, 512, 512), F32, True), ((4, 512, 512), LOW, True), ((1, 512), F32, False)]
        + [(IN_FFN, LOW, True), (OUT_FFN, LOW, True)],
        low_scratch(IN_FFN, OUT_FFN, SQUARE, (4, 512, 512))
        + full_scratch(SQUARE, (4, 512, 512))
        + [DMA((4,)), DMA((4,)), DMA((2,))],
        2 * LARGE,
    )


def run_last(paired, length, h, vectors, cotangent, pieces):
    return call(
        functools.partial(last_kernel, paired),
        [length],
        [h, vectors, cotangent, *pieces],
        [(SQUARE, F32, False), (SQUARE, F32, False), ((8, 512), F32, False), *grads_of(8)]
        + [(IN_FFN, LOW, False), ((4, 512, 512), LOW, False)],
        low_scratch(OUT_FFN, SQUARE, SQUARE)
        + full_scratch(SQUARE, (4, 512, 512))
        + low_scratch(SQUARE, PIECES, PIECES),
        6 * LARGE,
    )


def run_back_out(paired, grad, act):
    return call(functools.partial(back_out_kernel, paired), [], [grad, act], grads_of(4), low_scratch(SQUARE), LARGE)


def run_back_in(paired, h, vectors, grad, w_out, pre):
    return call(
        functools.partial(back_in_kernel, paired),
        [],
        [h, vectors, grad, w_out, pre],
        [*grads_of(4), ((4, 512, 512), LOW, False)],
        low_scratch(SQUARE, SQUARE, PIECES, PIECES),
        2 * LARGE,
    )


def run_ffn_grad(index, h, vectors, grad, w_in, grad_pre):
    return call(
        functools.partial(ffn_grad_kernel, index),
        [],
        [h, vectors, grad, w_in, grad_pre],
        [(SQUARE, F32, False), ((8, 512), F32, False)],
        full_scratch(SQUARE),
        LARGE,
    )


def run_vector_step(rows, pair, master, first, second):
    shape = master.shape
    results = call(
        functools.partial(vector_step_kernel, shape[0]),
        [],
        [rows, *pair, master, first, second],
        [(shape, F32, False)] * 3 + [(shape, LOW, False)],
        [],
        SMALL // 40,
    )
    return tuple(part.T for part in results)


def run_mix_step(kept, got, mix_in, mix_out):
    outs = []
    for parts in (mix_in, mix_out):
        outs += [(parts[0].shape, F32, False)] * 3 + [(parts[0].shape, LOW, False)]
    results = call(mix_step_kernel, [], [kept, got, *mix_in, *mix_out], outs, [], SMALL // 40)
    return tuple(results[:4]), tuple(results[4:])


def run_mix(kernel, paired, length, h, vectors, pieces, last_scratch):
    return call(
        functools.partial(kernel, paired),
        [length],
        [h, vectors, *pieces],
        [(SQUARE, F32, False), ((3, 512, 512), F32, True), ((1, 512), F32, False), (MIX, LOW, True)],
        low_scratch(MIX, SQUARE, SQUARE) + full_scratch((3, 512, 512), last_scratch) + [DMA((3,)), DMA],
        4 * SMALL,
    )


def run_mix_back(kernel, paired, length, h, vectors, grad, weights, saved, more, rows, last_scratch):
    return call(
        functools.partial(kernel, paired),
        [length],
        [h, vectors, grad, *weights, saved, *more],
        [(SQUARE, F32, False), ((rows, 512), F32, False), *grads_of(3)],
        low_scratch(SQUARE, SQUARE, PIECES, PIECES, PIECES, PIECES, (2, 512, 512))
        + full_scratch(SQUARE, *last_scratch),
        8 * SMALL,
    )


def local(
    frames,
    cotangent,
    seq_lengths,
    ffn_in_master,
    ffn_out_master,
    mix_in_master,
    mix_out_master,
    vector_master,
    ffn_in_first,
    ffn_out_first,
    mix_in_first,
    mix_out_first,
    vector_first,
    ffn_in_second,
    ffn_out_second,
    mix_in_second,
    mix_out_second,
    vector_second,
):
    me = lax.axis_index(AXES)
    paired = (lax.axis_size("dp"), lax.axis_size("fsdp")) == (4, 8)
    low = jnp.bfloat16
    width, n = vector_master.shape[1], ffn_in_master.shape[1]
    placed = lax.dynamic_update_slice(
        jnp.zeros((32, 512), low), vector_master.astype(low), (0, width * me)
    ).reshape(2, 16, 512)
    first = [ffn_in_master[0], ffn_out_master[0]]
    middle = [mix_in_master[0], mix_out_master[0], mix_in_master[1], mix_out_master[1]]
    last = [ffn_in_master[1], ffn_out_master[1]]
    h0, length = frames[0], seq_lengths
    if paired:
        first, vectors, (mid, mid_got, mid_far), (end, end_got) = gather_all(first, middle, last, placed)
    else:
        first, middle, last = gather_whole(first), gather_whole(middle), gather_whole(last)
        vectors = lax.psum(placed, AXES)
    vectors = vectors.reshape(32, 512)
    h1, pre0, act0, stat1, *weights0 = run_first(paired, length, h0, vectors, first)
    if paired:
        mid_got, end_got, stat1 = sync(mid_got, end_got, stat1)
        end = join(end, end_got)
        end_got, end_far = swap(end, STAGES[3]), swap(end, CORE)
        middle = (mid, mid_got, mid_far, swap(mid_got, CORE))
    h2, saved1, stat2, *weights1 = run_mix(ssm_kernel, paired, length, h1, vectors, middle, (128, 512))
    h3, saved2, stat3, *weights2 = run_mix(
        conv_kernel, paired, length, h2, vectors, middle, (4, 512 + 2 * PAD, 128)
    )
    if paired:
        end_got, stat3 = sync(end_got, stat3)
        last = (end, end_got, end_far, swap(end_got, CORE))
    activations, grad4, rows3, kept3, sent3, w_in3, grad_pre3 = run_last(
        paired, length, h3, vectors, cotangent[0], last
    )
    sum3 = Reduce(((4, 1), (1, 4)), paired, stages=(STAGES[3], Z_LOW, Z_HIGH, STAGES[2]))
    sum3.add(kept3, sent3)
    grad3, rows4 = run_ffn_grad(4, h3, vectors, grad4, w_in3, grad_pre3)
    sum3.start(rows4)
    grad2, rows2, kept2, sent2 = run_mix_back(
        conv_back_kernel, paired, length, h2, vectors, after(grad3, *sum3.begun()), weights2, saved2, [stat3], 24,
        [(4, 512 + 2 * PAD, 128)] * 2,
    )
    grad1, rows, kept1, sent1 = run_mix_back(
        ssm_back_kernel, paired, length, h1, vectors, grad2, weights1, saved1,
        [stat1, stat2, rows2, rows3, rows4], 32, [(128, 512), (8, 512), (512, 128)],
    )
    sum1 = Reduce(
        ((2, 1), (1, 1)) * 2, paired, rows, pack_rows, unpack_rows, (STAGES[3], Z_LOW, STAGES[2], Z_HIGH)
    )
    sum1.add(kept1, sent1)
    sum1.add(kept2, sent2)
    sum3.start(rows)
    kept_out, sent_out = run_back_out(paired, after(grad1, *sum3.begun()), act0)
    sum_out = Reduce(((1, 4),), paired)
    sum_out.add(kept_out, sent_out)
    sum1.start(kept_out)
    grad1 = after(grad1, *sum1.begun())
    kept_in, sent_in, grad_pre0 = run_back_in(paired, h0, vectors, grad1, weights0[1], pre0)
    sum_in = Reduce(((4, 1),), paired, None, pack_pair, unpack_pair)
    sum_in.add(kept_in, sent_in)
    sum_out.start(kept_in)
    sum_in.start(*sum_out.begun())
    grad0, pair = run_ffn_grad(
        0, h0, vectors, after(grad1, *sum_in.begun()), weights0[0], grad_pre0
    )
    sum1.start(pair)
    sum3.start(pair)
    sum_in.attach(pair)
    sum_out.start(*sum1.begun())
    sum_in.catch_up()
    sum_in.start(*sum_out.begun())
    sum1.start(*sum_in.begun())
    sum3.start(*sum1.begun())
    sum_out.start(*sum3.begun())
    if paired:
        sum_in.spread(*sum_out.begun())
        sum_in.kept, sum1.got, sum_out.got = sync(sum_in.kept, sum1.got, sum_out.got)
    sum1.start(*sum_in.begun())
    sum_out.start(*sum1.begun())
    if paired:
        sum_out.kept, sum1.kept, *sum_in.got = sync(sum_out.kept, sum1.kept, *sum_in.got)
    whole3, _ = sum3.finish(*sum_out.begun())
    whole1, rows = sum1.finish(*sum_out.begun())
    whole_out, _ = sum_out.finish()
    whole_in, pair = sum_in.finish()
    reduced = (
        jnp.stack([join_columns(whole_in, 4), join_columns(whole3[: 4 * n], 4)]),
        jnp.stack([whole_out, whole3[4 * n :]]),
        jnp.stack([join_columns(whole1[: 2 * n], 2), join_columns(whole1[3 * n : 5 * n], 2)]),
        jnp.stack([whole1[2 * n : 3 * n], whole1[5 * n :]]),
    )
    sublayer_rms = jnp.sqrt(rows[30, :5] / (rows[30, 5] * frames.shape[2]))
    masters = (ffn_in_master, ffn_out_master, mix_in_master, mix_out_master)
    firsts = (ffn_in_first, ffn_out_first, mix_in_first, mix_out_first)
    seconds = (ffn_in_second, ffn_out_second, mix_in_second, mix_out_second)
    results = [
        adamw(
            masters[slot_index],
            firsts[slot_index],
            seconds[slot_index],
            reduced[slot_index],
            RATE_MATRIX,
            WEIGHT_DECAY,
        )
        for slot_index in range(4)
    ]
    if paired:
        results[2:] = run_mix_step(
            sum1.kept,
            sum1.got,
            [mix_in_master, mix_in_first, mix_in_second],
            [mix_out_master, mix_out_first, mix_out_second],
        )
    results.append(run_vector_step(rows, pair, vector_master.T, vector_first.T, vector_second.T))
    return (
        activations[None],
        grad0[None],
        results[0][0],
        results[1][0],
        results[2][0],
        results[3][0],
        results[4][0],
        results[0][1],
        results[1][1],
        results[2][1],
        results[3][1],
        results[4][1],
        results[0][2],
        results[1][2],
        results[2][2],
        results[3][2],
        results[4][2],
        results[0][3],
        results[1][3],
        results[2][3],
        results[3][3],
        results[4][3],
        sublayer_rms,
    )


def solution(mesh):
    return jax.shard_map(
        local,
        mesh=mesh,
        in_specs=(
            P(("dp", "fsdp"), None, None),
            P(("dp", "fsdp"), None, None),
            P(("dp", "fsdp")),
            P(None, ("dp", "fsdp"), None),
            P(None, ("dp", "fsdp"), None),
            P(None, ("dp", "fsdp"), None),
            P(None, ("dp", "fsdp"), None),
            P(None, ("dp", "fsdp")),
            P(None, ("dp", "fsdp"), None),
            P(None, ("dp", "fsdp"), None),
            P(None, ("dp", "fsdp"), None),
            P(None, ("dp", "fsdp"), None),
            P(None, ("dp", "fsdp")),
            P(None, ("dp", "fsdp"), None),
            P(None, ("dp", "fsdp"), None),
            P(None, ("dp", "fsdp"), None),
            P(None, ("dp", "fsdp"), None),
            P(None, ("dp", "fsdp")),
        ),
        out_specs=(
            P(("dp", "fsdp"), None, None),
            P(("dp", "fsdp"), None, None),
            P(None, ("dp", "fsdp"), None),
            P(None, ("dp", "fsdp"), None),
            P(None, ("dp", "fsdp"), None),
            P(None, ("dp", "fsdp"), None),
            P(None, ("dp", "fsdp")),
            P(None, ("dp", "fsdp"), None),
            P(None, ("dp", "fsdp"), None),
            P(None, ("dp", "fsdp"), None),
            P(None, ("dp", "fsdp"), None),
            P(None, ("dp", "fsdp")),
            P(None, ("dp", "fsdp"), None),
            P(None, ("dp", "fsdp"), None),
            P(None, ("dp", "fsdp"), None),
            P(None, ("dp", "fsdp"), None),
            P(None, ("dp", "fsdp")),
            P(None, ("dp", "fsdp"), None),
            P(None, ("dp", "fsdp"), None),
            P(None, ("dp", "fsdp"), None),
            P(None, ("dp", "fsdp"), None),
            P(None, ("dp", "fsdp")),
            P(),
        ),
        check_vma=False,
    )
```
